32 devices in a mesh: rows: 16 (over z, y, x), cols: 2 (over core).
Axes of the slice: x: 2, y: 2, z: 4, core: 2. Of those that a mesh axis runs over, the one named last changes fastest.
Arguments:
- lower_pivot: bfloat16 [4, 2048, 4, 2048], P(None, 'rows', None, 'cols'), may hold values from -0.0625 to 0.0625
- lower_rest: bfloat16 [24576, 4, 2048], P('rows', None, 'cols'), may hold values from -0.0625 to 0.0625
- diag_inverse: bfloat16 [4, 2048, 2048], P(None, 'cols', 'rows'), may hold values from -0.125 to 0.125
- rhs_pivot: bfloat16 [4, 2048, 512], P(None, 'rows', 'cols'), may hold values from -6 to 6
- rhs_rest: bfloat16 [512, 24576], P('cols', 'rows'), may hold values from -6 to 6
Outputs:
- solution: bfloat16 [4, 2048, 512], P(None, 'cols')
- remainder: bfloat16 [512, 24576], P('cols', 'rows')
The draws below stay inside these ranges and needn't reach their ends.
All inputs are finite; a program needn't handle non-finite values.
Results may differ from the reference program's by a relative error of at most 0.017.
Values may be sent and summed in bfloat16 or wider, within the bound.
No kernel may reach another device: no remote copies, remote signals or barrier semaphores. Data moves between devices by JAX's collectives and lax.ppermute only.
A program may use at most 64 MiB of HBM per device.

```python
import jax
import jax.numpy as jnp
from jax import lax

NB = 2048
NRHS = 512
NSTEP = 4
REST = 24576
N_COLS = 2


def levels(key, dims, shards, smallest, high):
    def one(axis_at, parts):
        draws = jax.random.uniform(jax.random.fold_in(jax.random.fold_in(key, 6), axis_at), (parts,), jnp.float32, smallest / len(shards), high / len(shards))
        return jnp.repeat(jnp.exp(draws), dims[axis_at] // parts).reshape((-1,) + (1,) * (len(dims) - axis_at - 1))

    factor_of = one(*shards[0])
    for cut in shards[1:]:
        factor_of = factor_of * one(*cut)
    return factor_of


def normal_values(rng, dims, spread, most, split=(), kind=jnp.bfloat16):
    drawn = spread * jax.random.normal(rng, dims, jnp.float32)
    if split:
        drawn = drawn * levels(rng, dims, split, -0.22, 0.18)
    return jnp.clip(drawn, -most, most).astype(kind)


def setup_inputs(seed: int = 0) -> dict:
    arg_keys = jax.random.split(jax.random.key(seed), 6)
    lower_pivot = normal_values(arg_keys[0], (NSTEP, NB, NSTEP, NB), (NSTEP * NB) ** -0.5, 0.0625, ((1, 16), (3, 2)))
    lower_rest = normal_values(arg_keys[1], (REST, NSTEP, NB), (NSTEP * NB) ** -0.5, 0.0625, ((0, 16), (2, 2)))
    diag_inverse = normal_values(arg_keys[2], (NSTEP, NB, NB), NB ** -0.5, 0.125, ((1, 2), (2, 16)))
    rhs_pivot = normal_values(arg_keys[3], (NSTEP, NB, NRHS), 1.0, 6.0, ((1, 16), (2, 2)))
    rhs_rest = normal_values(arg_keys[4], (NRHS, REST), 1.0, 6.0, ((0, 2), (1, 16)))
    return dict(lower_pivot=lower_pivot, lower_rest=lower_rest, diag_inverse=diag_inverse, rhs_pivot=rhs_pivot, rhs_rest=rhs_rest)


def reference(lower_pivot, lower_rest, diag_inverse, rhs_pivot, rhs_rest):
    solved = []
    for step_index in range(NSTEP):
        residual = rhs_pivot[step_index].astype(jnp.float32)
        if step_index > 0:
            factor_part = lower_pivot[step_index, :, :step_index, :].reshape(NB, step_index * NB)
            known_part = jnp.concatenate(solved, axis=0)
            residual = residual - jnp.dot(factor_part, known_part, preferred_element_type=jnp.float32)
        residual = residual.astype(jnp.bfloat16)
        solved.append(jnp.dot(diag_inverse[step_index], residual, preferred_element_type=jnp.float32).astype(jnp.bfloat16))
    solution = jnp.stack(solved)
    group_width = NB // N_COLS
    grouped_solution = solution.reshape(NSTEP, N_COLS, group_width, NRHS)
    grouped_lower = lower_rest.reshape(REST, NSTEP, N_COLS, group_width)
    total_sum = jnp.zeros((NRHS, REST), jnp.float32)
    for group_index in range(N_COLS):
        flat_solution = grouped_solution[:, group_index].reshape(NSTEP * group_width, NRHS)
        flat_lower = grouped_lower[:, :, group_index, :].reshape(REST, NSTEP * group_width)
        partial_sum = lax.dot_general(flat_solution, flat_lower, (((0,), (1,)), ((), ())), preferred_element_type=jnp.float32)
        rounded = lax.optimization_barrier(partial_sum.astype(jnp.bfloat16))
        total_sum = total_sum + rounded.astype(jnp.float32)
    remainder = (rhs_rest.astype(jnp.float32) - total_sum).astype(jnp.bfloat16)
    return solution, remainder
```

```python
import functools

import jax
import jax.numpy as jnp
from jax import lax
from jax.sharding import PartitionSpec as P
from jax.experimental import pallas as pl
from jax.experimental.pallas import tpu as pltpu

F32 = jnp.float32
BF16 = jnp.bfloat16


def split_of(count):
    best = 1
    for d in range(1, count + 1):
        if count % d == 0 and d * d <= count:
            best = d
    return best


def nt_dot(a, b):
    return lax.dot_general(a, b, (((1,), (1,)), ((), ())), preferred_element_type=F32)


def cut(n_rows, share):
    plane = split_of(n_rows)
    power = plane & (plane - 1) == 0
    code = [g ^ (g >> 1) if power else g for g in range(plane)]
    return plane, n_rows // plane, share // plane, code


def places(plane, code):
    row = lax.axis_index("rows")
    spot = row % plane
    g = sum(jnp.where(spot == code[i], i, 0) for i in range(plane))
    return g, row // plane, lax.axis_index("cols")


def movers(plane, depth, code, n_cols):
    def along_plane(x, k):
        pairs = [(b * plane + code[i], b * plane + code[(i + k) % plane]) for b in range(depth) for i in range(plane)]
        return lax.ppermute(x, "rows", pairs)

    def along_depth(x, k):
        pairs = [(b * plane + i, ((b + k) % depth) * plane + i) for b in range(depth) for i in range(plane)]
        return lax.ppermute(x, "rows", pairs)

    def along_cols(x, k):
        return lax.ppermute(x, "cols", [(i, (i + k) % n_cols) for i in range(n_cols)])

    return along_plane, along_depth, along_cols


def plain_path(lower_pivot, lower_rest, diag_inverse, rhs_pivot, rhs_rest):
    steps = lower_pivot.shape[0]
    eqs = lower_pivot.shape[1]
    share = lower_pivot.shape[3]
    sides = rhs_pivot.shape[2]
    rest = lower_rest.shape[0]
    n_rows = lax.axis_size("rows")
    n_cols = lax.axis_size("cols")
    plane, depth, width, code = cut(n_rows, share)
    g, z, core = places(plane, code)
    part = sides // depth
    along_plane, along_depth, along_cols = movers(plane, depth, code, n_cols)

    def gather(move, count, x, axis):
        return jnp.concatenate([x] + [move(x, k) for k in range(1, count)], axis=axis)

    def my_diag(s):
        block = diag_inverse[s].reshape(plane, width, eqs)
        parts = [lax.dynamic_index_in_dim(block, (g + k) % plane, 0, False) for k in range(plane)]
        held = jnp.concatenate([parts[0]] + [along_plane(parts[k], k) for k in range(1, plane)], axis=1)
        return gather(along_cols, n_cols, held, 0)

    def my_lower(s):
        parts = [
            lax.dynamic_slice_in_dim(lower_pivot[s, :, :s, :], ((g + k) % plane) * width, width, 2)
            for k in range(plane)
        ]
        held = jnp.concatenate([parts[0]] + [along_plane(parts[k], k) for k in range(1, plane)], axis=0)
        return gather(along_cols, n_cols, held, 2)

    def rolled(x, shift, axis):
        return jnp.roll(x, shift, axis)

    rhs_t = jnp.swapaxes(rhs_pivot, 1, 2)
    blocks = rhs_t.reshape(steps, depth, part, eqs)[:, ::-1]
    blocks = rolled(blocks, z + 1, 1).reshape(steps, sides, eqs)

    solved = []
    totals = jnp.zeros((sides, rest), F32)
    outs = []
    for s in range(steps):
        diag = my_diag(s)
        if s == 0:
            own = blocks[0]
        else:
            lower = my_lower(s)
            partial = jnp.zeros((sides, plane * eqs), F32)
            for t in range(s):
                partial = partial + nt_dot(solved[t], lower[:, t, :])
            total = blocks[s].astype(F32) - partial[:, :eqs]
            sent = partial.astype(BF16)
            for k in range(1, plane):
                total = total - along_plane(sent[:, k * eqs : (k + 1) * eqs], -k).astype(F32)
            own = total.astype(BF16)
        residual = gather(along_plane, plane, own, 1)
        product = nt_dot(residual, diag)
        sent = product.astype(BF16)
        total = product[:part]
        for k in range(1, depth):
            total = total + along_depth(sent[k * part : (k + 1) * part], -k).astype(F32)
        mine = total.astype(BF16)
        here = gather(along_depth, depth, mine, 0)
        solved.append(here)
        pieces = [here] + [along_plane(here, k) for k in range(1, plane)]
        pieces = [pieces[(-k) % plane] for k in range(plane)]
        full = jnp.stack([p.reshape(depth, part, n_cols, width) for p in pieces], axis=3)
        full = full[jnp.array([(-k) % depth for k in range(depth)])]
        full = rolled(full, z, 0)
        full = rolled(full, g, 3).reshape(sides, n_cols, share)
        rest_parts = [lower_rest[:, s, :]] + [along_cols(lower_rest[:, s, :], k) for k in range(1, n_cols)]
        for k in range(n_cols):
            totals = totals + nt_dot(full[:, k, :], rest_parts[k])
        theirs = [full[:, 0]] + [along_cols(full[:, k], -k) for k in range(1, n_cols)]
        theirs = rolled(jnp.stack(theirs, 0), core, 0).reshape(n_cols * sides, share)
        outs.append(theirs.T)
    remainder = (rhs_rest.astype(F32) - totals).astype(BF16)
    return jnp.stack(outs), remainder


VMEM_LIMIT = 40 * 1024 * 1024
SMALL = pl.BlockSpec(memory_space=pltpu.SMEM)
WHOLE = pl.BlockSpec(memory_space=pltpu.VMEM)


def call(body, outs, ins, specs, flops=0, scratch=(), **more):
    size = sum(x.size * x.dtype.itemsize for x in ins) + sum(o.size * o.dtype.itemsize for o in outs)
    return pl.pallas_call(
        body,
        out_shape=tuple(outs),
        in_specs=list(specs),
        scratch_shapes=list(scratch),
        compiler_params=pltpu.CompilerParams(vmem_limit_bytes=VMEM_LIMIT),
        cost_estimate=pl.CostEstimate(flops=flops, bytes_accessed=size, transcendentals=0),
        **more,
    )(*ins)


def shaped(dims, kind):
    return jax.ShapeDtypeStruct(dims, kind)


def prep_body(s, plane, width, eqs, meta, *refs):
    if s:
        diag, lower, *outs, flat = refs
        flat[...] = jnp.swapaxes(lower[0], 0, 1)
    else:
        diag, *outs = refs
    for k in range(plane):
        at = lax.rem(meta[0] + k, plane) * width
        for h in range(width // eqs):
            outs[k][0, :, h * eqs : (h + 1) * eqs] = diag[0, pl.ds(pl.multiple_of(at + h * eqs, eqs), eqs), :]
        for t in range(s):
            outs[k][1 + t] = flat[t, :, pl.ds(pl.multiple_of(at, width), width)]


def prep(s, plane, width, eqs, meta, diag_inverse, lower_pivot):
    share = plane * width
    steps = lower_pivot.shape[0]
    ins = [meta, diag_inverse]
    specs = [SMALL, pl.BlockSpec((1, share, eqs), lambda i: (s, 0, 0))]
    scratch = []
    if s:
        ins.append(lower_pivot)
        specs.append(pl.BlockSpec((1, eqs, steps, share), lambda i: (s, 0, 0, 0)))
        scratch.append(pltpu.VMEM((steps, eqs, share), BF16))
    out = shaped((s + 1, eqs, width), BF16)
    return call(
        functools.partial(prep_body, s, plane, width, eqs),
        [out] * plane,
        ins,
        specs,
        scratch=scratch,
        grid=(1,),
        out_specs=tuple(pl.BlockSpec((s + 1, eqs, width), lambda i: (0, 0, 0)) for _ in range(plane)),
    )


def diag_body(n_cols, plane, depth, width, eqs, meta, *refs):
    held = refs[: n_cols * plane]
    parts = refs[n_cols * plane : n_cols * plane + plane]
    outs, product = refs[n_cols * plane + plane : -1], refs[-1]
    sub = width // depth
    residual = jnp.concatenate([p[...] for p in parts], axis=0)
    for c in range(n_cols):
        for h in range(width // eqs):
            rows = jnp.concatenate(
                [held[c * plane + k][0, :, h * eqs : (h + 1) * eqs] for k in range(plane)], axis=1
            )
            product[c, h * eqs : (h + 1) * eqs] = jnp.dot(rows, residual, preferred_element_type=F32)
    for k in range(depth):
        at = pl.multiple_of(lax.rem(meta[1] + depth - k, depth) * sub, sub)
        for c in range(n_cols):
            outs[k][c * sub : (c + 1) * sub] = product[c, pl.ds(at, sub)].astype(outs[k].dtype)


def diag_product(n_cols, plane, depth, width, eqs, meta, held, parts):
    sides = parts[0].shape[1]
    dims = (n_cols * (width // depth), sides)
    first = pl.BlockSpec((1, eqs, width), lambda i: (0, 0, 0))
    full = pl.BlockSpec((eqs, sides), lambda i: (0, 0))
    return call(
        functools.partial(diag_body, n_cols, plane, depth, width, eqs),
        [shaped(dims, F32)] + [shaped(dims, BF16)] * (depth - 1),
        [meta, *held, *parts],
        [SMALL] + [first] * len(held) + [full] * plane,
        flops=2 * n_cols * width * plane * eqs * sides,
        scratch=[pltpu.VMEM((n_cols, width, sides), F32)],
        grid=(1,),
        out_specs=tuple(pl.BlockSpec(dims, lambda i: (0, 0)) for _ in range(depth)),
    )


def put_pieces(n_cols, depth, sub, meta, pieces, outs):
    for k in range(depth):
        at = pl.multiple_of(lax.rem(meta[1] + depth - k, depth) * sub, sub)
        for c in range(n_cols):
            outs[c][pl.ds(at, sub)] = pieces[k][c * sub : (c + 1) * sub]


def lower_body(s, n_cols, plane, depth, width, eqs, meta, *refs):
    refs = list(refs)
    held = [refs.pop(0) for _ in range(n_cols * plane)]
    known = [[refs.pop(0) for _ in range(n_cols)] for _ in range(s - 1)]
    pieces = [refs.pop(0) for _ in range(depth)]
    outs, newest = refs[:plane], refs[plane:]
    put_pieces(n_cols, depth, width // depth, meta, pieces, newest)
    total = None
    for t, blocks in enumerate(known + [newest]):
        for c in range(n_cols):
            rows = jnp.concatenate([held[c * plane + k][1 + t] for k in range(plane)], axis=0)
            term = jnp.dot(rows, blocks[c][...], preferred_element_type=F32)
            total = term if total is None else total + term
    for k in range(plane):
        outs[k][...] = total[k * eqs : (k + 1) * eqs].astype(outs[k].dtype)


def lower_product(s, n_cols, plane, depth, width, eqs, meta, held, known, pieces):
    sides = pieces[0].shape[1]
    flat = [x for blocks in known for x in blocks]
    ins = [meta, *held, *flat, *pieces]
    return call(
        functools.partial(lower_body, s, n_cols, plane, depth, width, eqs),
        [shaped((eqs, sides), F32)] + [shaped((eqs, sides), BF16)] * (plane - 1) + [shaped((width, sides), BF16)] * n_cols,
        ins,
        [SMALL] + [WHOLE] * (len(ins) - 1),
        flops=2 * s * n_cols * width * plane * eqs * sides,
    )


def place_body(n_cols, depth, sub, meta, *refs):
    put_pieces(n_cols, depth, sub, meta, refs[:depth], refs[depth:])


def place(n_cols, depth, width, meta, pieces):
    sides = pieces[0].shape[1]
    return call(
        functools.partial(place_body, n_cols, depth, width // depth),
        [shaped((width, sides), BF16)] * n_cols,
        [meta, *pieces],
        [SMALL] + [WHOLE] * depth,
    )


def join_body(n_cols, sides, meta, *refs):
    for k in range(n_cols):
        at = pl.multiple_of(lax.rem(meta[2] + k, n_cols) * sides, sides)
        refs[-1][:, pl.ds(at, sides)] = refs[k][...]


def join(n_cols, meta, parts):
    width, sides = parts[0].shape
    return call(
        functools.partial(join_body, n_cols, sides),
        [shaped((width, n_cols * sides), BF16)],
        [meta, *parts],
        [SMALL] + [WHOLE] * n_cols,
    )[0]


def flat_body(x, out):
    out[...] = jnp.swapaxes(x[...], 0, 1)


def flat_rest(lower_rest, start, count, block):
    _, steps, share = lower_rest.shape
    return call(
        flat_body,
        [shaped((steps, count, share), BF16)],
        [lower_rest],
        [pl.BlockSpec((block, steps, share), lambda i: (start // block + i, 0, 0))],
        grid=(count // block,),
        out_specs=(pl.BlockSpec((steps, block, share), lambda i: (0, i, 0)),),
    )[0]


def write_body(plane, width, has_buffer, meta, *refs):
    parts = refs[:plane]
    out, turned = refs[-2:]
    for k in range(plane):
        at = pl.multiple_of(lax.rem(meta[0] + plane - k, plane) * width, width)
        block = parts[k][...]
        out[0, pl.ds(at, width), :] = block
        turned[:, pl.ds(at, width)] = block.T


def write(s, steps, plane, meta, parts, buffer):
    width, total = parts[0].shape
    share = plane * width
    ins = [meta, *parts]
    specs = [SMALL] + [pl.BlockSpec((width, total), lambda i: (0, 0))] * plane
    alias = {}
    if buffer is not None:
        alias = {len(ins): 0}
        ins.append(buffer)
        specs.append(pl.BlockSpec(memory_space=pl.ANY))
    return call(
        functools.partial(write_body, plane, width, buffer is not None),
        [shaped((steps, share, total), BF16), shaped((total, share), BF16)],
        ins,
        specs,
        grid=(1,),
        out_specs=(
            pl.BlockSpec((1, share, total), lambda i: (s, 0, 0)),
            pl.BlockSpec((total, share), lambda i: (0, 0)),
        ),
        input_output_aliases=alias,
    )


def rest_body(ts, n_cols, sides, order, meta, *refs):
    turned = refs[: len(ts)]
    lower, out = refs[len(ts) :]
    at = pl.multiple_of(lax.rem(meta[2] + order, n_cols) * sides, sides)
    total = None
    for i, t in enumerate(ts):
        term = nt_dot(turned[i][pl.ds(at, sides), :], lower[i])
        total = term if total is None else total + term
    out[...] = total.astype(out.dtype)


def rest_product(ts, n_cols, sides, order, kind, meta, turned, lower):
    _, count, share = lower.shape
    return call(
        functools.partial(rest_body, ts, n_cols, sides, order),
        [shaped((sides, count), kind)],
        [meta, *turned, lower],
        [SMALL]
        + [pl.BlockSpec(x.shape, lambda i: (0, 0)) for x in turned]
        + [pl.BlockSpec((len(ts), count, share), lambda i: (ts[0] // len(ts), 0, 0))],
        flops=2 * len(ts) * share * sides * count,
        grid=(1,),
        out_specs=(pl.BlockSpec((sides, count), lambda i: (0, 0)),),
    )[0]


def kernel_path(lower_pivot, lower_rest, diag_inverse, rhs_pivot, rhs_rest):
    steps, eqs, _, share = lower_pivot.shape
    sides = rhs_pivot.shape[2]
    rest = lower_rest.shape[0]
    n_rows, n_cols = lax.axis_size("rows"), lax.axis_size("cols")
    plane, depth, width, code = cut(n_rows, share)
    g, z, core = places(plane, code)
    meta = jnp.stack([g, z, core]).astype(jnp.int32)
    along_plane, along_depth, along_cols = movers(plane, depth, code, n_cols)

    def held_of(s):
        packed = prep(s, plane, width, eqs, meta, diag_inverse, lower_pivot)
        mine = [packed[0]] + [along_plane(packed[k], k) for k in range(1, plane)]
        return mine + [along_cols(x, c) for c in range(1, n_cols) for x in mine]

    chunks = 4
    while rest % (chunks * 128):
        chunks -= 1
    count = rest // chunks
    rest_flat = [flat_rest(lower_rest, i * count, count, 128) for i in range(chunks)]

    known, pieces, buffer, turned = [], None, None, []

    def finish(s, blocks, buffer):
        parts = [blocks[0]] + [along_cols(blocks[k], -k) for k in range(1, n_cols)]
        whole = join(n_cols, meta, parts)
        gathered = [whole] + [along_plane(whole, k) for k in range(1, plane)]
        return write(s, steps, plane, meta, gathered, buffer)

    for s in range(steps):
        held = held_of(s)
        if s == 0:
            own = rhs_pivot[0]
        else:
            outs = lower_product(s, n_cols, plane, depth, width, eqs, meta, held, known, pieces)
            sums, blocks = outs[:plane], outs[plane:]
            known.append(blocks)
            total = rhs_pivot[s].astype(F32) - sums[0]
            for k in range(1, plane):
                total = total - along_plane(sums[k], -k).astype(F32)
            own = total.astype(BF16)
            buffer, last = finish(s - 1, blocks, buffer)
            turned.append(last)
        residual = [own] + [along_plane(own, k) for k in range(1, plane)]
        sums = diag_product(n_cols, plane, depth, width, eqs, meta, held, residual)
        total = sums[0]
        for k in range(1, depth):
            total = total + along_depth(sums[k], -k).astype(F32)
        mine = total.astype(BF16)
        pieces = [mine] + [along_depth(mine, k) for k in range(1, depth)]
    early = [
        [
            [rest_product([t], n_cols, sides, c, F32 if c == 0 else BF16, meta, [turned[t]], x) for x in rest_flat]
            for t in range(steps - 1)
        ]
        for c in range(n_cols)
    ]
    base = rhs_rest.astype(F32)
    for c in range(n_cols):
        lane = []
        for i in range(chunks):
            x = early[c][0][i].astype(F32)
            for t in range(1, steps - 1):
                x = x + early[c][t][i].astype(F32)
            lane.append(x)
        lane = jnp.concatenate(lane, axis=1)
        base = base - (lane if c == 0 else along_cols(lane.astype(BF16), c).astype(F32))
    buffer, last = finish(steps - 1, place(n_cols, depth, width, meta, pieces), buffer)
    late = [
        [rest_product([steps - 1], n_cols, sides, c, F32 if c == 0 else BF16, meta, [last], x) for x in rest_flat]
        for c in range(n_cols)
    ]
    total = base - jnp.concatenate(late[0], axis=1)
    for c in range(1, n_cols):
        total = total - along_cols(jnp.concatenate(late[c], axis=1), c).astype(F32)
    return buffer, total.astype(BF16)


def per_device(lower_pivot, lower_rest, diag_inverse, rhs_pivot, rhs_rest):
    eqs, share = lower_pivot.shape[1], lower_pivot.shape[3]
    plane, depth, width, _ = cut(lax.axis_size("rows"), share)
    fits = eqs % 128 == 0 and width % eqs == 0 and (width // depth) % 16 == 0 and rhs_pivot.shape[2] % 128 == 0
    fits = fits and lower_rest.shape[0] % 128 == 0
    path = kernel_path if fits else plain_path
    return path(lower_pivot, lower_rest, diag_inverse, rhs_pivot, rhs_rest)


def solution(mesh):
    placed = (
        P(None, "rows", None, "cols"),
        P("rows", None, "cols"),
        P(None, "cols", "rows"),
        P(None, "rows", "cols"),
        P("cols", "rows"),
    )
    return jax.shard_map(
        per_device,
        mesh=mesh,
        in_specs=placed,
        out_specs=(P(None, "cols", None), P("cols", "rows")),
        check_vma=False,
    )
```

```python
import dataclasses
import functools
import math

import jax
import jax.numpy as jnp
from jax import lax
from jax.sharding import PartitionSpec as P
from jax.experimental import pallas as pl
from jax.experimental.pallas import tpu as pltpu

F32 = jnp.float32
BF16 = jnp.bfloat16


def split_of(count):
    best = 1
    for d in range(1, count + 1):
        if count % d == 0 and d * d <= count:
            best = d
    return best


def nt_dot(a, b):
    return lax.dot_general(a, b, (((1,), (1,)), ((), ())), preferred_element_type=F32)


def cut(n_rows, share):
    plane = split_of(n_rows)
    power = plane & (plane - 1) == 0
    code = [g ^ (g >> 1) if power else g for g in range(plane)]
    return plane, n_rows // plane, share // plane, code


def places(plane, code):
    row = lax.axis_index("rows")
    spot = row % plane
    g = sum(jnp.where(spot == code[i], i, 0) for i in range(plane))
    return g, row // plane, lax.axis_index("cols")


def movers(plane, depth, code, n_cols):
    def along_plane(x, k):
        pairs = [(b * plane + code[i], b * plane + code[(i + k) % plane]) for b in range(depth) for i in range(plane)]
        return lax.ppermute(x, "rows", pairs)

    def along_depth(x, k):
        pairs = [(b * plane + i, ((b + k) % depth) * plane + i) for b in range(depth) for i in range(plane)]
        return lax.ppermute(x, "rows", pairs)

    def along_cols(x, k):
        return lax.ppermute(x, "cols", [(i, (i + k) % n_cols) for i in range(n_cols)])

    return along_plane, along_depth, along_cols


def plain_path(lower_pivot, lower_rest, diag_inverse, rhs_pivot, rhs_rest):
    steps = lower_pivot.shape[0]
    eqs = lower_pivot.shape[1]
    share = lower_pivot.shape[3]
    sides = rhs_pivot.shape[2]
    rest = lower_rest.shape[0]
    n_rows = lax.axis_size("rows")
    n_cols = lax.axis_size("cols")
    plane, depth, width, code = cut(n_rows, share)
    g, z, core = places(plane, code)
    part = sides // depth
    along_plane, along_depth, along_cols = movers(plane, depth, code, n_cols)

    def gather(move, count, x, axis):
        return jnp.concatenate([x] + [move(x, k) for k in range(1, count)], axis=axis)

    def my_diag(s):
        block = diag_inverse[s].reshape(plane, width, eqs)
        parts = [lax.dynamic_index_in_dim(block, (g + k) % plane, 0, False) for k in range(plane)]
        held = jnp.concatenate([parts[0]] + [along_plane(parts[k], k) for k in range(1, plane)], axis=1)
        return gather(along_cols, n_cols, held, 0)

    def my_lower(s):
        parts = [
            lax.dynamic_slice_in_dim(lower_pivot[s, :, :s, :], ((g + k) % plane) * width, width, 2)
            for k in range(plane)
        ]
        held = jnp.concatenate([parts[0]] + [along_plane(parts[k], k) for k in range(1, plane)], axis=0)
        return gather(along_cols, n_cols, held, 2)

    def rolled(x, shift, axis):
        return jnp.roll(x, shift, axis)

    rhs_t = jnp.swapaxes(rhs_pivot, 1, 2)
    blocks = rhs_t.reshape(steps, depth, part, eqs)[:, ::-1]
    blocks = rolled(blocks, z + 1, 1).reshape(steps, sides, eqs)

    solved = []
    totals = jnp.zeros((sides, rest), F32)
    outs = []
    for s in range(steps):
        diag = my_diag(s)
        if s == 0:
            own = blocks[0]
        else:
            lower = my_lower(s)
            partial = jnp.zeros((sides, plane * eqs), F32)
            for t in range(s):
                partial = partial + nt_dot(solved[t], lower[:, t, :])
            total = blocks[s].astype(F32) - partial[:, :eqs]
            sent = partial.astype(BF16)
            for k in range(1, plane):
                total = total - along_plane(sent[:, k * eqs : (k + 1) * eqs], -k).astype(F32)
            own = total.astype(BF16)
        residual = gather(along_plane, plane, own, 1)
        product = nt_dot(residual, diag)
        sent = product.astype(BF16)
        total = product[:part]
        for k in range(1, depth):
            total = total + along_depth(sent[k * part : (k + 1) * part], -k).astype(F32)
        mine = total.astype(BF16)
        here = gather(along_depth, depth, mine, 0)
        solved.append(here)
        pieces = [here] + [along_plane(here, k) for k in range(1, plane)]
        pieces = [pieces[(-k) % plane] for k in range(plane)]
        full = jnp.stack([p.reshape(depth, part, n_cols, width) for p in pieces], axis=3)
        full = full[jnp.array([(-k) % depth for k in range(depth)])]
        full = rolled(full, z, 0)
        full = rolled(full, g, 3).reshape(sides, n_cols, share)
        rest_parts = [lower_rest[:, s, :]] + [along_cols(lower_rest[:, s, :], k) for k in range(1, n_cols)]
        for k in range(n_cols):
            totals = totals + nt_dot(full[:, k, :], rest_parts[k])
        theirs = [full[:, 0]] + [along_cols(full[:, k], -k) for k in range(1, n_cols)]
        theirs = rolled(jnp.stack(theirs, 0), core, 0).reshape(n_cols * sides, share)
        outs.append(theirs.T)
    remainder = (rhs_rest.astype(F32) - totals).astype(BF16)
    return jnp.stack(outs), remainder


VMEM_LIMIT = 40 * 1024 * 1024
WEIGHT = 8
SMALL = pl.BlockSpec(memory_space=pltpu.SMEM)
WHOLE = pl.BlockSpec(memory_space=pltpu.VMEM)


def call(body, outs, ins, specs, flops=0, scratch=(), after=(), weight=1, **more):
    size = sum(math.prod(x.shape) * x.dtype.itemsize for x in [*ins, *outs])
    first, last = len(ins), len(ins) + len(after)

    def run(*refs):
        body(*refs[:first], *refs[last:])

    return pl.pallas_call(
        run,
        out_shape=tuple(outs),
        in_specs=list(specs) + [pl.BlockSpec(memory_space=pl.ANY)] * len(after),
        scratch_shapes=list(scratch),
        compiler_params=pltpu.CompilerParams(vmem_limit_bytes=VMEM_LIMIT),
        cost_estimate=pl.CostEstimate(flops=flops, bytes_accessed=size * weight, transcendentals=0),
        **more,
    )(*ins, *after)


def shaped(dims, kind):
    return jax.ShapeDtypeStruct(dims, kind)


def prep_body(ss, form, meta, *refs):
    py, width, eqs = form.py, form.width, form.eqs
    refs = list(refs)
    diag, rhs = refs.pop(0), refs.pop(0)
    lower = refs.pop(0) if ss[-1] else None
    flat = refs.pop() if ss[-1] else None
    for i, s in enumerate(ss):
        outs = refs[i * py : (i + 1) * py]
        if s:
            flat[...] = jnp.swapaxes(lower[i], 0, 1)
        for dy in range(py):
            at = lax.rem(meta[0] + dy, py) * width
            for h in range(width // eqs):
                outs[dy][:, h * eqs : (h + 1) * eqs] = diag[i, pl.ds(pl.multiple_of(at + h * eqs, eqs), eqs), :]
            for t in range(s):
                outs[dy][:, (1 + t) * width : (2 + t) * width] = flat[t, :, pl.ds(pl.multiple_of(at, width), width)]
            outs[dy][:, (1 + s) * width :] = rhs[i]


def prep(ss, form, meta, diag_inverse, rhs_pivot, lower_pivot, after=()):
    width, eqs, share, sides = form.width, form.eqs, form.py * form.width, form.px * form.sides
    steps, count = lower_pivot.shape[0], len(ss)
    ins = [meta, diag_inverse, rhs_pivot]
    specs = [
        SMALL,
        pl.BlockSpec((pl.Element(count), pl.Element(share), pl.Element(eqs)), lambda i: (ss[0], 0, 0)),
        pl.BlockSpec((pl.Element(count), pl.Element(eqs), pl.Element(sides)), lambda i: (ss[0], 0, 0)),
    ]
    scratch = []
    if ss[-1]:
        ins.append(lower_pivot)
        specs.append(
            pl.BlockSpec(
                (pl.Element(count), pl.Element(eqs), pl.Element(steps), pl.Element(share)), lambda i: (ss[0], 0, 0, 0)
            )
        )
        scratch.append(pltpu.VMEM((steps, eqs, share), BF16))
    dims = [(eqs, (s + 1) * width + sides) for s in ss for _ in range(form.py)]
    outs = call(
        functools.partial(prep_body, ss, form),
        [shaped(d, BF16) for d in dims],
        ins,
        specs,
        scratch=scratch,
        after=after,
        weight=WEIGHT,
        grid=(1,),
        out_specs=tuple(pl.BlockSpec(d, lambda i: (0, 0)) for d in dims),
    )
    return {s: outs[i * form.py : (i + 1) * form.py] for i, s in enumerate(ss)}


def pack_body(chips, *refs):
    for k in range(chips):
        refs[-1][k] = refs[k][...]


def pack(parts, after=()):
    return call(
        functools.partial(pack_body, len(parts)),
        [shaped((len(parts), *parts[0].shape), BF16)],
        parts,
        [WHOLE] * len(parts),
        after=after,
        weight=WEIGHT,
    )[0]


def take_held(form, refs):
    held = []
    while len(held) < form.n_cols * form.chips:
        ref = refs.pop(0)
        held += [ref] if len(ref.shape) == 2 else [ref.at[k] for k in range(form.chips)]
    return held


def diag_body(form, terms, meta, *refs):
    chips, n_cols, depth, eqs, width, sides = form.chips, form.n_cols, form.depth, form.eqs, form.width, form.sides
    refs = list(refs)
    held = take_held(form, refs)
    sums = [refs.pop(0) for _ in range(terms)]
    outs, product = refs[:-1], refs[-1]
    sub = width // depth
    right = held[0].shape[-1] - form.px * sides
    right = pl.ds(pl.multiple_of(right + meta[1] * sides, sides), sides)
    residual = jnp.concatenate([held[k][:, right] for k in range(chips)], axis=0)
    if terms:
        total = residual.astype(F32)
        for x in sums:
            total = total - x[...].astype(F32)
        residual = total.astype(BF16)
    for c in range(n_cols):
        for h in range(width // eqs):
            rows = jnp.concatenate(
                [held[c * chips + k][:, h * eqs : (h + 1) * eqs] for k in range(chips)], axis=1
            )
            product[c, h * eqs : (h + 1) * eqs] = jnp.dot(rows, residual, preferred_element_type=F32)
    for k in range(depth):
        at = pl.multiple_of(lax.rem(meta[2] + depth - k, depth) * sub, sub)
        for c in range(n_cols):
            outs[k][c * sub : (c + 1) * sub] = product[c, pl.ds(at, sub)].astype(outs[k].dtype)


def diag_product(form, meta, held, sums, after=()):
    width, eqs, sides, depth, n_cols, chips = form.width, form.eqs, form.sides, form.depth, form.n_cols, form.chips
    dims = (n_cols * (width // depth), sides)
    return call(
        functools.partial(diag_body, form, len(sums)),
        [shaped(dims, F32)] + [shaped(dims, BF16)] * (depth - 1),
        [meta, *held, *sums],
        [SMALL] + [WHOLE] * (len(held) + len(sums)),
        flops=2 * n_cols * width * chips * eqs * sides,
        scratch=[pltpu.VMEM((n_cols, width, sides), F32)],
        after=after,
    )


def put_pieces(form, meta, pieces, outs):
    depth, sub = form.depth, form.width // form.depth
    for k in range(depth):
        at = pl.multiple_of(lax.rem(meta[2] + depth - k, depth) * sub, sub)
        for c in range(form.n_cols):
            outs[c][pl.ds(at, sub)] = pieces[k][c * sub : (c + 1) * sub]


def lower_body(s, form, meta, *refs):
    chips, n_cols, eqs = form.chips, form.n_cols, form.eqs
    refs = list(refs)
    held = take_held(form, refs)
    width = form.width
    known = [[refs.pop(0) for _ in range(n_cols)] for _ in range(s - 1)]
    pieces = [refs.pop(0) for _ in range(form.depth)]
    outs, newest = refs[: form.py], refs[form.py :]
    put_pieces(form, meta, pieces, newest)
    total = None
    for t, blocks in enumerate(known + [newest]):
        for c in range(n_cols):
            lanes = slice((1 + t) * width, (2 + t) * width)
            rows = jnp.concatenate([held[c * chips + k][:, lanes] for k in range(chips)], axis=0)
            term = jnp.dot(rows, blocks[c][...], preferred_element_type=F32)
            total = term if total is None else total + term
    for e in range(form.py):
        for k, (dy, dx) in enumerate(form.shifts):
            mine = form.shifts.index(((dy - e) % form.py, dx))
            outs[e][k * eqs : (k + 1) * eqs] = total[mine * eqs : (mine + 1) * eqs].astype(outs[e].dtype)


def lower_product(s, form, meta, held, known, pieces, after=()):
    rows, sides = form.chips * form.eqs, form.sides
    flat = [x for blocks in known for x in blocks]
    ins = [meta, *held, *flat, *pieces]
    return call(
        functools.partial(lower_body, s, form),
        [shaped((rows, sides), F32)]
        + [shaped((rows, sides), BF16)] * (form.py - 1)
        + [shaped((form.width, sides), BF16)] * form.n_cols,
        ins,
        [SMALL] + [WHOLE] * (len(ins) - 1),
        flops=2 * s * form.n_cols * form.width * rows * sides,
        after=after,
    )


def place_body(form, meta, *refs):
    put_pieces(form, meta, refs[: form.depth], refs[form.depth :])


def place(form, meta, pieces, after=()):
    return call(
        functools.partial(place_body, form),
        [shaped((form.width, form.sides), BF16)] * form.n_cols,
        [meta, *pieces],
        [SMALL] + [WHOLE] * form.depth,
        after=after,
    )


def gate_body(*refs):
    pass


def gate(x, after):
    return call(
        gate_body,
        [shaped(x.shape, x.dtype)],
        [x],
        [pl.BlockSpec(memory_space=pl.ANY)],
        after=after,
        out_specs=(pl.BlockSpec(memory_space=pl.ANY),),
        input_output_aliases={0: 0},
    )[0]


def join_body(form, count, meta, *refs):
    width, sides = form.width, form.sides
    for i in range(count):
        for k in range(form.n_cols):
            at = pl.multiple_of(lax.rem(meta[3] + k, form.n_cols) * sides, sides)
            refs[-1][i * width : (i + 1) * width, pl.ds(at, sides)] = refs[i * form.n_cols + k][...]


def join(form, meta, parts, after=()):
    count = len(parts) // form.n_cols
    return call(
        functools.partial(join_body, form, count),
        [shaped((count * form.width, form.n_cols * form.sides), BF16)],
        [meta, *parts],
        [SMALL] + [WHOLE] * len(parts),
        after=after,
    )[0]


def flat_body(x, *refs):
    refs[-2][...] = jnp.swapaxes(x[...], 0, 1)
    refs[-1][...] = jnp.zeros_like(refs[-1])


def flat_rest(lower_rest, buffer, turn, turns, block, after=()):
    rest, steps, share = lower_rest.shape
    first = turn * (rest // turns // block)
    ins, alias = [lower_rest], {}
    specs = [pl.BlockSpec((block, steps, share), lambda i: (first + i, 0, 0))]
    if buffer is not None:
        alias = {1: 0}
        ins.append(buffer)
        specs.append(pl.BlockSpec(memory_space=pltpu.HBM))
    return call(
        flat_body,
        [pltpu.HBM((steps, rest, share), BF16), shaped((8, 128), F32)],
        ins,
        specs,
        after=after,
        grid=(rest // turns // block,),
        out_specs=(
            pl.BlockSpec((steps, block, share), lambda i: (0, first + i, 0)),
            pl.BlockSpec((8, 128), lambda i: (0, 0)),
        ),
        input_output_aliases=alias,
    )


def write_body(form, count, meta, *refs):
    parts = refs[: form.chips]
    out, turned = refs[-2:]
    width, sides = form.width, form.sides
    for i in range(count):
        for k, (dy, dx) in enumerate(form.shifts):
            y, x = lax.rem(meta[0] + form.py - dy, form.py), lax.rem(meta[1] + form.px - dx, form.px)
            block = parts[k][i * width : (i + 1) * width]
            row = pl.ds(pl.multiple_of(y * width, width), width)
            for c in range(form.n_cols):
                lane = pl.ds(pl.multiple_of((c * form.px + x) * sides, sides), sides)
                piece = block[:, c * sides : (c + 1) * sides]
                out[i, row, lane] = piece
                turned[i, lane, row] = piece.T


def write(s, steps, form, meta, parts, buffer, after=()):
    share, total = form.py * form.width, form.px * form.n_cols * form.sides
    count = parts[0].shape[0] // form.width
    ins = [meta, *parts]
    specs = [SMALL] + [pl.BlockSpec(x.shape, lambda i: (0, 0)) for x in parts]
    alias = {}
    if buffer is not None:
        alias = {len(ins): 0}
        ins.append(buffer)
        specs.append(pl.BlockSpec(memory_space=pltpu.HBM))
    return call(
        functools.partial(write_body, form, count),
        [pltpu.HBM((steps, share, total), BF16), shaped((count, total, share), BF16)],
        ins,
        specs,
        after=after,
        grid=(1,),
        out_specs=(
            pl.BlockSpec((count, share, total), lambda i: (s // count, 0, 0)),
            pl.BlockSpec((count, total, share), lambda i: (0, 0, 0)),
        ),
        input_output_aliases=alias,
    )


def rest_body(form, orders, counts, meta, *refs):
    turned, lower, outs = refs[: len(counts)], refs[len(counts)], refs[len(counts) + 1 :]
    sides = form.px * form.sides
    for order, out in zip(orders, outs):
        at = pl.multiple_of(lax.rem(meta[3] + order, form.n_cols) * sides, sides)
        total, t = None, 0
        for x, count in zip(turned, counts):
            for i in range(count):
                term = nt_dot(x[i, pl.ds(at, sides), :], lower[t])
                total = term if total is None else total + term
                t += 1
        out[...] = total.astype(out.dtype)


def rest_product(first, form, orders, meta, turned, lower, after=()):
    _, rest, share = lower.shape
    counts = [x.shape[0] for x in turned]
    count = sum(counts)
    sides = form.px * form.sides
    block = max(n for n in (512, 384, 256, 128) if rest % n == 0)
    return call(
        functools.partial(rest_body, form, orders, counts),
        [shaped((sides, rest), F32 if order == 0 else BF16) for order in orders],
        [meta, *turned, pltpu.with_memory_space_constraint(lower, pltpu.HBM)],
        [SMALL]
        + [pl.BlockSpec(x.shape, lambda i: (0, 0, 0)) for x in turned]
        + [pl.BlockSpec((count, block, share), lambda i: (first // count, i, 0))],
        flops=2 * count * share * sides * rest * len(orders),
        after=after,
        grid=(rest // block,),
        out_specs=tuple(pl.BlockSpec((sides, block), lambda i: (0, i)) for _ in orders),
    )


@dataclasses.dataclass
class Form:
    py: int
    px: int
    depth: int
    n_cols: int
    eqs: int
    width: int
    sides: int

    def __post_init__(self):
        self.shifts = [(dy, dx) for dy in range(self.py) for dx in range(self.px)]
        self.chips = len(self.shifts)


def form_of(lower_pivot, rhs_pivot):
    n_rows = lax.axis_size("rows")
    plane = split_of(n_rows)
    px = split_of(plane)
    py = plane // px
    return Form(
        py, px, n_rows // plane, lax.axis_size("cols"), lower_pivot.shape[1], lower_pivot.shape[3] // py,
        rhs_pivot.shape[2] // px,
    )


def kernel_path(form, lower_pivot, lower_rest, diag_inverse, rhs_pivot, rhs_rest):
    lower_pivot, lower_rest, diag_inverse, rhs_pivot = (
        pltpu.with_memory_space_constraint(x, pltpu.HBM) for x in (lower_pivot, lower_rest, diag_inverse, rhs_pivot)
    )
    steps = lower_pivot.shape[0]
    rest = lower_rest.shape[0]
    py, px, depth, n_cols, chips = form.py, form.px, form.depth, form.n_cols, form.chips
    row = lax.axis_index("rows")
    meta = jnp.stack([row // px % py, row % px, row // chips, lax.axis_index("cols")]).astype(jnp.int32)

    def along_plane(x, dy, dx):
        pairs = [
            ((b * py + y) * px + i, (b * py + (y + dy) % py) * px + (i + dx) % px)
            for b in range(depth)
            for y in range(py)
            for i in range(px)
        ]
        return lax.ppermute(x, "rows", pairs)

    def along_depth(x, k):
        pairs = [(b * chips + i, (b + k) % depth * chips + i) for b in range(depth) for i in range(chips)]
        return lax.ppermute(x, "rows", pairs)

    def along_cols(x, k):
        return lax.ppermute(x, "cols", [(i, (i + k) % n_cols) for i in range(n_cols)])

    def out(blocks):
        first = [blocks[0]] + [along_plane(blocks[dy], dy, 0) for dy in range(1, py)]
        return first, [along_plane(blocks[0], 0, dx) for dx in range(1, px)]

    def onward(state, after=()):
        first, got = state
        got = [first[0], *got]
        for x in first[1:]:
            x = gate(x, after) if after else x
            got += [x] + [along_plane(x, 0, dx) for dx in range(1, px)]
        return got

    def held_of(parts, after):
        if not after:
            return parts + [along_cols(x, c) for c in range(1, n_cols) for x in parts]
        mine = pack(parts, after)
        return [mine] + [along_cols(mine, c) for c in range(1, n_cols)]

    def joined(ts, after=()):
        parts = []
        for t in ts:
            parts += [known[t][0]] + [along_cols(known[t][k], -k) for k in range(1, n_cols)]
        return join(form, meta, parts, after)

    turns = 3
    block = 128
    while rest % (turns * block):
        turns -= 1
    last = steps - 1
    inputs = (diag_inverse, rhs_pivot, lower_pivot)
    first = out(prep((0,), form, meta, *inputs)[0])
    packed = prep(tuple(range(1, steps)), form, meta, *inputs)
    held = held_of(onward(first), ())
    moving, moved, leaving = {}, {}, {}
    known, sums, turned, flat, buffer = [], [], [], None, None
    by_lower, by_diag, by_sum = ({s: [] for s in range(steps + 1)} for _ in range(3))
    if last:
        moving[1] = out(packed[1])
        by_diag[0] += [packed[last][0], *moving[1][0][1:], *moving[1][1]]
    for s in range(steps):
        if s > 0:
            outs = lower_product(s, form, meta, held, known, pieces, by_lower[s])
            known.append(outs[py:])
            sums = [outs[0]] + [along_plane(outs[e], e, 0) for e in range(1, py)]
            if s < last:
                moved[s + 1] = onward(moving[s + 1], [outs[0]])
                by_sum[s] += moved[s + 1]
            else:
                ready = onward(leaving[0], [outs[0]])
                by_sum[s] += ready
            if s == last - 1:
                whole = joined(range(s), [outs[0]])
                by_diag[s].append(whole)
            if s == last:
                newest = joined([s - 1], [outs[0]])
                by_diag[s].append(newest)
        products = diag_product(form, meta, held, sums, by_diag[s])
        if s == 0 and last:
            moved[1] = onward(moving[1], [products[0]])
            by_sum[0] += moved[1]
        if s < last - 1:
            first = [gate(x, [products[0]]) for x in packed[s + 2]]
        elif s == last - 1:
            first = [gate(whole, [products[0]])] * py
        else:
            first = [gate(newest, [products[0]])] * py
        first = [first[0]] + [along_plane(first[dy], dy, 0) for dy in range(1, py)]
        by_sum[s] += first[1:]
        arrivals = [along_depth(products[k], -k) for k in range(1, depth)]
        arrivals[-1] = gate(arrivals[-1], by_sum[s])
        total = products[0]
        for x in arrivals:
            total = total + x.astype(F32)
        mine = total.astype(BF16)
        if s < last:
            held = held_of(moved[s + 1], [mine])
        send = gate(first[0], [mine])
        direct = [along_plane(send, 0, dx) for dx in range(1, px)]
        (by_diag if 0 < s < last else by_lower)[s + 1] += direct
        if s < last - 1:
            moving[s + 2] = ([send, *first[1:]], direct)
        else:
            leaving[s - last + 1] = ([send, *first[1:]], direct)
        pieces = [mine] + [along_depth(mine, k) for k in range(1, depth)]
        if s < turns:
            flat, mark = flat_rest(lower_rest, flat, s, turns, block, [mine])
            by_lower[s + 1].append(mark)
        if s == last:
            buffer, new = write(0, steps, form, meta, ready, buffer, [mine])
            turned.append(new)
            by_lower[s + 1].append(new)
    newest = onward(leaving[1], [mine])
    known.append(place(form, meta, pieces, by_lower[steps]))
    final, direct = out([joined([last])] * py)
    gathered = onward((final, direct))
    buffer, new = write(last - 1, steps, form, meta, newest, buffer, [mine])
    turned.append(new)
    early = rest_product(0, form, range(n_cols), meta, turned, flat, direct)
    base = rhs_rest.astype(F32) - early[0]
    for c in range(1, n_cols):
        base = base - along_cols(early[c], c).astype(F32)
    buffer, new = write(last, steps, form, meta, gathered, buffer)
    late = rest_product(last, form, range(n_cols), meta, [new], flat)
    total = base - late[0]
    for c in range(1, n_cols):
        total = total - along_cols(late[c], c).astype(F32)
    return buffer, total.astype(BF16)


def per_device(lower_pivot, lower_rest, diag_inverse, rhs_pivot, rhs_rest):
    form = form_of(lower_pivot, rhs_pivot)
    fits = form.eqs % 128 == 0 and form.width % form.eqs == 0 and form.sides % 128 == 0
    fits = fits and (form.width // form.depth) % 16 == 0 and lower_rest.shape[0] % 128 == 0
    if fits:
        return kernel_path(form, lower_pivot, lower_rest, diag_inverse, rhs_pivot, rhs_rest)
    return plain_path(lower_pivot, lower_rest, diag_inverse, rhs_pivot, rhs_rest)


def solution(mesh):
    placed = (
        P(None, "rows", None, "cols"),
        P("rows", None, "cols"),
        P(None, "cols", "rows"),
        P(None, "rows", "cols"),
        P("cols", "rows"),
    )
    return jax.shard_map(
        per_device,
        mesh=mesh,
        in_specs=placed,
        out_specs=(P(None, "cols", None), P("cols", "rows")),
        check_vma=False,
    )
```

```python
import dataclasses
import functools
import math

import jax
import jax.numpy as jnp
from jax import lax
from jax.sharding import PartitionSpec as P
from jax.experimental import pallas as pl
from jax.experimental.pallas import tpu as pltpu

F32 = jnp.float32
BF16 = jnp.bfloat16


def split_of(count):
    best = 1
    for d in range(1, count + 1):
        if count % d == 0 and d * d <= count:
            best = d
    return best


def nt_dot(a, b):
    return lax.dot_general(a, b, (((1,), (1,)), ((), ())), preferred_element_type=F32)


def cut(n_rows, share):
    plane = split_of(n_rows)
    power = plane & (plane - 1) == 0
    code = [g ^ (g >> 1) if power else g for g in range(plane)]
    return plane, n_rows // plane, share // plane, code


def places(plane, code):
    row = lax.axis_index("rows")
    spot = row % plane
    g = sum(jnp.where(spot == code[i], i, 0) for i in range(plane))
    return g, row // plane, lax.axis_index("cols")


def movers(plane, depth, code, n_cols):
    def along_plane(x, k):
        pairs = [(b * plane + code[i], b * plane + code[(i + k) % plane]) for b in range(depth) for i in range(plane)]
        return lax.ppermute(x, "rows", pairs)

    def along_depth(x, k):
        pairs = [(b * plane + i, ((b + k) % depth) * plane + i) for b in range(depth) for i in range(plane)]
        return lax.ppermute(x, "rows", pairs)

    def along_cols(x, k):
        return lax.ppermute(x, "cols", [(i, (i + k) % n_cols) for i in range(n_cols)])

    return along_plane, along_depth, along_cols


def plain_path(lower_pivot, lower_rest, diag_inverse, rhs_pivot, rhs_rest):
    steps = lower_pivot.shape[0]
    eqs = lower_pivot.shape[1]
    share = lower_pivot.shape[3]
    sides = rhs_pivot.shape[2]
    rest = lower_rest.shape[0]
    n_rows = lax.axis_size("rows")
    n_cols = lax.axis_size("cols")
    plane, depth, width, code = cut(n_rows, share)
    g, z, core = places(plane, code)
    part = sides // depth
    along_plane, along_depth, along_cols = movers(plane, depth, code, n_cols)

    def gather(move, count, x, axis):
        return jnp.concatenate([x] + [move(x, k) for k in range(1, count)], axis=axis)

    def my_diag(s):
        block = diag_inverse[s].reshape(plane, width, eqs)
        parts = [lax.dynamic_index_in_dim(block, (g + k) % plane, 0, False) for k in range(plane)]
        held = jnp.concatenate([parts[0]] + [along_plane(parts[k], k) for k in range(1, plane)], axis=1)
        return gather(along_cols, n_cols, held, 0)

    def my_lower(s):
        parts = [
            lax.dynamic_slice_in_dim(lower_pivot[s, :, :s, :], ((g + k) % plane) * width, width, 2)
            for k in range(plane)
        ]
        held = jnp.concatenate([parts[0]] + [along_plane(parts[k], k) for k in range(1, plane)], axis=0)
        return gather(along_cols, n_cols, held, 2)

    def rolled(x, shift, axis):
        return jnp.roll(x, shift, axis)

    rhs_t = jnp.swapaxes(rhs_pivot, 1, 2)
    blocks = rhs_t.reshape(steps, depth, part, eqs)[:, ::-1]
    blocks = rolled(blocks, z + 1, 1).reshape(steps, sides, eqs)

    solved = []
    totals = jnp.zeros((sides, rest), F32)
    outs = []
    for s in range(steps):
        diag = my_diag(s)
        if s == 0:
            own = blocks[0]
        else:
            lower = my_lower(s)
            partial = jnp.zeros((sides, plane * eqs), F32)
            for t in range(s):
                partial = partial + nt_dot(solved[t], lower[:, t, :])
            total = blocks[s].astype(F32) - partial[:, :eqs]
            sent = partial.astype(BF16)
            for k in range(1, plane):
                total = total - along_plane(sent[:, k * eqs : (k + 1) * eqs], -k).astype(F32)
            own = total.astype(BF16)
        residual = gather(along_plane, plane, own, 1)
        product = nt_dot(residual, diag)
        sent = product.astype(BF16)
        total = product[:part]
        for k in range(1, depth):
            total = total + along_depth(sent[k * part : (k + 1) * part], -k).astype(F32)
        mine = total.astype(BF16)
        here = gather(along_depth, depth, mine, 0)
        solved.append(here)
        pieces = [here] + [along_plane(here, k) for k in range(1, plane)]
        pieces = [pieces[(-k) % plane] for k in range(plane)]
        full = jnp.stack([p.reshape(depth, part, n_cols, width) for p in pieces], axis=3)
        full = full[jnp.array([(-k) % depth for k in range(depth)])]
        full = rolled(full, z, 0)
        full = rolled(full, g, 3).reshape(sides, n_cols, share)
        rest_parts = [lower_rest[:, s, :]] + [along_cols(lower_rest[:, s, :], k) for k in range(1, n_cols)]
        for k in range(n_cols):
            totals = totals + nt_dot(full[:, k, :], rest_parts[k])
        theirs = [full[:, 0]] + [along_cols(full[:, k], -k) for k in range(1, n_cols)]
        theirs = rolled(jnp.stack(theirs, 0), core, 0).reshape(n_cols * sides, share)
        outs.append(theirs.T)
    remainder = (rhs_rest.astype(F32) - totals).astype(BF16)
    return jnp.stack(outs), remainder


VMEM_LIMIT = 40 * 1024 * 1024
WEIGHT = 8
SMALL = pl.BlockSpec(memory_space=pltpu.SMEM)
WHOLE = pl.BlockSpec(memory_space=pltpu.VMEM)


def call(body, outs, ins, specs, flops=0, scratch=(), after=(), weight=1, **more):
    size = sum(math.prod(x.shape) * x.dtype.itemsize for x in [*ins, *outs])
    first, last = len(ins), len(ins) + len(after)

    def run(*refs):
        body(*refs[:first], *refs[last:])

    return pl.pallas_call(
        run,
        out_shape=tuple(outs),
        in_specs=list(specs) + [pl.BlockSpec(memory_space=pl.ANY)] * len(after),
        scratch_shapes=list(scratch),
        compiler_params=pltpu.CompilerParams(vmem_limit_bytes=VMEM_LIMIT),
        cost_estimate=pl.CostEstimate(flops=flops, bytes_accessed=size * weight, transcendentals=0),
        **more,
    )(*ins, *after)


def shaped(dims, kind):
    return jax.ShapeDtypeStruct(dims, kind)


def put_diag(form, meta, dy, block, out):
    at = lax.rem(meta[0] + dy, form.py) * form.width
    for h in range(form.width // form.eqs):
        lanes = slice(h * form.eqs, (h + 1) * form.eqs)
        out[:, lanes] = block[pl.ds(pl.multiple_of(at + h * form.eqs, form.eqs), form.eqs), :]


def start_body(form, meta, diag, rhs, *refs):
    py, px, width, sides = form.py, form.px, form.width, form.sides
    own, outs, far = refs[-1], refs[:py], refs[py:-1]

    def part(s, dx):
        return rhs[s, :, pl.ds(pl.multiple_of(lax.rem(meta[1] + dx, px) * sides, sides), sides)]

    for dy in range(py):
        put_diag(form, meta, dy, diag.at[0], outs[dy])
        outs[dy][:, width:] = rhs[0]
    for dx in range(1, px):
        out = far[dx - 1]
        put_diag(form, meta, 0, diag.at[0], out)
        out[:, width : width + px * sides] = rhs[0]
        for s in range(1, rhs.shape[0]):
            out[:, width + (px + s - 1) * sides : width + (px + s) * sides] = part(s, dx)
    for s in range(rhs.shape[0]):
        own[s] = part(s, 0)


def start(form, meta, diag_inverse, rhs_pivot):
    width, eqs, sides, share = form.width, form.eqs, form.sides, form.py * form.width
    steps = rhs_pivot.shape[0]
    dims = [(eqs, width + form.px * sides)] * form.py
    dims += [(eqs, width + (form.px + steps - 1) * sides)] * (form.px - 1) + [(steps, eqs, sides)]
    outs = call(
        functools.partial(start_body, form),
        [shaped(d, BF16) for d in dims],
        [meta, diag_inverse, rhs_pivot],
        [
            SMALL,
            pl.BlockSpec((1, share, eqs), lambda i: (0, 0, 0)),
            pl.BlockSpec(rhs_pivot.shape, lambda i: (0, 0, 0)),
        ],
        weight=WEIGHT,
        grid=(1,),
        out_specs=tuple(pl.BlockSpec(d, lambda i, n=len(d): (0,) * n) for d in dims),
    )
    return outs[: form.py], outs[form.py : -1], outs[-1]


def prep_body(ss, form, meta, diag, lower, *refs):
    py, width = form.py, form.width
    flat = refs[-1]
    for i, s in enumerate(ss):
        outs = refs[i * py : (i + 1) * py]
        flat[...] = jnp.swapaxes(lower[i], 0, 1)
        for dy in range(py):
            put_diag(form, meta, dy, diag.at[i], outs[dy])
            at = lax.rem(meta[0] + dy, py) * width
            for t in range(s):
                outs[dy][:, (1 + t) * width : (2 + t) * width] = flat[t, :, pl.ds(pl.multiple_of(at, width), width)]


def prep(ss, form, meta, diag_inverse, lower_pivot, after=()):
    width, eqs, share = form.width, form.eqs, form.py * form.width
    steps, count = lower_pivot.shape[0], len(ss)
    dims = [(eqs, (s + 1) * width) for s in ss for _ in range(form.py)]
    outs = call(
        functools.partial(prep_body, ss, form),
        [shaped(d, BF16) for d in dims],
        [meta, diag_inverse, lower_pivot],
        [
            SMALL,
            pl.BlockSpec((pl.Element(count), pl.Element(share), pl.Element(eqs)), lambda i: (ss[0], 0, 0)),
            pl.BlockSpec(
                (pl.Element(count), pl.Element(eqs), pl.Element(steps), pl.Element(share)), lambda i: (ss[0], 0, 0, 0)
            ),
        ],
        scratch=[pltpu.VMEM((steps, eqs, share), BF16)],
        after=after,
        weight=WEIGHT,
        grid=(1,),
        out_specs=tuple(pl.BlockSpec(d, lambda i: (0, 0)) for d in dims),
    )
    return {s: outs[i * form.py : (i + 1) * form.py] for i, s in enumerate(ss)}


def pack_body(count, *refs):
    for k, part in enumerate(take(list(refs), count)):
        refs[-1][k] = part[...]


def pack(parts, after=()):
    count = sum(1 if x.ndim == 2 else x.shape[0] for x in parts)
    return call(
        functools.partial(pack_body, count),
        [shaped((count, *parts[0].shape[-2:]), BF16)],
        parts,
        [WHOLE] * len(parts),
        after=after,
        weight=WEIGHT,
    )[0]


def take(refs, count):
    got = []
    while len(got) < count:
        ref = refs.pop(0)
        got += [ref] if len(ref.shape) == 2 else [ref.at[k] for k in range(ref.shape[0])]
    return got


def diag_body(form, terms, meta, *refs):
    chips, n_cols, depth, eqs, width, sides = form.chips, form.n_cols, form.depth, form.eqs, form.width, form.sides
    refs = list(refs)
    held = take(refs, n_cols * chips)
    sums = [refs.pop(0) for _ in range(terms)]
    outs, product = refs[:-1], refs[-1]
    sub = width // depth
    if terms:
        total = sums[0][...]
        for x in sums[1:]:
            total = total + x[...].astype(F32)
        residual = (-total).astype(BF16)
    else:
        right = pl.ds(pl.multiple_of(width + meta[1] * sides, sides), sides)
        residual = jnp.concatenate([held[k][:, right] for k in range(chips)], axis=0)
    for c in range(n_cols):
        for h in range(width // eqs):
            rows = jnp.concatenate(
                [held[c * chips + k][:, h * eqs : (h + 1) * eqs] for k in range(chips)], axis=1
            )
            product[c, h * eqs : (h + 1) * eqs] = jnp.dot(rows, residual, preferred_element_type=F32)
    for k in range(depth):
        at = pl.multiple_of(lax.rem(meta[2] + depth - k, depth) * sub, sub)
        for c in range(n_cols):
            outs[k][c * sub : (c + 1) * sub] = product[c, pl.ds(at, sub)].astype(outs[k].dtype)


def diag_product(form, meta, held, sums, after=()):
    width, eqs, sides, depth, n_cols, chips = form.width, form.eqs, form.sides, form.depth, form.n_cols, form.chips
    dims = (n_cols * (width // depth), sides)
    return call(
        functools.partial(diag_body, form, len(sums)),
        [shaped(dims, F32)] + [shaped(dims, BF16)] * (depth - 1),
        [meta, *held, *sums],
        [SMALL] + [WHOLE] * (len(held) + len(sums)),
        flops=2 * n_cols * width * chips * eqs * sides,
        scratch=[pltpu.VMEM((n_cols, width, sides), F32)],
        after=after,
    )


def put_pieces(form, meta, pieces, outs):
    depth, sub = form.depth, form.width // form.depth
    for k in range(depth):
        at = pl.multiple_of(lax.rem(meta[2] + depth - k, depth) * sub, sub)
        for c in range(form.n_cols):
            outs[c][pl.ds(at, sub)] = pieces[k][c * sub : (c + 1) * sub]


def lower_body(s, form, meta, *refs):
    chips, n_cols, eqs = form.chips, form.n_cols, form.eqs
    refs = list(refs)
    held = take(refs, n_cols * chips)
    width = form.width
    known = [[refs.pop(0) for _ in range(n_cols)] for _ in range(s - 1)]
    pieces = [refs.pop(0) for _ in range(form.depth)]
    own = refs.pop(0)
    far = [refs.pop(0) for _ in range(form.px - 1)]
    outs, newest = refs[: form.py], refs[form.py :]
    put_pieces(form, meta, pieces, newest)
    total = None
    for t, blocks in enumerate(known + [newest]):
        for c in range(n_cols):
            lanes = slice((1 + t) * width, (2 + t) * width)
            rows = jnp.concatenate([held[c * chips + k][:, lanes] for k in range(chips)], axis=0)
            term = jnp.dot(rows, blocks[c][...], preferred_element_type=F32)
            total = term if total is None else total + term
    parts = [total[k * eqs : (k + 1) * eqs] for k in range(chips)]
    lane = width + (form.px + s - 1) * form.sides
    for k, (dy, dx) in enumerate(form.shifts):
        if dy == 0:
            right = far[dx - 1][:, lane : lane + form.sides] if dx else own[s]
            parts[k] = parts[k] - right.astype(F32)
    for e in range(form.py):
        for k, (dy, dx) in enumerate(form.shifts):
            mine = form.shifts.index(((dy - e) % form.py, dx))
            outs[e][k * eqs : (k + 1) * eqs] = parts[mine].astype(outs[e].dtype)


def lower_product(s, form, meta, held, known, pieces, own, far, after=()):
    rows, sides = form.chips * form.eqs, form.sides
    flat = [x for blocks in known for x in blocks]
    ins = [meta, *held, *flat, *pieces, own, *far]
    return call(
        functools.partial(lower_body, s, form),
        [shaped((rows, sides), F32)]
        + [shaped((rows, sides), BF16)] * (form.py - 1)
        + [shaped((form.width, sides), BF16)] * form.n_cols,
        ins,
        [SMALL] + [WHOLE] * (len(ins) - 1),
        flops=2 * s * form.n_cols * form.width * rows * sides,
        after=after,
    )


def place_body(form, meta, *refs):
    put_pieces(form, meta, refs[: form.depth], refs[form.depth :])


def place(form, meta, pieces, after=()):
    return call(
        functools.partial(place_body, form),
        [shaped((form.width, form.sides), BF16)] * form.n_cols,
        [meta, *pieces],
        [SMALL] + [WHOLE] * form.depth,
        after=after,
    )


def gate_body(*refs):
    pass


def gate(x, after):
    return call(
        gate_body,
        [shaped(x.shape, x.dtype)],
        [x],
        [pl.BlockSpec(memory_space=pl.ANY)],
        after=after,
        out_specs=(pl.BlockSpec(memory_space=pl.ANY),),
        input_output_aliases={0: 0},
    )[0]


def join_body(form, count, meta, *refs):
    width, sides = form.width, form.sides
    for i in range(count):
        for k in range(form.n_cols):
            at = pl.multiple_of(lax.rem(meta[3] + k, form.n_cols) * sides, sides)
            refs[-1][i * width : (i + 1) * width, pl.ds(at, sides)] = refs[i * form.n_cols + k][...]


def join(form, meta, parts, after=()):
    count = len(parts) // form.n_cols
    return call(
        functools.partial(join_body, form, count),
        [shaped((count * form.width, form.n_cols * form.sides), BF16)],
        [meta, *parts],
        [SMALL] + [WHOLE] * len(parts),
        after=after,
    )[0]


def flat_body(x, *refs):
    refs[-2][...] = jnp.swapaxes(x[...], 0, 1)
    refs[-1][...] = jnp.zeros_like(refs[-1])


def flat_rest(lower_rest, buffer, turn, turns, block, after=()):
    rest, steps, share = lower_rest.shape
    first = turn * (rest // turns // block)
    ins, alias = [lower_rest], {}
    specs = [pl.BlockSpec((block, steps, share), lambda i: (first + i, 0, 0))]
    if buffer is not None:
        alias = {1: 0}
        ins.append(buffer)
        specs.append(pl.BlockSpec(memory_space=pltpu.HBM))
    return call(
        flat_body,
        [pltpu.HBM((steps, rest, share), BF16), shaped((8, 128), F32)],
        ins,
        specs,
        after=after,
        grid=(rest // turns // block,),
        out_specs=(
            pl.BlockSpec((steps, block, share), lambda i: (0, first + i, 0)),
            pl.BlockSpec((8, 128), lambda i: (0, 0)),
        ),
        input_output_aliases=alias,
    )


def write_body(form, count, meta, *refs):
    parts = take(list(refs), form.chips)
    put_solved(form, count, meta, parts, *refs[-2:])


def put_solved(form, count, meta, parts, out, turned):
    width, sides = form.width, form.sides
    for i in range(count):
        for k, (dy, dx) in enumerate(form.shifts):
            y, x = lax.rem(meta[0] + form.py - dy, form.py), lax.rem(meta[1] + form.px - dx, form.px)
            block = parts[k][i * width : (i + 1) * width]
            row = pl.ds(pl.multiple_of(y * width, width), width)
            for c in range(form.n_cols):
                lane = pl.ds(pl.multiple_of((c * form.px + x) * sides, sides), sides)
                piece = block[:, c * sides : (c + 1) * sides]
                out[i, row, lane] = piece
                turned[i, lane, row] = piece.T


def write(s, steps, form, meta, parts, buffer, after=()):
    share, total = form.py * form.width, form.px * form.n_cols * form.sides
    count = parts[0].shape[-2] // form.width
    ins = [meta, *parts]
    specs = [SMALL] + [pl.BlockSpec(x.shape, lambda i, n=x.ndim: (0,) * n) for x in parts]
    alias = {}
    if buffer is not None:
        alias = {len(ins): 0}
        ins.append(buffer)
        specs.append(pl.BlockSpec(memory_space=pltpu.HBM))
    return call(
        functools.partial(write_body, form, count),
        [pltpu.HBM((steps, share, total), BF16), shaped((count, total, share), BF16)],
        ins,
        specs,
        after=after,
        grid=(1,),
        out_specs=(
            pl.BlockSpec((count, share, total), lambda i: (s // count, 0, 0)),
            pl.BlockSpec((count, total, share), lambda i: (0, 0, 0)),
        ),
        input_output_aliases=alias,
    )


def rest_body(form, orders, counts, running, meta, *refs):
    turned, lower, refs = refs[: len(counts)], refs[len(counts)], refs[len(counts) + 1 :]
    before, outs = refs[:running], refs[running:]
    sides = form.px * form.sides
    for order, out in zip(orders, outs):
        at = pl.multiple_of(lax.rem(meta[3] + order, form.n_cols) * sides, sides)
        total, t = None, 0
        for x, count in zip(turned, counts):
            for i in range(count):
                term = nt_dot(x[i, pl.ds(at, sides), :], lower[t])
                total = term if total is None else total + term
                t += 1
        if running:
            total = total + before[order][...].astype(F32)
        out[...] = total.astype(out.dtype)


def rest_product(first, form, meta, turned, lower, before=(), after=()):
    orders = range(form.n_cols)
    _, rest, share = lower.shape
    counts = [x.shape[0] for x in turned]
    count = sum(counts)
    sides = form.px * form.sides
    block = max(n for n in (512, 384, 256, 128) if rest % n == 0)
    side_block = pl.BlockSpec((sides, block), lambda i: (0, i))
    return call(
        functools.partial(rest_body, form, orders, counts, len(before)),
        [shaped((sides, rest), F32 if order == 0 else BF16) for order in orders],
        [meta, *turned, pltpu.with_memory_space_constraint(lower, pltpu.HBM), *before],
        [SMALL]
        + [pl.BlockSpec(x.shape, lambda i: (0, 0, 0)) for x in turned]
        + [pl.BlockSpec((count, block, share), lambda i: (first // count, i, 0))]
        + [side_block] * len(before),
        flops=2 * count * share * sides * rest * len(orders),
        after=after,
        grid=(rest // block,),
        out_specs=(side_block,) * len(orders),
    )


def last_body(form, meta, *refs):
    refs = list(refs)
    parts = take(refs, form.chips)
    lower, _, out, *sums, turned = refs

    @pl.when(pl.program_id(0) == 0)
    def _():
        put_solved(form, 1, meta, parts, out, turned)

    sides = form.px * form.sides
    for order, to in enumerate(sums):
        at = pl.multiple_of(lax.rem(meta[3] + order, form.n_cols) * sides, sides)
        to[...] = nt_dot(turned[0, pl.ds(at, sides), :], lower[0]).astype(to.dtype)


def last_step(form, meta, parts, lower, buffer):
    steps, rest, share = lower.shape
    total, sides = form.px * form.n_cols * form.sides, form.px * form.sides
    block = max(n for n in (512, 384, 256, 128) if rest % n == 0)
    lower = pltpu.with_memory_space_constraint(lower, pltpu.HBM)
    side_block = pl.BlockSpec((sides, block), lambda i: (0, i))
    return call(
        functools.partial(last_body, form),
        [pltpu.HBM((steps, share, total), BF16)]
        + [shaped((sides, rest), F32 if order == 0 else BF16) for order in range(form.n_cols)],
        [meta, *parts, lower, buffer],
        [SMALL]
        + [pl.BlockSpec(x.shape, lambda i, n=x.ndim: (0,) * n) for x in parts]
        + [pl.BlockSpec((1, block, share), lambda i: (steps - 1, i, 0))]
        + [pl.BlockSpec(memory_space=pltpu.HBM)],
        flops=2 * share * total * rest,
        scratch=[pltpu.VMEM((1, total, share), BF16)],
        grid=(rest // block,),
        out_specs=(pl.BlockSpec((1, share, total), lambda i: (steps - 1, 0, 0)), *[side_block] * form.n_cols),
        input_output_aliases={len(parts) + 2: 0},
    )


@dataclasses.dataclass
class Form:
    py: int
    px: int
    depth: int
    n_cols: int
    eqs: int
    width: int
    sides: int

    def __post_init__(self):
        self.shifts = [(dy, dx) for dx in range(self.px) for dy in range(self.py)]
        self.chips = len(self.shifts)


def form_of(lower_pivot, rhs_pivot):
    n_rows = lax.axis_size("rows")
    plane = split_of(n_rows)
    px = split_of(plane)
    py = plane // px
    return Form(
        py, px, n_rows // plane, lax.axis_size("cols"), lower_pivot.shape[1], lower_pivot.shape[3] // py,
        rhs_pivot.shape[2] // px,
    )


def kernel_path(form, lower_pivot, lower_rest, diag_inverse, rhs_pivot, rhs_rest):
    lower_pivot, lower_rest, diag_inverse, rhs_pivot = (
        pltpu.with_memory_space_constraint(x, pltpu.HBM) for x in (lower_pivot, lower_rest, diag_inverse, rhs_pivot)
    )
    steps = lower_pivot.shape[0]
    rest = lower_rest.shape[0]
    py, px, depth, n_cols, chips = form.py, form.px, form.depth, form.n_cols, form.chips
    row = lax.axis_index("rows")
    meta = jnp.stack([row // px % py, row % px, row // chips, lax.axis_index("cols")]).astype(jnp.int32)

    def along_plane(x, dy, dx):
        pairs = [
            ((b * py + y) * px + i, (b * py + (y + dy) % py) * px + (i + dx) % px)
            for b in range(depth)
            for y in range(py)
            for i in range(px)
        ]
        return lax.ppermute(x, "rows", pairs)

    def along_depth(x, k):
        pairs = [(b * chips + i, (b + k) % depth * chips + i) for b in range(depth) for i in range(chips)]
        return lax.ppermute(x, "rows", pairs)

    def along_cols(x, k):
        return lax.ppermute(x, "cols", [(i, (i + k) % n_cols) for i in range(n_cols)])

    def up(blocks):
        return [blocks[0]] + [along_plane(blocks[dy], dy, 0) for dy in range(1, py)]

    def across(x):
        return [along_plane(x, 0, dx) for dx in range(1, px)]

    def onward(first, direct, after=()):
        rest = [gate(x, after) if after else x for x in first[1:]]
        far = [across(x) for x in rest]
        got = [first[0], *rest]
        for dx in range(px - 1):
            got += [direct[dx]] + [x[dx] for x in far]
        return got

    def held_of(parts, after):
        mine = [pack(parts, after)] if after else parts
        return mine + [along_cols(x, c) for c in range(1, n_cols) for x in mine]

    def joined(ts, after=()):
        parts = []
        for t in ts:
            parts += [known[t][0]] + [along_cols(known[t][k], -k) for k in range(1, n_cols)]
        return join(form, meta, parts, after)

    turns = 3
    block = 128
    while rest % (turns * block):
        turns -= 1
    last = steps - 1
    near, far, own = start(form, meta, diag_inverse, rhs_pivot)
    got = up(near)
    here = [along_plane(x, 0, dx + 1) for dx, x in enumerate(far)]
    held = held_of(onward(got, here), ())
    packed = prep(tuple(range(1, steps)), form, meta, diag_inverse, lower_pivot)
    first = up([gate(x, here + got[1:]) for x in packed[1]])
    moved = pack(first)
    moved = [moved, *across(moved)]
    known, sums, turned, flat, buffer = [], [], [], None, None
    by_lower, by_diag, by_sum = ({s: [] for s in range(steps + 1)} for _ in range(3))
    by_diag[0] += [packed[last][0], *first[1:]]
    for s in range(steps):
        if s > 0:
            outs = lower_product(s, form, meta, held, known, pieces, own, here, by_lower[s])
            known.append(outs[py:])
            sums = [outs[0]] + [along_plane(outs[e], e, 0) for e in range(1, py)]
            if s > 0:
                moved = onward(first, direct, [outs[0]])
            if s >= last - 1:
                whole = joined(range(s) if s < last else [s - 1], [outs[0]])
                by_diag[s].append(whole)
        products = diag_product(form, meta, held, sums, by_diag[s])
        if s < last - 1:
            first = up([gate(x, [products[0]]) for x in packed[s + 2]])
        else:
            first = up([gate(whole, [products[0]])] * py)
        by_sum[s] += moved + first[1:]
        arrivals = [along_depth(products[k], -k) for k in range(1, depth)]
        arrivals[-1] = gate(arrivals[-1], by_sum[s])
        total = products[0]
        for x in arrivals:
            total = total + x.astype(F32)
        mine = total.astype(BF16)
        if s < last:
            held = held_of(moved, [mine])
            first = [gate(first[0], [mine]), *first[1:]]
            direct = across(first[0])
            by_diag[s + 1] += direct
        else:
            newest = pack(first, [mine])
            newest = [newest, *across(newest)]
        pieces = [mine] + [along_depth(mine, k) for k in range(1, depth)]
        if s < turns:
            flat, mark = flat_rest(lower_rest, flat, s, turns, block, [mine])
            by_lower[s + 1].append(mark)
        if s == last:
            buffer, new = write(0, steps, form, meta, moved, buffer, [mine])
            turned.append(new)
            by_lower[s + 1].append(new)
    known.append(place(form, meta, pieces, by_lower[steps]))
    whole = joined([last])
    got = up([whole] * py)
    direct = across(got[0])
    early = rest_product(0, form, meta, turned, flat, (), [whole, *newest])
    got = onward(got, direct, [early[0]])
    buffer, new = write(last - 1, steps, form, meta, newest, buffer, [early[0]])
    early = rest_product(last - 1, form, meta, [new], flat, early)
    buffer, *late = last_step(form, meta, got, flat, buffer)
    total = rhs_rest.astype(F32) - early[0] - late[0]
    for c in range(1, n_cols):
        total = total - along_cols(early[c], c).astype(F32) - along_cols(late[c], c).astype(F32)
    return buffer, total.astype(BF16)


def per_device(lower_pivot, lower_rest, diag_inverse, rhs_pivot, rhs_rest):
    form = form_of(lower_pivot, rhs_pivot)
    fits = form.eqs % 128 == 0 and form.width % form.eqs == 0 and form.sides % 128 == 0
    fits = fits and (form.width // form.depth) % 16 == 0 and lower_rest.shape[0] % 128 == 0
    if fits:
        return kernel_path(form, lower_pivot, lower_rest, diag_inverse, rhs_pivot, rhs_rest)
    return plain_path(lower_pivot, lower_rest, diag_inverse, rhs_pivot, rhs_rest)


def solution(mesh):
    placed = (
        P(None, "rows", None, "cols"),
        P("rows", None, "cols"),
        P(None, "cols", "rows"),
        P(None, "rows", "cols"),
        P("cols", "rows"),
    )
    return jax.shard_map(
        per_device,
        mesh=mesh,
        in_specs=placed,
        out_specs=(P(None, "cols", None), P("cols", "rows")),
        check_vma=False,
    )
```

```python
import dataclasses
import functools
import math

import jax
import jax.numpy as jnp
from jax import lax
from jax.sharding import PartitionSpec as P
from jax.experimental import pallas as pl
from jax.experimental.pallas import tpu as pltpu

F32 = jnp.float32
BF16 = jnp.bfloat16


def split_of(count):
    best = 1
    for d in range(1, count + 1):
        if count % d == 0 and d * d <= count:
            best = d
    return best


def nt_dot(a, b):
    return lax.dot_general(a, b, (((1,), (1,)), ((), ())), preferred_element_type=F32)


def cut(n_rows, share):
    plane = split_of(n_rows)
    power = plane & (plane - 1) == 0
    code = [g ^ (g >> 1) if power else g for g in range(plane)]
    return plane, n_rows // plane, share // plane, code


def places(plane, code):
    row = lax.axis_index("rows")
    spot = row % plane
    g = sum(jnp.where(spot == code[i], i, 0) for i in range(plane))
    return g, row // plane, lax.axis_index("cols")


def movers(plane, depth, code, n_cols):
    def along_plane(x, k):
        pairs = [(b * plane + code[i], b * plane + code[(i + k) % plane]) for b in range(depth) for i in range(plane)]
        return lax.ppermute(x, "rows", pairs)

    def along_depth(x, k):
        pairs = [(b * plane + i, ((b + k) % depth) * plane + i) for b in range(depth) for i in range(plane)]
        return lax.ppermute(x, "rows", pairs)

    def along_cols(x, k):
        return lax.ppermute(x, "cols", [(i, (i + k) % n_cols) for i in range(n_cols)])

    return along_plane, along_depth, along_cols


def plain_path(lower_pivot, lower_rest, diag_inverse, rhs_pivot, rhs_rest):
    steps = lower_pivot.shape[0]
    eqs = lower_pivot.shape[1]
    share = lower_pivot.shape[3]
    sides = rhs_pivot.shape[2]
    rest = lower_rest.shape[0]
    n_rows = lax.axis_size("rows")
    n_cols = lax.axis_size("cols")
    plane, depth, width, code = cut(n_rows, share)
    g, z, core = places(plane, code)
    part = sides // depth
    along_plane, along_depth, along_cols = movers(plane, depth, code, n_cols)

    def gather(move, count, x, axis):
        return jnp.concatenate([x] + [move(x, k) for k in range(1, count)], axis=axis)

    def my_diag(s):
        block = diag_inverse[s].reshape(plane, width, eqs)
        parts = [lax.dynamic_index_in_dim(block, (g + k) % plane, 0, False) for k in range(plane)]
        held = jnp.concatenate([parts[0]] + [along_plane(parts[k], k) for k in range(1, plane)], axis=1)
        return gather(along_cols, n_cols, held, 0)

    def my_lower(s):
        parts = [
            lax.dynamic_slice_in_dim(lower_pivot[s, :, :s, :], ((g + k) % plane) * width, width, 2)
            for k in range(plane)
        ]
        held = jnp.concatenate([parts[0]] + [along_plane(parts[k], k) for k in range(1, plane)], axis=0)
        return gather(along_cols, n_cols, held, 2)

    def rolled(x, shift, axis):
        return jnp.roll(x, shift, axis)

    rhs_t = jnp.swapaxes(rhs_pivot, 1, 2)
    blocks = rhs_t.reshape(steps, depth, part, eqs)[:, ::-1]
    blocks = rolled(blocks, z + 1, 1).reshape(steps, sides, eqs)

    solved = []
    totals = jnp.zeros((sides, rest), F32)
    outs = []
    for s in range(steps):
        diag = my_diag(s)
        if s == 0:
            own = blocks[0]
        else:
            lower = my_lower(s)
            partial = jnp.zeros((sides, plane * eqs), F32)
            for t in range(s):
                partial = partial + nt_dot(solved[t], lower[:, t, :])
            total = blocks[s].astype(F32) - partial[:, :eqs]
            sent = partial.astype(BF16)
            for k in range(1, plane):
                total = total - along_plane(sent[:, k * eqs : (k + 1) * eqs], -k).astype(F32)
            own = total.astype(BF16)
        residual = gather(along_plane, plane, own, 1)
        product = nt_dot(residual, diag)
        sent = product.astype(BF16)
        total = product[:part]
        for k in range(1, depth):
            total = total + along_depth(sent[k * part : (k + 1) * part], -k).astype(F32)
        mine = total.astype(BF16)
        here = gather(along_depth, depth, mine, 0)
        solved.append(here)
        pieces = [here] + [along_plane(here, k) for k in range(1, plane)]
        pieces = [pieces[(-k) % plane] for k in range(plane)]
        full = jnp.stack([p.reshape(depth, part, n_cols, width) for p in pieces], axis=3)
        full = full[jnp.array([(-k) % depth for k in range(depth)])]
        full = rolled(full, z, 0)
        full = rolled(full, g, 3).reshape(sides, n_cols, share)
        rest_parts = [lower_rest[:, s, :]] + [along_cols(lower_rest[:, s, :], k) for k in range(1, n_cols)]
        for k in range(n_cols):
            totals = totals + nt_dot(full[:, k, :], rest_parts[k])
        theirs = [full[:, 0]] + [along_cols(full[:, k], -k) for k in range(1, n_cols)]
        theirs = rolled(jnp.stack(theirs, 0), core, 0).reshape(n_cols * sides, share)
        outs.append(theirs.T)
    remainder = (rhs_rest.astype(F32) - totals).astype(BF16)
    return jnp.stack(outs), remainder


VMEM_LIMIT = 40 * 1024 * 1024
WEIGHT = 8
SMALL = pl.BlockSpec(memory_space=pltpu.SMEM)
WHOLE = pl.BlockSpec(memory_space=pltpu.VMEM)


def call(body, outs, ins, specs, flops=0, scratch=(), after=(), weight=1, **more):
    size = sum(math.prod(x.shape) * x.dtype.itemsize for x in [*ins, *outs])
    first, last = len(ins), len(ins) + len(after)

    def run(*refs):
        body(*refs[:first], *refs[last:])

    return pl.pallas_call(
        run,
        out_shape=tuple(outs),
        in_specs=list(specs) + [pl.BlockSpec(memory_space=pl.ANY)] * len(after),
        scratch_shapes=list(scratch),
        compiler_params=pltpu.CompilerParams(vmem_limit_bytes=VMEM_LIMIT),
        cost_estimate=pl.CostEstimate(flops=flops, bytes_accessed=size * weight, transcendentals=0),
        **more,
    )(*ins, *after)


def shaped(dims, kind):
    return jax.ShapeDtypeStruct(dims, kind)


def put_diag(form, meta, dy, block, out):
    at = lax.rem(meta[0] + dy, form.py) * form.width
    for h in range(form.width // form.eqs):
        lanes = slice(h * form.eqs, (h + 1) * form.eqs)
        out[:, lanes] = block[pl.ds(pl.multiple_of(at + h * form.eqs, form.eqs), form.eqs), :]


def start_body(form, meta, diag, rhs, *refs):
    py, px, width, sides = form.py, form.px, form.width, form.sides
    own, outs, far = refs[-1], refs[:py], refs[py:-1]

    def part(s, dx):
        return rhs[s, :, pl.ds(pl.multiple_of(lax.rem(meta[1] + dx, px) * sides, sides), sides)]

    for dy in range(py):
        put_diag(form, meta, dy, diag.at[0], outs[dy])
        outs[dy][:, width:] = rhs[0]
    for dx in range(1, px):
        out = far[dx - 1]
        put_diag(form, meta, 0, diag.at[0], out)
        out[:, width : width + px * sides] = rhs[0]
        for s in range(1, rhs.shape[0]):
            out[:, width + (px + s - 1) * sides : width + (px + s) * sides] = part(s, dx)
    for s in range(rhs.shape[0]):
        own[s] = part(s, 0)


def start(form, meta, diag_inverse, rhs_pivot):
    width, eqs, sides, share = form.width, form.eqs, form.sides, form.py * form.width
    steps = rhs_pivot.shape[0]
    dims = [(eqs, width + form.px * sides)] * form.py
    dims += [(eqs, width + (form.px + steps - 1) * sides)] * (form.px - 1) + [(steps, eqs, sides)]
    outs = call(
        functools.partial(start_body, form),
        [shaped(d, BF16) for d in dims],
        [meta, diag_inverse, rhs_pivot],
        [
            SMALL,
            pl.BlockSpec((1, share, eqs), lambda i: (0, 0, 0)),
            pl.BlockSpec(rhs_pivot.shape, lambda i: (0, 0, 0)),
        ],
        weight=WEIGHT,
        grid=(1,),
        out_specs=tuple(pl.BlockSpec(d, lambda i, n=len(d): (0,) * n) for d in dims),
    )
    return outs[: form.py], outs[form.py : -1], outs[-1]


def slots(s, steps):
    own = [(s, t) for t in range(s) if s < 3 or t > 0]
    return own + ([(s + 1, 0)] if 2 <= s < steps - 1 else [])


def slot_of(s, t, steps):
    for by in (s, s - 1):
        if (s, t) in slots(by, steps):
            return by, 1 + slots(by, steps).index((s, t))


def prep_body(ss, form, meta, diag, lower, *refs):
    py, width, steps = form.py, form.width, lower.shape[2]
    flat = refs[-1]
    for i, s in enumerate(ss):
        flat[...] = jnp.swapaxes(lower[i], 0, 1)
        for dy in range(py):
            put_diag(form, meta, dy, diag.at[i], refs[i * py + dy])
            at = lax.rem(meta[0] + dy, py) * width
            for t in range(s):
                by, slot = slot_of(s, t, steps)
                out = refs[ss.index(by) * py + dy]
                out[:, slot * width : (slot + 1) * width] = flat[t, :, pl.ds(pl.multiple_of(at, width), width)]


def prep(ss, form, meta, diag_inverse, lower_pivot, after=()):
    width, eqs, share = form.width, form.eqs, form.py * form.width
    steps, count = lower_pivot.shape[0], len(ss)
    dims = [(eqs, (1 + len(slots(s, steps))) * width) for s in ss for _ in range(form.py)]
    outs = call(
        functools.partial(prep_body, ss, form),
        [shaped(d, BF16) for d in dims],
        [meta, diag_inverse, lower_pivot],
        [
            SMALL,
            pl.BlockSpec((pl.Element(count), pl.Element(share), pl.Element(eqs)), lambda i: (ss[0], 0, 0)),
            pl.BlockSpec(
                (pl.Element(count), pl.Element(eqs), pl.Element(steps), pl.Element(share)), lambda i: (ss[0], 0, 0, 0)
            ),
        ],
        scratch=[pltpu.VMEM((steps, eqs, share), BF16)],
        after=after,
        weight=WEIGHT,
        grid=(1,),
        out_specs=tuple(pl.BlockSpec(d, lambda i: (0, 0)) for d in dims),
    )
    return {s: outs[i * form.py : (i + 1) * form.py] for i, s in enumerate(ss)}


def pack_body(count, *refs):
    for k, part in enumerate(take(list(refs), count)):
        refs[-1][k] = part[...]


def pack(parts, after=()):
    count = sum(1 if x.ndim == 2 else x.shape[0] for x in parts)
    return call(
        functools.partial(pack_body, count),
        [shaped((count, *parts[0].shape[-2:]), BF16)],
        parts,
        [WHOLE] * len(parts),
        after=after,
        weight=WEIGHT,
    )[0]


def take(refs, count):
    got = []
    while len(got) < count:
        ref = refs.pop(0)
        got += [ref] if len(ref.shape) == 2 else [ref.at[k] for k in range(ref.shape[0])]
    return got


def diag_body(form, terms, meta, *refs):
    chips, n_cols, depth, eqs, width, sides = form.chips, form.n_cols, form.depth, form.eqs, form.width, form.sides
    refs = list(refs)
    held = take(refs, n_cols * chips)
    sums = [refs.pop(0) for _ in range(terms)]
    outs, product = refs[:-1], refs[-1]
    sub = width // depth
    if terms:
        total = sums[0][...]
        for x in sums[1:]:
            total = total + x[...].astype(F32)
        residual = (-total).astype(BF16)
    else:
        right = pl.ds(pl.multiple_of(width + meta[1] * sides, sides), sides)
        residual = jnp.concatenate([held[k][:, right] for k in range(chips)], axis=0)
    for c in range(n_cols):
        for h in range(width // eqs):
            rows = jnp.concatenate(
                [held[c * chips + k][:, h * eqs : (h + 1) * eqs] for k in range(chips)], axis=1
            )
            product[c, h * eqs : (h + 1) * eqs] = jnp.dot(rows, residual, preferred_element_type=F32)
    for k in range(depth):
        at = pl.multiple_of(lax.rem(meta[2] + depth - k, depth) * sub, sub)
        for c in range(n_cols):
            outs[k][c * sub : (c + 1) * sub] = product[c, pl.ds(at, sub)].astype(outs[k].dtype)


def diag_product(form, meta, held, sums, after=()):
    width, eqs, sides, depth, n_cols, chips = form.width, form.eqs, form.sides, form.depth, form.n_cols, form.chips
    dims = (n_cols * (width // depth), sides)
    return call(
        functools.partial(diag_body, form, len(sums)),
        [shaped(dims, F32)] + [shaped(dims, BF16)] * (depth - 1),
        [meta, *held, *sums],
        [SMALL] + [WHOLE] * (len(held) + len(sums)),
        flops=2 * n_cols * width * chips * eqs * sides,
        scratch=[pltpu.VMEM((n_cols, width, sides), F32)],
        after=after,
    )


def put_pieces(form, meta, pieces, outs):
    depth, sub = form.depth, form.width // form.depth
    for k in range(depth):
        at = pl.multiple_of(lax.rem(meta[2] + depth - k, depth) * sub, sub)
        for c in range(form.n_cols):
            outs[c][pl.ds(at, sub)] = pieces[k][c * sub : (c + 1) * sub]


def lower_body(s, form, meta, *refs):
    chips, n_cols, eqs = form.chips, form.n_cols, form.eqs
    refs = list(refs)
    held = {s: take(refs, n_cols * chips)}
    if s > 2:
        held[s - 1] = take(refs, n_cols * chips)
    width = form.width
    known = [[refs.pop(0) for _ in range(n_cols)] for _ in range(s - 1)]
    pieces = [refs.pop(0) for _ in range(form.depth)]
    own = refs.pop(0)
    far = [refs.pop(0) for _ in range(form.px - 1)]
    outs, newest = refs[: form.py], refs[form.py :]
    put_pieces(form, meta, pieces, newest)
    total = None
    for t, blocks in enumerate(known + [newest]):
        for c in range(n_cols):
            by, slot = slot_of(s, t, form.steps)
            lanes = slice(slot * width, (slot + 1) * width)
            rows = jnp.concatenate([held[by][c * chips + k][:, lanes] for k in range(chips)], axis=0)
            term = jnp.dot(rows, blocks[c][...], preferred_element_type=F32)
            total = term if total is None else total + term
    parts = [total[k * eqs : (k + 1) * eqs] for k in range(chips)]
    lane = width + (form.px + s - 1) * form.sides
    for k, (dy, dx) in enumerate(form.shifts):
        if dy == 0:
            right = far[dx - 1][:, lane : lane + form.sides] if dx else own[s]
            parts[k] = parts[k] - right.astype(F32)
    for e in range(form.py):
        for k, (dy, dx) in enumerate(form.shifts):
            mine = form.shifts.index(((dy - e) % form.py, dx))
            outs[e][k * eqs : (k + 1) * eqs] = parts[mine].astype(outs[e].dtype)


def lower_product(s, form, meta, held, older, known, pieces, own, far, after=()):
    rows, sides = form.chips * form.eqs, form.sides
    flat = [x for blocks in known for x in blocks]
    ins = [meta, *held, *(older if s > 2 else []), *flat, *pieces, own, *far]
    return call(
        functools.partial(lower_body, s, form),
        [shaped((rows, sides), F32)]
        + [shaped((rows, sides), BF16)] * (form.py - 1)
        + [shaped((form.width, sides), BF16)] * form.n_cols,
        ins,
        [SMALL] + [WHOLE] * (len(ins) - 1),
        flops=2 * s * form.n_cols * form.width * rows * sides,
        after=after,
    )


def place_body(form, meta, *refs):
    put_pieces(form, meta, refs[: form.depth], refs[form.depth :])


def place(form, meta, pieces, after=()):
    return call(
        functools.partial(place_body, form),
        [shaped((form.width, form.sides), BF16)] * form.n_cols,
        [meta, *pieces],
        [SMALL] + [WHOLE] * form.depth,
        after=after,
    )


def gate_body(*refs):
    pass


def gate(x, after):
    return call(
        gate_body,
        [shaped(x.shape, x.dtype)],
        [x],
        [pl.BlockSpec(memory_space=pl.ANY)],
        after=after,
        out_specs=(pl.BlockSpec(memory_space=pl.ANY),),
        input_output_aliases={0: 0},
    )[0]


def join_body(form, count, meta, *refs):
    width, sides = form.width, form.sides
    for i in range(count):
        for k in range(form.n_cols):
            at = pl.multiple_of(lax.rem(meta[3] + k, form.n_cols) * sides, sides)
            refs[-1][i * width : (i + 1) * width, pl.ds(at, sides)] = refs[i * form.n_cols + k][...]


def join(form, meta, parts, after=()):
    count = len(parts) // form.n_cols
    return call(
        functools.partial(join_body, form, count),
        [shaped((count * form.width, form.n_cols * form.sides), BF16)],
        [meta, *parts],
        [SMALL] + [WHOLE] * len(parts),
        after=after,
    )[0]


def flat_body(x, *refs):
    refs[-2][...] = jnp.swapaxes(x[...], 0, 1)
    refs[-1][...] = jnp.zeros_like(refs[-1])


def flat_rest(lower_rest, buffer, turn, turns, block, after=()):
    rest, steps, share = lower_rest.shape
    first = turn * (rest // turns // block)
    ins, alias = [lower_rest], {}
    specs = [pl.BlockSpec((block, steps, share), lambda i: (first + i, 0, 0))]
    if buffer is not None:
        alias = {1: 0}
        ins.append(buffer)
        specs.append(pl.BlockSpec(memory_space=pltpu.HBM))
    return call(
        flat_body,
        [pltpu.HBM((steps, rest, share), BF16), shaped((8, 128), F32)],
        ins,
        specs,
        after=after,
        grid=(rest // turns // block,),
        out_specs=(
            pl.BlockSpec((steps, block, share), lambda i: (0, first + i, 0)),
            pl.BlockSpec((8, 128), lambda i: (0, 0)),
        ),
        input_output_aliases=alias,
    )


def write_body(form, count, meta, *refs):
    parts = take(list(refs), form.chips)
    put_solved(form, count, meta, parts, *refs[-2:])


def put_solved(form, count, meta, parts, out, turned):
    width, sides = form.width, form.sides
    for i in range(count):
        for k, (dy, dx) in enumerate(form.shifts):
            y, x = lax.rem(meta[0] + form.py - dy, form.py), lax.rem(meta[1] + form.px - dx, form.px)
            block = parts[k][i * width : (i + 1) * width]
            row = pl.ds(pl.multiple_of(y * width, width), width)
            for c in range(form.n_cols):
                lane = pl.ds(pl.multiple_of((c * form.px + x) * sides, sides), sides)
                piece = block[:, c * sides : (c + 1) * sides]
                out[i, row, lane] = piece
                turned[i, lane, row] = piece.T


def write(s, steps, form, meta, parts, buffer, after=()):
    share, total = form.py * form.width, form.px * form.n_cols * form.sides
    count = parts[0].shape[-2] // form.width
    ins = [meta, *parts]
    specs = [SMALL] + [pl.BlockSpec(x.shape, lambda i, n=x.ndim: (0,) * n) for x in parts]
    alias = {}
    if buffer is not None:
        alias = {len(ins): 0}
        ins.append(buffer)
        specs.append(pl.BlockSpec(memory_space=pltpu.HBM))
    return call(
        functools.partial(write_body, form, count),
        [pltpu.HBM((steps, share, total), BF16), shaped((count, total, share), BF16)],
        ins,
        specs,
        after=after,
        grid=(1,),
        out_specs=(
            pl.BlockSpec((count, share, total), lambda i: (s // count, 0, 0)),
            pl.BlockSpec((count, total, share), lambda i: (0, 0, 0)),
        ),
        input_output_aliases=alias,
    )


def rest_body(form, counts, running, meta, *refs):
    turned, lower, refs = refs[: len(counts)], refs[len(counts)], refs[len(counts) + 1 :]
    before, outs = refs[:running], refs[running:]
    sides = form.px * form.sides
    for order, out in enumerate(outs):
        at = pl.multiple_of(lax.rem(meta[3] + order, form.n_cols) * sides, sides)
        total, t = None, 0
        for x, count in zip(turned, counts):
            for i in range(count):
                term = nt_dot(x[i, pl.ds(at, sides), :], lower[t])
                total = term if total is None else total + term
                t += 1
        if running:
            total = total + before[order][...].astype(F32)
        out[...] = total.astype(out.dtype)


def rest_product(first, form, meta, turned, lower, before=(), after=()):
    orders = range(form.n_cols)
    _, rest, share = lower.shape
    counts = [x.shape[0] for x in turned]
    count = sum(counts)
    sides = form.px * form.sides
    block = max(n for n in (768, 512, 384, 256, 128) if rest % n == 0)
    side_block = pl.BlockSpec((sides, block), lambda i: (0, i))
    return call(
        functools.partial(rest_body, form, counts, len(before)),
        [shaped((sides, rest), F32 if order == 0 else BF16) for order in orders],
        [meta, *turned, pltpu.with_memory_space_constraint(lower, pltpu.HBM), *before],
        [SMALL]
        + [pl.BlockSpec(x.shape, lambda i: (0, 0, 0)) for x in turned]
        + [pl.BlockSpec((count, block, share), lambda i: (first // count, i, 0))]
        + [side_block] * len(before),
        flops=2 * count * share * sides * rest * len(orders),
        after=after,
        grid=(rest // block,),
        out_specs=(side_block,) * len(orders),
    )


def last_body(form, meta, *refs):
    refs = list(refs)
    parts = take(refs, form.chips)
    lower, _, out, *sums, turned = refs

    @pl.when(pl.program_id(0) == 0)
    def _():
        put_solved(form, 1, meta, parts, out, turned)

    sides = form.px * form.sides
    for order, to in enumerate(sums):
        at = pl.multiple_of(lax.rem(meta[3] + order, form.n_cols) * sides, sides)
        to[...] = nt_dot(turned[0, pl.ds(at, sides), :], lower[0]).astype(to.dtype)


def last_step(form, meta, parts, lower, buffer):
    steps, rest, share = lower.shape
    total, sides = form.px * form.n_cols * form.sides, form.px * form.sides
    block = max(n for n in (768, 512, 384, 256, 128) if rest % n == 0)
    lower = pltpu.with_memory_space_constraint(lower, pltpu.HBM)
    side_block = pl.BlockSpec((sides, block), lambda i: (0, i))
    return call(
        functools.partial(last_body, form),
        [pltpu.HBM((steps, share, total), BF16)]
        + [shaped((sides, rest), F32 if order == 0 else BF16) for order in range(form.n_cols)],
        [meta, *parts, lower, buffer],
        [SMALL]
        + [pl.BlockSpec(x.shape, lambda i, n=x.ndim: (0,) * n) for x in parts]
        + [pl.BlockSpec((1, block, share), lambda i: (steps - 1, i, 0))]
        + [pl.BlockSpec(memory_space=pltpu.HBM)],
        flops=2 * share * total * rest,
        scratch=[pltpu.VMEM((1, total, share), BF16)],
        grid=(rest // block,),
        out_specs=(pl.BlockSpec((1, share, total), lambda i: (steps - 1, 0, 0)), *[side_block] * form.n_cols),
        input_output_aliases={len(parts) + 2: 0},
    )


@dataclasses.dataclass
class Form:
    py: int
    px: int
    depth: int
    n_cols: int
    eqs: int
    width: int
    sides: int
    steps: int

    def __post_init__(self):
        self.shifts = [(dy, dx) for dx in range(self.px) for dy in range(self.py)]
        self.chips = len(self.shifts)


def form_of(lower_pivot, rhs_pivot):
    n_rows = lax.axis_size("rows")
    plane = split_of(n_rows)
    px = split_of(plane)
    py = plane // px
    return Form(
        py, px, n_rows // plane, lax.axis_size("cols"), lower_pivot.shape[1], lower_pivot.shape[3] // py,
        rhs_pivot.shape[2] // px, lower_pivot.shape[0],
    )


def kernel_path(form, lower_pivot, lower_rest, diag_inverse, rhs_pivot, rhs_rest):
    lower_pivot, lower_rest, diag_inverse, rhs_pivot = (
        pltpu.with_memory_space_constraint(x, pltpu.HBM) for x in (lower_pivot, lower_rest, diag_inverse, rhs_pivot)
    )
    steps = lower_pivot.shape[0]
    rest = lower_rest.shape[0]
    py, px, depth, n_cols, chips = form.py, form.px, form.depth, form.n_cols, form.chips
    row = lax.axis_index("rows")
    meta = jnp.stack([row // px % py, row % px, row // chips, lax.axis_index("cols")]).astype(jnp.int32)

    def along_plane(x, dy, dx):
        pairs = [
            ((b * py + y) * px + i, (b * py + (y + dy) % py) * px + (i + dx) % px)
            for b in range(depth)
            for y in range(py)
            for i in range(px)
        ]
        return lax.ppermute(x, "rows", pairs)

    def along_depth(x, k):
        pairs = [(b * chips + i, (b + k) % depth * chips + i) for b in range(depth) for i in range(chips)]
        return lax.ppermute(x, "rows", pairs)

    def along_cols(x, k):
        return lax.ppermute(x, "cols", [(i, (i + k) % n_cols) for i in range(n_cols)])

    def up(blocks):
        return [blocks[0]] + [along_plane(blocks[dy], dy, 0) for dy in range(1, py)]

    def across(x):
        return [along_plane(x, 0, dx) for dx in range(1, px)]

    def onward(first, direct, after=()):
        rest = [gate(x, after) if after else x for x in first[1:]]
        far = [across(x) for x in rest]
        got = [first[0], *rest]
        for dx in range(px - 1):
            got += [direct[dx]] + [x[dx] for x in far]
        return got

    def held_of(parts, after):
        mine = [pack(parts, after)] if after else parts
        return mine + [along_cols(x, c) for c in range(1, n_cols) for x in mine]

    def joined(ts, after=()):
        parts = []
        for t in ts:
            parts += [known[t][0]] + [along_cols(known[t][k], -k) for k in range(1, n_cols)]
        return join(form, meta, parts, after)

    turns = 3
    block = 128
    while rest % (turns * block):
        turns -= 1
    last = steps - 1
    near, far, own = start(form, meta, diag_inverse, rhs_pivot)
    got = up(near)
    here = [along_plane(x, 0, dx + 1) for dx, x in enumerate(far)]
    packed = prep(tuple(range(1, steps)), form, meta, diag_inverse, lower_pivot)
    first = up([gate(x, got[1:]) for x in packed[1]])
    got = onward(got, here, [packed[1][0]])
    later = [gate(x, [*got[py + 1 :], *first[1:]]) for x in got[py :: py]]
    held = held_of([later[k // py - 1] if k >= py and k % py == 0 else x for k, x in enumerate(got)], ())
    moved = pack(first)
    moved = [moved, *across(moved)]
    known, sums, turned, flat, buffer = [], [], [], None, None
    by_lower, by_diag, by_sum = ({s: [] for s in range(steps + 1)} for _ in range(3))
    by_diag[0] += [packed[last][0], *first[1:]]
    by_sum[0] += moved
    for s in range(steps):
        if s > 0:
            outs = lower_product(s, form, meta, held, older, known, pieces, own, here, by_lower[s])
            known.append(outs[py:])
            sums = [outs[0]] + [along_plane(outs[e], e, 0) for e in range(1, py)]
            if s >= last - 1:
                whole = joined(range(s) if s < last else [s - 1], [outs[0]])
                by_diag[s].append(whole)
        products = diag_product(form, meta, held, sums, by_diag[s])
        if s < last - 1:
            first = up([gate(x, [products[0]]) for x in packed[s + 2]])
        else:
            first = up([gate(whole, [products[0]])] * py)
        by_sum[s] += first[1:]
        arrivals = [along_depth(products[k], -k) for k in range(1, depth)]
        arrivals[-1] = gate(arrivals[-1], by_sum[s])
        total = products[0]
        for x in arrivals:
            total = total + x.astype(F32)
        mine = total.astype(BF16)
        if s < last:
            held, older = held_of(moved, [mine]), held
        ready, moved = moved, pack(first, [mine])
        moved = [moved, *across(moved)]
        by_sum[s + 1] += moved if s < last else []
        pieces = [mine] + [along_depth(mine, k) for k in range(1, depth)]
        if s < turns:
            flat, mark = flat_rest(lower_rest, flat, s, turns, block, [mine])
            by_lower[s + 1].append(mark)
        if s == last:
            buffer, new = write(0, steps, form, meta, ready, buffer, [mine])
            turned.append(new)
            by_lower[s + 1].append(new)
    known.append(place(form, meta, pieces, by_lower[steps]))
    whole = joined([last])
    got = up([whole] * py)
    direct = across(got[0])
    early = rest_product(0, form, meta, turned, flat, (), [whole, *moved])
    got = onward(got, direct, [early[0]])
    buffer, new = write(last - 1, steps, form, meta, moved, buffer, [early[0]])
    early = rest_product(last - 1, form, meta, [new], flat, early)
    buffer, *late = last_step(form, meta, got, flat, buffer)
    total = rhs_rest.astype(F32) - early[0] - late[0]
    for c in range(1, n_cols):
        total = total - along_cols(early[c], c).astype(F32) - along_cols(late[c], c).astype(F32)
    return buffer, total.astype(BF16)


def per_device(lower_pivot, lower_rest, diag_inverse, rhs_pivot, rhs_rest):
    form = form_of(lower_pivot, rhs_pivot)
    fits = form.eqs % 128 == 0 and form.width % form.eqs == 0 and form.sides % 128 == 0
    fits = fits and (form.width // form.depth) % 16 == 0 and lower_rest.shape[0] % 128 == 0
    if fits:
        return kernel_path(form, lower_pivot, lower_rest, diag_inverse, rhs_pivot, rhs_rest)
    return plain_path(lower_pivot, lower_rest, diag_inverse, rhs_pivot, rhs_rest)


def solution(mesh):
    placed = (
        P(None, "rows", None, "cols"),
        P("rows", None, "cols"),
        P(None, "cols", "rows"),
        P(None, "rows", "cols"),
        P("cols", "rows"),
    )
    return jax.shard_map(
        per_device,
        mesh=mesh,
        in_specs=placed,
        out_specs=(P(None, "cols", None), P("cols", "rows")),
        check_vma=False,
    )
```

```python
import dataclasses
import functools
import math

import jax
import jax.numpy as jnp
from jax import lax
from jax.sharding import PartitionSpec as P
from jax.experimental import pallas as pl
from jax.experimental.pallas import tpu as pltpu

F32 = jnp.float32
BF16 = jnp.bfloat16


def split_of(count):
    best = 1
    for d in range(1, count + 1):
        if count % d == 0 and d * d <= count:
            best = d
    return best


def nt_dot(a, b):
    return lax.dot_general(a, b, (((1,), (1,)), ((), ())), preferred_element_type=F32)


def cut(n_rows, share):
    plane = split_of(n_rows)
    power = plane & (plane - 1) == 0
    code = [g ^ (g >> 1) if power else g for g in range(plane)]
    return plane, n_rows // plane, share // plane, code


def places(plane, code):
    row = lax.axis_index("rows")
    spot = row % plane
    g = sum(jnp.where(spot == code[i], i, 0) for i in range(plane))
    return g, row // plane, lax.axis_index("cols")


def movers(plane, depth, code, n_cols):
    def along_plane(x, k):
        pairs = [(b * plane + code[i], b * plane + code[(i + k) % plane]) for b in range(depth) for i in range(plane)]
        return lax.ppermute(x, "rows", pairs)

    def along_depth(x, k):
        pairs = [(b * plane + i, ((b + k) % depth) * plane + i) for b in range(depth) for i in range(plane)]
        return lax.ppermute(x, "rows", pairs)

    def along_cols(x, k):
        return lax.ppermute(x, "cols", [(i, (i + k) % n_cols) for i in range(n_cols)])

    return along_plane, along_depth, along_cols


def plain_path(lower_pivot, lower_rest, diag_inverse, rhs_pivot, rhs_rest):
    steps = lower_pivot.shape[0]
    eqs = lower_pivot.shape[1]
    share = lower_pivot.shape[3]
    sides = rhs_pivot.shape[2]
    rest = lower_rest.shape[0]
    n_rows = lax.axis_size("rows")
    n_cols = lax.axis_size("cols")
    plane, depth, width, code = cut(n_rows, share)
    g, z, core = places(plane, code)
    part = sides // depth
    along_plane, along_depth, along_cols = movers(plane, depth, code, n_cols)

    def gather(move, count, x, axis):
        return jnp.concatenate([x] + [move(x, k) for k in range(1, count)], axis=axis)

    def my_diag(s):
        block = diag_inverse[s].reshape(plane, width, eqs)
        parts = [lax.dynamic_index_in_dim(block, (g + k) % plane, 0, False) for k in range(plane)]
        held = jnp.concatenate([parts[0]] + [along_plane(parts[k], k) for k in range(1, plane)], axis=1)
        return gather(along_cols, n_cols, held, 0)

    def my_lower(s):
        parts = [
            lax.dynamic_slice_in_dim(lower_pivot[s, :, :s, :], ((g + k) % plane) * width, width, 2)
            for k in range(plane)
        ]
        held = jnp.concatenate([parts[0]] + [along_plane(parts[k], k) for k in range(1, plane)], axis=0)
        return gather(along_cols, n_cols, held, 2)

    def rolled(x, shift, axis):
        return jnp.roll(x, shift, axis)

    rhs_t = jnp.swapaxes(rhs_pivot, 1, 2)
    blocks = rhs_t.reshape(steps, depth, part, eqs)[:, ::-1]
    blocks = rolled(blocks, z + 1, 1).reshape(steps, sides, eqs)

    solved = []
    totals = jnp.zeros((sides, rest), F32)
    outs = []
    for s in range(steps):
        diag = my_diag(s)
        if s == 0:
            own = blocks[0]
        else:
            lower = my_lower(s)
            partial = jnp.zeros((sides, plane * eqs), F32)
            for t in range(s):
                partial = partial + nt_dot(solved[t], lower[:, t, :])
            total = blocks[s].astype(F32) - partial[:, :eqs]
            sent = partial.astype(BF16)
            for k in range(1, plane):
                total = total - along_plane(sent[:, k * eqs : (k + 1) * eqs], -k).astype(F32)
            own = total.astype(BF16)
        residual = gather(along_plane, plane, own, 1)
        product = nt_dot(residual, diag)
        sent = product.astype(BF16)
        total = product[:part]
        for k in range(1, depth):
            total = total + along_depth(sent[k * part : (k + 1) * part], -k).astype(F32)
        mine = total.astype(BF16)
        here = gather(along_depth, depth, mine, 0)
        solved.append(here)
        pieces = [here] + [along_plane(here, k) for k in range(1, plane)]
        pieces = [pieces[(-k) % plane] for k in range(plane)]
        full = jnp.stack([p.reshape(depth, part, n_cols, width) for p in pieces], axis=3)
        full = full[jnp.array([(-k) % depth for k in range(depth)])]
        full = rolled(full, z, 0)
        full = rolled(full, g, 3).reshape(sides, n_cols, share)
        rest_parts = [lower_rest[:, s, :]] + [along_cols(lower_rest[:, s, :], k) for k in range(1, n_cols)]
        for k in range(n_cols):
            totals = totals + nt_dot(full[:, k, :], rest_parts[k])
        theirs = [full[:, 0]] + [along_cols(full[:, k], -k) for k in range(1, n_cols)]
        theirs = rolled(jnp.stack(theirs, 0), core, 0).reshape(n_cols * sides, share)
        outs.append(theirs.T)
    remainder = (rhs_rest.astype(F32) - totals).astype(BF16)
    return jnp.stack(outs), remainder


VMEM_LIMIT = 40 * 1024 * 1024
WEIGHT = 8
SMALL = pl.BlockSpec(memory_space=pltpu.SMEM)
WHOLE = pl.BlockSpec(memory_space=pltpu.VMEM)


def call(body, outs, ins, specs, flops=0, scratch=(), after=(), weight=1, **more):
    size = sum(math.prod(x.shape) * x.dtype.itemsize for x in [*ins, *outs])
    first, last = len(ins), len(ins) + len(after)

    def run(*refs):
        body(*refs[:first], *refs[last:])

    return pl.pallas_call(
        run,
        out_shape=tuple(outs),
        in_specs=list(specs) + [pl.BlockSpec(memory_space=pl.ANY)] * len(after),
        scratch_shapes=list(scratch),
        compiler_params=pltpu.CompilerParams(vmem_limit_bytes=VMEM_LIMIT),
        cost_estimate=pl.CostEstimate(flops=flops, bytes_accessed=size * weight, transcendentals=0),
        **more,
    )(*ins, *after)


def shaped(dims, kind):
    return jax.ShapeDtypeStruct(dims, kind)


def put_diag(form, meta, dy, block, out):
    at = lax.rem(meta[0] + dy, form.py) * form.width
    for h in range(form.width // form.eqs):
        lanes = slice(h * form.eqs, (h + 1) * form.eqs)
        out[:, lanes] = block[pl.ds(pl.multiple_of(at + h * form.eqs, form.eqs), form.eqs), :]


def start_body(form, meta, diag, rhs, *refs):
    py, px, width, sides = form.py, form.px, form.width, form.sides
    own, outs, far = refs[-1], refs[:py], refs[py:-1]

    def part(s, dx):
        return rhs[s, :, pl.ds(pl.multiple_of(lax.rem(meta[1] + dx, px) * sides, sides), sides)]

    for dy in range(py):
        put_diag(form, meta, dy, diag.at[0], outs[dy])
        outs[dy][:, width:] = rhs[0]
    for dx in range(1, px):
        out = far[dx - 1]
        put_diag(form, meta, 0, diag.at[0], out)
        out[:, width : width + px * sides] = rhs[0]
        for s in range(1, rhs.shape[0]):
            out[:, width + (px + s - 1) * sides : width + (px + s) * sides] = part(s, dx)
    for s in range(rhs.shape[0]):
        own[s] = part(s, 0)


def start(form, meta, diag_inverse, rhs_pivot):
    width, eqs, sides, share = form.width, form.eqs, form.sides, form.py * form.width
    steps = rhs_pivot.shape[0]
    dims = [(eqs, width + form.px * sides)] * form.py
    dims += [(eqs, width + (form.px + steps - 1) * sides)] * (form.px - 1) + [(steps, eqs, sides)]
    outs = call(
        functools.partial(start_body, form),
        [shaped(d, BF16) for d in dims],
        [meta, diag_inverse, rhs_pivot],
        [
            SMALL,
            pl.BlockSpec((1, share, eqs), lambda i: (0, 0, 0)),
            pl.BlockSpec(rhs_pivot.shape, lambda i: (0, 0, 0)),
        ],
        weight=WEIGHT,
        grid=(1,),
        out_specs=tuple(pl.BlockSpec(d, lambda i, n=len(d): (0,) * n) for d in dims),
    )
    return outs[: form.py], outs[form.py : -1], outs[-1]


def slots(s):
    return [t for t in range(s) if s < 3 or t > 0], [0] if s > 2 else []


def slot_of(s, t):
    later, ahead = slots(s)
    return 1 + (later + ahead).index(t)


def prep_body(ss, form, meta, diag, lower, *refs):
    py, width = form.py, form.width
    refs, flat = list(refs[:-1]), refs[-1]
    for i, s in enumerate(ss):
        flat[...] = jnp.swapaxes(lower[i], 0, 1)
        later, ahead = slots(s)
        outs = [refs.pop(0) for _ in range(py)]
        early = [refs.pop(0) for _ in range(py)] if ahead else []
        for dy in range(py):
            put_diag(form, meta, dy, diag.at[i], outs[dy])
            at = pl.ds(pl.multiple_of(lax.rem(meta[0] + dy, py) * width, width), width)
            for j, t in enumerate(later):
                outs[dy][:, (1 + j) * width : (2 + j) * width] = flat[t, :, at]
            for j, t in enumerate(ahead):
                early[dy][:, j * width : (j + 1) * width] = flat[t, :, at]


def prep(ss, form, meta, diag_inverse, lower_pivot, after=()):
    width, eqs, share = form.width, form.eqs, form.py * form.width
    steps, count = lower_pivot.shape[0], len(ss)
    dims = []
    for s in ss:
        later, ahead = slots(s)
        dims += [(eqs, (1 + len(later)) * width)] * form.py + [(eqs, len(ahead) * width)] * (form.py if ahead else 0)
    outs = call(
        functools.partial(prep_body, ss, form),
        [shaped(d, BF16) for d in dims],
        [meta, diag_inverse, lower_pivot],
        [
            SMALL,
            pl.BlockSpec((pl.Element(count), pl.Element(share), pl.Element(eqs)), lambda i: (ss[0], 0, 0)),
            pl.BlockSpec(
                (pl.Element(count), pl.Element(eqs), pl.Element(steps), pl.Element(share)), lambda i: (ss[0], 0, 0, 0)
            ),
        ],
        scratch=[pltpu.VMEM((steps, eqs, share), BF16)],
        after=after,
        weight=WEIGHT,
        grid=(1,),
        out_specs=tuple(pl.BlockSpec(d, lambda i: (0, 0)) for d in dims),
    )
    packed, ahead, outs = {}, {}, list(outs)
    for s in ss:
        packed[s] = [outs.pop(0) for _ in range(form.py)]
        if slots(s)[1]:
            ahead[s] = [outs.pop(0) for _ in range(form.py)]
    return packed, ahead


def pack_body(count, first, *refs):
    refs = list(refs)
    for k, part in enumerate(take(refs, count)):
        refs[-1][k, :, :first] = part[...]
    for k in range(len(refs) - 1):
        refs[-1][k, :, first:] = refs[k][...]


def pack(parts, after=(), beside=()):
    count = sum(1 if x.ndim == 2 else x.shape[0] for x in parts)
    rows, first = parts[0].shape[-2:]
    lanes = first + (beside[0].shape[-1] if beside else 0)
    ins = [*parts, *beside]
    return call(
        functools.partial(pack_body, count, first),
        [shaped((count, rows, lanes), BF16)],
        ins,
        [WHOLE] * len(ins),
        after=after,
        weight=WEIGHT,
    )[0]


def take(refs, count):
    got = []
    while len(got) < count:
        ref = refs.pop(0)
        got += [ref] if len(ref.shape) == 2 else [ref.at[k] for k in range(ref.shape[0])]
    return got


def diag_body(form, terms, meta, *refs):
    chips, n_cols, depth, eqs, width, sides = form.chips, form.n_cols, form.depth, form.eqs, form.width, form.sides
    refs = list(refs)
    held = take(refs, n_cols * chips)
    sums = [refs.pop(0) for _ in range(terms)]
    outs, product = refs[:-1], refs[-1]
    sub = width // depth
    if terms:
        total = sums[0][...]
        for x in sums[1:]:
            total = total + x[...].astype(F32)
        residual = (-total).astype(BF16)
    else:
        right = pl.ds(pl.multiple_of(width + meta[1] * sides, sides), sides)
        residual = jnp.concatenate([held[k][:, right] for k in range(chips)], axis=0)
    for c in range(n_cols):
        for h in range(width // eqs):
            rows = jnp.concatenate(
                [held[c * chips + k][:, h * eqs : (h + 1) * eqs] for k in range(chips)], axis=1
            )
            product[c, h * eqs : (h + 1) * eqs] = jnp.dot(rows, residual, preferred_element_type=F32)
    for k in range(depth):
        at = pl.multiple_of(lax.rem(meta[2] + depth - k, depth) * sub, sub)
        for c in range(n_cols):
            outs[k][c * sub : (c + 1) * sub] = product[c, pl.ds(at, sub)].astype(outs[k].dtype)


def diag_product(form, meta, held, sums, after=()):
    width, eqs, sides, depth, n_cols, chips = form.width, form.eqs, form.sides, form.depth, form.n_cols, form.chips
    dims = (n_cols * (width // depth), sides)
    return call(
        functools.partial(diag_body, form, len(sums)),
        [shaped(dims, F32)] + [shaped(dims, BF16)] * (depth - 1),
        [meta, *held, *sums],
        [SMALL] + [WHOLE] * (len(held) + len(sums)),
        flops=2 * n_cols * width * chips * eqs * sides,
        scratch=[pltpu.VMEM((n_cols, width, sides), F32)],
        after=after,
    )


def put_pieces(form, meta, pieces, outs):
    depth, sub = form.depth, form.width // form.depth
    for k in range(depth):
        at = pl.multiple_of(lax.rem(meta[2] + depth - k, depth) * sub, sub)
        for c in range(form.n_cols):
            outs[c][pl.ds(at, sub)] = pieces[k][c * sub : (c + 1) * sub]


def lower_body(s, form, meta, *refs):
    chips, n_cols, eqs = form.chips, form.n_cols, form.eqs
    refs = list(refs)
    held = take(refs, n_cols * chips)
    width = form.width
    known = [[refs.pop(0) for _ in range(n_cols)] for _ in range(s - 1)]
    pieces = [refs.pop(0) for _ in range(form.depth)]
    own = refs.pop(0)
    far = [refs.pop(0) for _ in range(form.px - 1)]
    outs, newest = refs[: form.py], refs[form.py :]
    put_pieces(form, meta, pieces, newest)
    total = None
    for t, blocks in enumerate(known + [newest]):
        for c in range(n_cols):
            lanes = slice(slot_of(s, t) * width, (slot_of(s, t) + 1) * width)
            rows = jnp.concatenate([held[c * chips + k][:, lanes] for k in range(chips)], axis=0)
            term = jnp.dot(rows, blocks[c][...], preferred_element_type=F32)
            total = term if total is None else total + term
    parts = [total[k * eqs : (k + 1) * eqs] for k in range(chips)]
    lane = width + (form.px + s - 1) * form.sides
    for k, (dy, dx) in enumerate(form.shifts):
        if dy == 0:
            right = far[dx - 1][:, lane : lane + form.sides] if dx else own[s]
            parts[k] = parts[k] - right.astype(F32)
    for e in range(form.py):
        for k, (dy, dx) in enumerate(form.shifts):
            mine = form.shifts.index(((dy - e) % form.py, dx))
            outs[e][k * eqs : (k + 1) * eqs] = parts[mine].astype(outs[e].dtype)


def lower_product(s, form, meta, held, known, pieces, own, far, after=()):
    rows, sides = form.chips * form.eqs, form.sides
    flat = [x for blocks in known for x in blocks]
    ins = [meta, *held, *flat, *pieces, own, *far]
    return call(
        functools.partial(lower_body, s, form),
        [shaped((rows, sides), F32)]
        + [shaped((rows, sides), BF16)] * (form.py - 1)
        + [shaped((form.width, sides), BF16)] * form.n_cols,
        ins,
        [SMALL] + [WHOLE] * (len(ins) - 1),
        flops=2 * s * form.n_cols * form.width * rows * sides,
        after=after,
    )


def place_body(form, meta, *refs):
    put_pieces(form, meta, refs[: form.depth], refs[form.depth :])


def place(form, meta, pieces, after=()):
    return call(
        functools.partial(place_body, form),
        [shaped((form.width, form.sides), BF16)] * form.n_cols,
        [meta, *pieces],
        [SMALL] + [WHOLE] * form.depth,
        after=after,
    )


def gate_body(*refs):
    pass


def gate(x, after):
    return call(
        gate_body,
        [shaped(x.shape, x.dtype)],
        [x],
        [pl.BlockSpec(memory_space=pl.ANY)],
        after=after,
        out_specs=(pl.BlockSpec(memory_space=pl.ANY),),
        input_output_aliases={0: 0},
    )[0]


def join_body(form, count, meta, *refs):
    width, sides = form.width, form.sides
    for i in range(count):
        for k in range(form.n_cols):
            at = pl.multiple_of(lax.rem(meta[3] + k, form.n_cols) * sides, sides)
            refs[-1][i * width : (i + 1) * width, pl.ds(at, sides)] = refs[i * form.n_cols + k][...]


def join(form, meta, parts, after=()):
    count = len(parts) // form.n_cols
    return call(
        functools.partial(join_body, form, count),
        [shaped((count * form.width, form.n_cols * form.sides), BF16)],
        [meta, *parts],
        [SMALL] + [WHOLE] * len(parts),
        after=after,
    )[0]


def flat_body(x, *refs):
    refs[-2][...] = jnp.swapaxes(x[...], 0, 1)
    refs[-1][...] = jnp.zeros_like(refs[-1])


def flat_rest(lower_rest, buffer, turn, turns, block, after=()):
    rest, steps, share = lower_rest.shape
    first = turn * (rest // turns // block)
    ins, alias = [lower_rest], {}
    specs = [pl.BlockSpec((block, steps, share), lambda i: (first + i, 0, 0))]
    if buffer is not None:
        alias = {1: 0}
        ins.append(buffer)
        specs.append(pl.BlockSpec(memory_space=pltpu.HBM))
    return call(
        flat_body,
        [pltpu.HBM((steps, rest, share), BF16), shaped((8, 128), F32)],
        ins,
        specs,
        after=after,
        grid=(rest // turns // block,),
        out_specs=(
            pl.BlockSpec((steps, block, share), lambda i: (0, first + i, 0)),
            pl.BlockSpec((8, 128), lambda i: (0, 0)),
        ),
        input_output_aliases=alias,
    )


def write_body(form, count, meta, *refs):
    parts = take(list(refs), form.chips)
    put_solved(form, count, meta, parts, *refs[-2:])


def put_solved(form, count, meta, parts, out, turned):
    width, sides = form.width, form.sides
    for i in range(count):
        for k, (dy, dx) in enumerate(form.shifts):
            y, x = lax.rem(meta[0] + form.py - dy, form.py), lax.rem(meta[1] + form.px - dx, form.px)
            block = parts[k][i * width : (i + 1) * width]
            row = pl.ds(pl.multiple_of(y * width, width), width)
            for c in range(form.n_cols):
                lane = pl.ds(pl.multiple_of((c * form.px + x) * sides, sides), sides)
                piece = block[:, c * sides : (c + 1) * sides]
                out[i, row, lane] = piece
                turned[i, lane, row] = piece.T


def write(s, steps, form, meta, parts, buffer, after=()):
    share, total = form.py * form.width, form.px * form.n_cols * form.sides
    count = parts[0].shape[-2] // form.width
    ins = [meta, *parts]
    specs = [SMALL] + [pl.BlockSpec(x.shape, lambda i, n=x.ndim: (0,) * n) for x in parts]
    alias = {}
    if buffer is not None:
        alias = {len(ins): 0}
        ins.append(buffer)
        specs.append(pl.BlockSpec(memory_space=pltpu.HBM))
    return call(
        functools.partial(write_body, form, count),
        [pltpu.HBM((steps, share, total), BF16), shaped((count, total, share), BF16)],
        ins,
        specs,
        after=after,
        grid=(1,),
        out_specs=(
            pl.BlockSpec((count, share, total), lambda i: (s // count, 0, 0)),
            pl.BlockSpec((count, total, share), lambda i: (0, 0, 0)),
        ),
        input_output_aliases=alias,
    )


def rest_body(form, counts, running, meta, *refs):
    turned, lower, refs = refs[: len(counts)], refs[len(counts)], refs[len(counts) + 1 :]
    before, outs = refs[:running], refs[running:]
    sides = form.px * form.sides
    for order, out in enumerate(outs):
        at = pl.multiple_of(lax.rem(meta[3] + order, form.n_cols) * sides, sides)
        total, t = None, 0
        for x, count in zip(turned, counts):
            for i in range(count):
                term = nt_dot(x[i, pl.ds(at, sides), :], lower[t])
                total = term if total is None else total + term
                t += 1
        if running:
            total = total + before[order][...].astype(F32)
        out[...] = total.astype(out.dtype)


def rest_product(first, form, meta, turned, lower, before=(), after=()):
    orders = range(form.n_cols)
    _, rest, share = lower.shape
    counts = [x.shape[0] for x in turned]
    count = sum(counts)
    sides = form.px * form.sides
    block = max(n for n in (768, 512, 384, 256, 128) if rest % n == 0)
    side_block = pl.BlockSpec((sides, block), lambda i: (0, i))
    return call(
        functools.partial(rest_body, form, counts, len(before)),
        [shaped((sides, rest), F32 if order == 0 else BF16) for order in orders],
        [meta, *turned, pltpu.with_memory_space_constraint(lower, pltpu.HBM), *before],
        [SMALL]
        + [pl.BlockSpec(x.shape, lambda i: (0, 0, 0)) for x in turned]
        + [pl.BlockSpec((count, block, share), lambda i: (first // count, i, 0))]
        + [side_block] * len(before),
        flops=2 * count * share * sides * rest * len(orders),
        after=after,
        grid=(rest // block,),
        out_specs=(side_block,) * len(orders),
    )


def last_body(form, running, meta, *refs):
    refs = list(refs)
    parts = take(refs, form.chips)
    lower, before, (out, *sums, turned) = refs[0], refs[1 : 1 + running], refs[2 + running :]

    @pl.when(pl.program_id(0) == 0)
    def _():
        put_solved(form, 1, meta, parts, out, turned)

    sides = form.px * form.sides
    for order, to in enumerate(sums):
        at = pl.multiple_of(lax.rem(meta[3] + order, form.n_cols) * sides, sides)
        total = nt_dot(turned[0, pl.ds(at, sides), :], lower[0])
        if running:
            total = total + before[order][...].astype(F32)
        to[...] = total.astype(to.dtype)


def late_step(s, form, meta, parts, lower, buffer, before=(), after=()):
    steps, rest, share = lower.shape
    total, sides = form.px * form.n_cols * form.sides, form.px * form.sides
    block = max(n for n in (768, 512, 384, 256, 128) if rest % n == 0)
    lower = pltpu.with_memory_space_constraint(lower, pltpu.HBM)
    side_block = pl.BlockSpec((sides, block), lambda i: (0, i))
    return call(
        functools.partial(last_body, form, len(before)),
        [pltpu.HBM((steps, share, total), BF16)]
        + [shaped((sides, rest), F32 if order == 0 else BF16) for order in range(form.n_cols)],
        [meta, *parts, lower, *before, buffer],
        [SMALL]
        + [pl.BlockSpec(x.shape, lambda i, n=x.ndim: (0,) * n) for x in parts]
        + [pl.BlockSpec((1, block, share), lambda i: (s, i, 0))]
        + [side_block] * len(before)
        + [pl.BlockSpec(memory_space=pltpu.HBM)],
        flops=2 * share * total * rest,
        scratch=[pltpu.VMEM((1, total, share), BF16)],
        after=after,
        grid=(rest // block,),
        out_specs=(pl.BlockSpec((1, share, total), lambda i: (s, 0, 0)), *[side_block] * form.n_cols),
        input_output_aliases={len(parts) + 2 + len(before): 0},
    )


@dataclasses.dataclass
class Form:
    py: int
    px: int
    depth: int
    n_cols: int
    eqs: int
    width: int
    sides: int

    def __post_init__(self):
        self.shifts = [(dy, dx) for dx in range(self.px) for dy in range(self.py)]
        self.chips = len(self.shifts)


def form_of(lower_pivot, rhs_pivot):
    n_rows = lax.axis_size("rows")
    plane = split_of(n_rows)
    px = split_of(plane)
    py = plane // px
    return Form(
        py, px, n_rows // plane, lax.axis_size("cols"), lower_pivot.shape[1], lower_pivot.shape[3] // py,
        rhs_pivot.shape[2] // px,
    )


def kernel_path(form, lower_pivot, lower_rest, diag_inverse, rhs_pivot, rhs_rest):
    lower_pivot, lower_rest, diag_inverse, rhs_pivot = (
        pltpu.with_memory_space_constraint(x, pltpu.HBM) for x in (lower_pivot, lower_rest, diag_inverse, rhs_pivot)
    )
    steps = lower_pivot.shape[0]
    rest = lower_rest.shape[0]
    py, px, depth, n_cols, chips = form.py, form.px, form.depth, form.n_cols, form.chips
    row = lax.axis_index("rows")
    meta = jnp.stack([row // px % py, row % px, row // chips, lax.axis_index("cols")]).astype(jnp.int32)

    def along_plane(x, dy, dx):
        pairs = [
            ((b * py + y) * px + i, (b * py + (y + dy) % py) * px + (i + dx) % px)
            for b in range(depth)
            for y in range(py)
            for i in range(px)
        ]
        return lax.ppermute(x, "rows", pairs)

    def along_depth(x, k):
        pairs = [(b * chips + i, (b + k) % depth * chips + i) for b in range(depth) for i in range(chips)]
        return lax.ppermute(x, "rows", pairs)

    def along_cols(x, k):
        return lax.ppermute(x, "cols", [(i, (i + k) % n_cols) for i in range(n_cols)])

    def up(blocks):
        return [blocks[0]] + [along_plane(blocks[dy], dy, 0) for dy in range(1, py)]

    def across(x):
        return [along_plane(x, 0, dx) for dx in range(1, px)]

    def onward(first, direct, after=()):
        rest = [gate(x, after) if after else x for x in first[1:]]
        far = [across(x) for x in rest]
        got = [first[0], *rest]
        for dx in range(px - 1):
            got += [direct[dx]] + [x[dx] for x in far]
        return got

    def held_of(parts, after):
        mine = [pack(parts, after)] if after else parts
        return mine + [along_cols(x, c) for c in range(1, n_cols) for x in mine]

    def joined(ts, after=()):
        parts = []
        for t in ts:
            parts += [known[t][0]] + [along_cols(known[t][k], -k) for k in range(1, n_cols)]
        return join(form, meta, parts, after)

    turns = 3
    block = 128
    while rest % (turns * block):
        turns -= 1
    last = steps - 1
    near, far, own = start(form, meta, diag_inverse, rhs_pivot)
    got = up(near)
    here = [along_plane(x, 0, dx + 1) for dx, x in enumerate(far)]
    packed, ahead = prep(tuple(range(1, steps)), form, meta, diag_inverse, lower_pivot)
    first = up([gate(x, got[1:]) for x in packed[1]])
    got = onward(got, here, [packed[1][0]])
    later = [gate(x, [*got[py + 1 :], *first[1:]]) for x in got[py :: py]]
    held = held_of([later[k // py - 1] if k >= py and k % py == 0 else x for k, x in enumerate(got)], ())
    moved = pack(first)
    moved = [moved, *across(moved)]
    known, sums, turned, flat, buffer = [], [], [], None, None
    by_lower, by_diag, by_sum = ({s: [] for s in range(steps + 1)} for _ in range(3))
    by_diag[0] += [packed[last][0], *first[1:]]
    by_sum[0] += moved
    for s in range(steps):
        if s > 0:
            outs = lower_product(s, form, meta, held, known, pieces, own, here, by_lower[s])
            known.append(outs[py:])
            sums = [outs[0]] + [along_plane(outs[e], e, 0) for e in range(1, py)]
            if s >= last - 1:
                whole = joined(range(s) if s < last else [s - 1], [outs[0]])
                by_diag[s].append(whole)
        products = diag_product(form, meta, held, sums, by_diag[s])
        if s < last - 1:
            first = up([gate(x, [products[0]]) for x in packed[s + 2]])
        else:
            first = up([gate(whole, [products[0]])] * py)
        by_sum[s] += first[1:]
        if s < turns and s % 2 == 0:
            flat, mark = flat_rest(lower_rest, flat, s, turns, block, [products[0]])
            by_sum[s].append(mark)
        arrivals = [along_depth(products[k], -k) for k in range(1, depth)]
        arrivals[-1] = gate(arrivals[-1], by_sum[s])
        total = products[0]
        for x in arrivals:
            total = total + x.astype(F32)
        mine = total.astype(BF16)
        if s < last:
            held = held_of(moved, [mine])
        pieces = [mine] + [along_depth(mine, k) for k in range(1, depth)]
        ready, moved = moved, pack(first, [mine], ahead.get(s + 2, ()))
        moved = [moved, *across(moved)]
        by_sum[s + 1] += moved if s < last - 1 else []
        if s + 3 in ahead:
            ahead[s + 3] = up([gate(x, pieces[1:2]) for x in ahead[s + 3]])
            by_diag[s + 1] += ahead[s + 3][1:]
        if s < turns and s % 2:
            flat, mark = flat_rest(lower_rest, flat, s, turns, block, [mine])
            by_lower[s + 1].append(mark)
        if s == last:
            buffer, new = write(0, steps, form, meta, ready, buffer, [mine])
            turned.append(new)
            by_lower[s + 1].append(new)
    known.append(place(form, meta, pieces, by_lower[steps]))
    whole = joined([last])
    got = up([whole] * py)
    direct = across(got[0])
    early = rest_product(0, form, meta, turned, flat, (), [whole])
    got = onward(got, direct, [early[0], *moved])
    buffer, *early = late_step(last - 1, form, meta, moved, flat, buffer, early)
    buffer, *late = late_step(last, form, meta, got, flat, buffer)
    total = rhs_rest.astype(F32) - early[0] - late[0]
    for c in range(1, n_cols):
        total = total - along_cols(early[c], c).astype(F32) - along_cols(late[c], c).astype(F32)
    return buffer, total.astype(BF16)


def per_device(lower_pivot, lower_rest, diag_inverse, rhs_pivot, rhs_rest):
    form = form_of(lower_pivot, rhs_pivot)
    fits = form.eqs % 128 == 0 and form.width % form.eqs == 0 and form.sides % 128 == 0
    fits = fits and (form.width // form.depth) % 16 == 0 and lower_rest.shape[0] % 128 == 0
    if fits:
        return kernel_path(form, lower_pivot, lower_rest, diag_inverse, rhs_pivot, rhs_rest)
    return plain_path(lower_pivot, lower_rest, diag_inverse, rhs_pivot, rhs_rest)


def solution(mesh):
    placed = (
        P(None, "rows", None, "cols"),
        P("rows", None, "cols"),
        P(None, "cols", "rows"),
        P(None, "rows", "cols"),
        P("cols", "rows"),
    )
    return jax.shard_map(
        per_device,
        mesh=mesh,
        in_specs=placed,
        out_specs=(P(None, "cols", None), P("cols", "rows")),
        check_vma=False,
    )
```

```python
import dataclasses
import functools
import math

import jax
import jax.numpy as jnp
from jax import lax
from jax.sharding import PartitionSpec as P
from jax.experimental import pallas as pl
from jax.experimental.pallas import tpu as pltpu

F32 = jnp.float32
BF16 = jnp.bfloat16


def split_of(count):
    best = 1
    for d in range(1, count + 1):
        if count % d == 0 and d * d <= count:
            best = d
    return best


def nt_dot(a, b):
    return lax.dot_general(a, b, (((1,), (1,)), ((), ())), preferred_element_type=F32)


def cut(n_rows, share):
    plane = split_of(n_rows)
    power = plane & (plane - 1) == 0
    code = [g ^ (g >> 1) if power else g for g in range(plane)]
    return plane, n_rows // plane, share // plane, code


def places(plane, code):
    row = lax.axis_index("rows")
    spot = row % plane
    g = sum(jnp.where(spot == code[i], i, 0) for i in range(plane))
    return g, row // plane, lax.axis_index("cols")


def movers(plane, depth, code, n_cols):
    def along_plane(x, k):
        pairs = [(b * plane + code[i], b * plane + code[(i + k) % plane]) for b in range(depth) for i in range(plane)]
        return lax.ppermute(x, "rows", pairs)

    def along_depth(x, k):
        pairs = [(b * plane + i, ((b + k) % depth) * plane + i) for b in range(depth) for i in range(plane)]
        return lax.ppermute(x, "rows", pairs)

    def along_cols(x, k):
        return lax.ppermute(x, "cols", [(i, (i + k) % n_cols) for i in range(n_cols)])

    return along_plane, along_depth, along_cols


def plain_path(lower_pivot, lower_rest, diag_inverse, rhs_pivot, rhs_rest):
    steps = lower_pivot.shape[0]
    eqs = lower_pivot.shape[1]
    share = lower_pivot.shape[3]
    sides = rhs_pivot.shape[2]
    rest = lower_rest.shape[0]
    n_rows = lax.axis_size("rows")
    n_cols = lax.axis_size("cols")
    plane, depth, width, code = cut(n_rows, share)
    g, z, core = places(plane, code)
    part = sides // depth
    along_plane, along_depth, along_cols = movers(plane, depth, code, n_cols)

    def gather(move, count, x, axis):
        return jnp.concatenate([x] + [move(x, k) for k in range(1, count)], axis=axis)

    def my_diag(s):
        block = diag_inverse[s].reshape(plane, width, eqs)
        parts = [lax.dynamic_index_in_dim(block, (g + k) % plane, 0, False) for k in range(plane)]
        held = jnp.concatenate([parts[0]] + [along_plane(parts[k], k) for k in range(1, plane)], axis=1)
        return gather(along_cols, n_cols, held, 0)

    def my_lower(s):
        parts = [
            lax.dynamic_slice_in_dim(lower_pivot[s, :, :s, :], ((g + k) % plane) * width, width, 2)
            for k in range(plane)
        ]
        held = jnp.concatenate([parts[0]] + [along_plane(parts[k], k) for k in range(1, plane)], axis=0)
        return gather(along_cols, n_cols, held, 2)

    def rolled(x, shift, axis):
        return jnp.roll(x, shift, axis)

    rhs_t = jnp.swapaxes(rhs_pivot, 1, 2)
    blocks = rhs_t.reshape(steps, depth, part, eqs)[:, ::-1]
    blocks = rolled(blocks, z + 1, 1).reshape(steps, sides, eqs)

    solved = []
    totals = jnp.zeros((sides, rest), F32)
    outs = []
    for s in range(steps):
        diag = my_diag(s)
        if s == 0:
            own = blocks[0]
        else:
            lower = my_lower(s)
            partial = jnp.zeros((sides, plane * eqs), F32)
            for t in range(s):
                partial = partial + nt_dot(solved[t], lower[:, t, :])
            total = blocks[s].astype(F32) - partial[:, :eqs]
            sent = partial.astype(BF16)
            for k in range(1, plane):
                total = total - along_plane(sent[:, k * eqs : (k + 1) * eqs], -k).astype(F32)
            own = total.astype(BF16)
        residual = gather(along_plane, plane, own, 1)
        product = nt_dot(residual, diag)
        sent = product.astype(BF16)
        total = product[:part]
        for k in range(1, depth):
            total = total + along_depth(sent[k * part : (k + 1) * part], -k).astype(F32)
        mine = total.astype(BF16)
        here = gather(along_depth, depth, mine, 0)
        solved.append(here)
        pieces = [here] + [along_plane(here, k) for k in range(1, plane)]
        pieces = [pieces[(-k) % plane] for k in range(plane)]
        full = jnp.stack([p.reshape(depth, part, n_cols, width) for p in pieces], axis=3)
        full = full[jnp.array([(-k) % depth for k in range(depth)])]
        full = rolled(full, z, 0)
        full = rolled(full, g, 3).reshape(sides, n_cols, share)
        rest_parts = [lower_rest[:, s, :]] + [along_cols(lower_rest[:, s, :], k) for k in range(1, n_cols)]
        for k in range(n_cols):
            totals = totals + nt_dot(full[:, k, :], rest_parts[k])
        theirs = [full[:, 0]] + [along_cols(full[:, k], -k) for k in range(1, n_cols)]
        theirs = rolled(jnp.stack(theirs, 0), core, 0).reshape(n_cols * sides, share)
        outs.append(theirs.T)
    remainder = (rhs_rest.astype(F32) - totals).astype(BF16)
    return jnp.stack(outs), remainder


VMEM_LIMIT = 40 * 1024 * 1024
WEIGHT = 8
SMALL = pl.BlockSpec(memory_space=pltpu.SMEM)
WHOLE = pl.BlockSpec(memory_space=pltpu.VMEM)


def call(body, outs, ins, specs, flops=0, scratch=(), after=(), weight=1, **more):
    size = sum(math.prod(x.shape) * x.dtype.itemsize for x in [*ins, *outs])
    first, last = len(ins), len(ins) + len(after)

    def run(*refs):
        body(*refs[:first], *refs[last:])

    return pl.pallas_call(
        run,
        out_shape=tuple(outs),
        in_specs=list(specs) + [pl.BlockSpec(memory_space=pl.ANY)] * len(after),
        scratch_shapes=list(scratch),
        compiler_params=pltpu.CompilerParams(vmem_limit_bytes=VMEM_LIMIT),
        cost_estimate=pl.CostEstimate(flops=flops, bytes_accessed=size * weight, transcendentals=0),
        **more,
    )(*ins, *after)


def shaped(dims, kind):
    return jax.ShapeDtypeStruct(dims, kind)


def put_diag(form, meta, dy, block, out):
    at = lax.rem(meta[0] + dy, form.py) * form.width
    for h in range(form.width // form.eqs):
        lanes = slice(h * form.eqs, (h + 1) * form.eqs)
        out[:, lanes] = block[pl.ds(pl.multiple_of(at + h * form.eqs, form.eqs), form.eqs), :]


def start_body(form, meta, diag, rhs, *refs):
    py, px, width, sides = form.py, form.px, form.width, form.sides
    own, outs, far = refs[-1], refs[:py], refs[py:-1]

    def part(s, dx):
        return rhs[s, :, pl.ds(pl.multiple_of(lax.rem(meta[1] + dx, px) * sides, sides), sides)]

    for dy in range(py):
        put_diag(form, meta, dy, diag.at[0], outs[dy])
        outs[dy][:, width:] = rhs[0]
    for dx in range(1, px):
        out = far[dx - 1]
        put_diag(form, meta, 0, diag.at[0], out)
        out[:, width : width + px * sides] = rhs[0]
        for s in range(1, rhs.shape[0]):
            out[:, width + (px + s - 1) * sides : width + (px + s) * sides] = part(s, dx)
    for s in range(rhs.shape[0]):
        own[s] = part(s, 0)


def start(form, meta, diag_inverse, rhs_pivot):
    width, eqs, sides, share = form.width, form.eqs, form.sides, form.py * form.width
    steps = rhs_pivot.shape[0]
    dims = [(eqs, width + form.px * sides)] * form.py
    dims += [(eqs, width + (form.px + steps - 1) * sides)] * (form.px - 1) + [(steps, eqs, sides)]
    outs = call(
        functools.partial(start_body, form),
        [shaped(d, BF16) for d in dims],
        [meta, diag_inverse, rhs_pivot],
        [
            SMALL,
            pl.BlockSpec((1, share, eqs), lambda i: (0, 0, 0)),
            pl.BlockSpec(rhs_pivot.shape, lambda i: (0, 0, 0)),
        ],
        weight=WEIGHT,
        grid=(1,),
        out_specs=tuple(pl.BlockSpec(d, lambda i, n=len(d): (0,) * n) for d in dims),
    )
    return outs[: form.py], outs[form.py : -1], outs[-1]


def slots(s):
    return [t for t in range(s) if s < 3 or t > 0], [0] if s > 2 else []


def slot_of(s, t):
    later, ahead = slots(s)
    return 1 + (later + ahead).index(t)


def prep_body(ss, form, meta, diag, lower, *refs):
    py, width = form.py, form.width
    refs, flat = list(refs[:-1]), refs[-1]
    for i, s in enumerate(ss):
        flat[...] = jnp.swapaxes(lower[i], 0, 1)
        later, ahead = slots(s)
        outs = [refs.pop(0) for _ in range(py)]
        early = [refs.pop(0) for _ in range(py)] if ahead else []
        for dy in range(py):
            put_diag(form, meta, dy, diag.at[i], outs[dy])
            at = pl.ds(pl.multiple_of(lax.rem(meta[0] + dy, py) * width, width), width)
            for j, t in enumerate(later):
                outs[dy][:, (1 + j) * width : (2 + j) * width] = flat[t, :, at]
            for j, t in enumerate(ahead):
                early[dy][:, j * width : (j + 1) * width] = flat[t, :, at]


def prep(ss, form, meta, diag_inverse, lower_pivot, after=()):
    width, eqs, share = form.width, form.eqs, form.py * form.width
    steps, count = lower_pivot.shape[0], len(ss)
    dims = []
    for s in ss:
        later, ahead = slots(s)
        dims += [(eqs, (1 + len(later)) * width)] * form.py + [(eqs, len(ahead) * width)] * (form.py if ahead else 0)
    outs = call(
        functools.partial(prep_body, ss, form),
        [shaped(d, BF16) for d in dims],
        [meta, diag_inverse, lower_pivot],
        [
            SMALL,
            pl.BlockSpec((pl.Element(count), pl.Element(share), pl.Element(eqs)), lambda i: (ss[0], 0, 0)),
            pl.BlockSpec(
                (pl.Element(count), pl.Element(eqs), pl.Element(steps), pl.Element(share)), lambda i: (ss[0], 0, 0, 0)
            ),
        ],
        scratch=[pltpu.VMEM((steps, eqs, share), BF16)],
        after=after,
        weight=WEIGHT,
        grid=(1,),
        out_specs=tuple(pl.BlockSpec(d, lambda i: (0, 0)) for d in dims),
    )
    packed, ahead, outs = {}, {}, list(outs)
    for s in ss:
        packed[s] = [outs.pop(0) for _ in range(form.py)]
        if slots(s)[1]:
            ahead[s] = [outs.pop(0) for _ in range(form.py)]
    return packed, ahead


def pack_body(count, first, *refs):
    refs = list(refs)
    for k, part in enumerate(take(refs, count)):
        refs[-1][k, :, :first] = part[...]
    for k in range(len(refs) - 1):
        refs[-1][k, :, first:] = refs[k][...]


def pack(parts, after=(), beside=()):
    count = sum(1 if x.ndim == 2 else x.shape[0] for x in parts)
    rows, first = parts[0].shape[-2:]
    lanes = first + (beside[0].shape[-1] if beside else 0)
    ins = [*parts, *beside]
    return call(
        functools.partial(pack_body, count, first),
        [shaped((count, rows, lanes), BF16)],
        ins,
        [WHOLE] * len(ins),
        after=after,
        weight=WEIGHT,
    )[0]


def take(refs, count):
    got = []
    while len(got) < count:
        ref = refs.pop(0)
        got += [ref] if len(ref.shape) == 2 else [ref.at[k] for k in range(ref.shape[0])]
    return got


def diag_body(form, terms, meta, *refs):
    chips, n_cols, depth, eqs, width, sides = form.chips, form.n_cols, form.depth, form.eqs, form.width, form.sides
    refs = list(refs)
    held = take(refs, n_cols * chips)
    sums = [refs.pop(0) for _ in range(terms)]
    outs, product = refs[:-1], refs[-1]
    sub = width // depth
    if terms:
        total = sums[0][...]
        for x in sums[1:]:
            total = total + x[...].astype(F32)
        residual = (-total).astype(BF16)
    else:
        right = pl.ds(pl.multiple_of(width + meta[1] * sides, sides), sides)
        residual = jnp.concatenate([held[k][:, right] for k in range(chips)], axis=0)
    for c in range(n_cols):
        rows = [
            jnp.concatenate([held[c * chips + k][:, h * eqs : (h + 1) * eqs] for k in range(chips)], axis=1)
            for h in range(width // eqs)
        ]
        product[c] = jnp.dot(jnp.concatenate(rows, axis=0), residual, preferred_element_type=F32)
    for k in range(depth):
        at = pl.multiple_of(lax.rem(meta[2] + depth - k, depth) * sub, sub)
        for c in range(n_cols):
            outs[k][c * sub : (c + 1) * sub] = product[c, pl.ds(at, sub)].astype(outs[k].dtype)


def diag_product(form, meta, held, sums, after=()):
    width, eqs, sides, depth, n_cols, chips = form.width, form.eqs, form.sides, form.depth, form.n_cols, form.chips
    dims = (n_cols * (width // depth), sides)
    return call(
        functools.partial(diag_body, form, len(sums)),
        [shaped(dims, F32)] + [shaped(dims, BF16)] * (depth - 1),
        [meta, *held, *sums],
        [SMALL] + [WHOLE] * (len(held) + len(sums)),
        flops=2 * n_cols * width * chips * eqs * sides,
        scratch=[pltpu.VMEM((n_cols, width, sides), F32)],
        after=after,
    )


def put_pieces(form, meta, pieces, outs):
    depth, sub = form.depth, form.width // form.depth
    for k in range(depth):
        at = pl.multiple_of(lax.rem(meta[2] + depth - k, depth) * sub, sub)
        for c in range(form.n_cols):
            outs[c][pl.ds(at, sub)] = pieces[k][c * sub : (c + 1) * sub]


def lower_body(s, form, meta, *refs):
    chips, n_cols, eqs = form.chips, form.n_cols, form.eqs
    refs = list(refs)
    held = take(refs, n_cols * chips)
    width = form.width
    known = [[refs.pop(0) for _ in range(n_cols)] for _ in range(s - 1)]
    pieces = [refs.pop(0) for _ in range(form.depth)]
    own = refs.pop(0)
    far = [refs.pop(0) for _ in range(form.px - 1)]
    outs, newest = refs[: form.py], refs[form.py :]
    put_pieces(form, meta, pieces, newest)
    total = None
    for t, blocks in enumerate(known + [newest]):
        for c in range(n_cols):
            lanes = slice(slot_of(s, t) * width, (slot_of(s, t) + 1) * width)
            rows = jnp.concatenate([held[c * chips + k][:, lanes] for k in range(chips)], axis=0)
            term = jnp.dot(rows, blocks[c][...], preferred_element_type=F32)
            total = term if total is None else total + term
    parts = [total[k * eqs : (k + 1) * eqs] for k in range(chips)]
    lane = width + (form.px + s - 1) * form.sides
    for k, (dy, dx) in enumerate(form.shifts):
        if dy == 0:
            right = far[dx - 1][:, lane : lane + form.sides] if dx else own[s]
            parts[k] = parts[k] - right.astype(F32)
    for e in range(form.py):
        for k, (dy, dx) in enumerate(form.shifts):
            mine = form.shifts.index(((dy - e) % form.py, dx))
            outs[e][k * eqs : (k + 1) * eqs] = parts[mine].astype(outs[e].dtype)


def lower_product(s, form, meta, held, known, pieces, own, far, after=()):
    rows, sides = form.chips * form.eqs, form.sides
    flat = [x for blocks in known for x in blocks]
    ins = [meta, *held, *flat, *pieces, own, *far]
    return call(
        functools.partial(lower_body, s, form),
        [shaped((rows, sides), F32)]
        + [shaped((rows, sides), BF16)] * (form.py - 1)
        + [shaped((form.width, sides), BF16)] * form.n_cols,
        ins,
        [SMALL] + [WHOLE] * (len(ins) - 1),
        flops=2 * s * form.n_cols * form.width * rows * sides,
        after=after,
    )


def place_body(form, meta, *refs):
    put_pieces(form, meta, refs[: form.depth], refs[form.depth :])


def place(form, meta, pieces, after=()):
    return call(
        functools.partial(place_body, form),
        [shaped((form.width, form.sides), BF16)] * form.n_cols,
        [meta, *pieces],
        [SMALL] + [WHOLE] * form.depth,
        after=after,
    )


def gate_body(*refs):
    pass


def gate(x, after):
    return call(
        gate_body,
        [shaped(x.shape, x.dtype)],
        [x],
        [pl.BlockSpec(memory_space=pl.ANY)],
        after=after,
        out_specs=(pl.BlockSpec(memory_space=pl.ANY),),
        input_output_aliases={0: 0},
    )[0]


def join_body(form, count, meta, *refs):
    width, sides = form.width, form.sides
    for i in range(count):
        for k in range(form.n_cols):
            at = pl.multiple_of(lax.rem(meta[3] + k, form.n_cols) * sides, sides)
            refs[-1][i * width : (i + 1) * width, pl.ds(at, sides)] = refs[i * form.n_cols + k][...]


def join(form, meta, parts, after=()):
    count = len(parts) // form.n_cols
    return call(
        functools.partial(join_body, form, count),
        [shaped((count * form.width, form.n_cols * form.sides), BF16)],
        [meta, *parts],
        [SMALL] + [WHOLE] * len(parts),
        after=after,
    )[0]


def flat_body(x, *refs):
    refs[-2][...] = jnp.swapaxes(x[...], 0, 1)
    refs[-1][...] = jnp.zeros_like(refs[-1])


def flat_rest(lower_rest, buffer, turn, turns, block, after=()):
    rest, steps, share = lower_rest.shape
    first = turn * (rest // turns // block)
    ins, alias = [lower_rest], {}
    specs = [pl.BlockSpec((block, steps, share), lambda i: (first + i, 0, 0))]
    if buffer is not None:
        alias = {1: 0}
        ins.append(buffer)
        specs.append(pl.BlockSpec(memory_space=pltpu.HBM))
    return call(
        flat_body,
        [pltpu.HBM((steps, rest, share), BF16), shaped((8, 128), F32)],
        ins,
        specs,
        after=after,
        grid=(rest // turns // block,),
        out_specs=(
            pl.BlockSpec((steps, block, share), lambda i: (0, first + i, 0)),
            pl.BlockSpec((8, 128), lambda i: (0, 0)),
        ),
        input_output_aliases=alias,
    )


def write_body(form, count, meta, *refs):
    parts = take(list(refs), form.chips)
    put_solved(form, count, meta, parts, *refs[-2:])


def put_solved(form, count, meta, parts, out, turned):
    width, sides = form.width, form.sides
    for i in range(count):
        for k, (dy, dx) in enumerate(form.shifts):
            y, x = lax.rem(meta[0] + form.py - dy, form.py), lax.rem(meta[1] + form.px - dx, form.px)
            block = parts[k][i * width : (i + 1) * width]
            row = pl.ds(pl.multiple_of(y * width, width), width)
            for c in range(form.n_cols):
                lane = pl.ds(pl.multiple_of((c * form.px + x) * sides, sides), sides)
                piece = block[:, c * sides : (c + 1) * sides]
                out[i, row, lane] = piece
                turned[i, lane, row] = piece.T


def write(s, steps, form, meta, parts, buffer, after=()):
    share, total = form.py * form.width, form.px * form.n_cols * form.sides
    count = parts[0].shape[-2] // form.width
    ins = [meta, *parts]
    specs = [SMALL] + [pl.BlockSpec(x.shape, lambda i, n=x.ndim: (0,) * n) for x in parts]
    alias = {}
    if buffer is not None:
        alias = {len(ins): 0}
        ins.append(buffer)
        specs.append(pl.BlockSpec(memory_space=pltpu.HBM))
    return call(
        functools.partial(write_body, form, count),
        [pltpu.HBM((steps, share, total), BF16), shaped((count, total, share), BF16)],
        ins,
        specs,
        after=after,
        grid=(1,),
        out_specs=(
            pl.BlockSpec((count, share, total), lambda i: (s // count, 0, 0)),
            pl.BlockSpec((count, total, share), lambda i: (0, 0, 0)),
        ),
        input_output_aliases=alias,
    )


def rest_body(form, counts, running, meta, *refs):
    turned, lower, refs = refs[: len(counts)], refs[len(counts)], refs[len(counts) + 1 :]
    before, outs = refs[:running], refs[running:]
    sides = form.px * form.sides
    for order, out in enumerate(outs):
        at = pl.multiple_of(lax.rem(meta[3] + order, form.n_cols) * sides, sides)
        total, t = None, 0
        for x, count in zip(turned, counts):
            for i in range(count):
                term = nt_dot(x[i, pl.ds(at, sides), :], lower[t])
                total = term if total is None else total + term
                t += 1
        if running:
            total = total + before[order][...].astype(F32)
        out[...] = total.astype(out.dtype)


def rest_product(first, form, meta, turned, lower, before=(), after=()):
    orders = range(form.n_cols)
    _, rest, share = lower.shape
    counts = [x.shape[0] for x in turned]
    count = sum(counts)
    sides = form.px * form.sides
    block = max(n for n in (768, 512, 384, 256, 128) if rest % n == 0)
    side_block = pl.BlockSpec((sides, block), lambda i: (0, i))
    return call(
        functools.partial(rest_body, form, counts, len(before)),
        [shaped((sides, rest), F32 if order == 0 else BF16) for order in orders],
        [meta, *turned, pltpu.with_memory_space_constraint(lower, pltpu.HBM), *before],
        [SMALL]
        + [pl.BlockSpec(x.shape, lambda i: (0, 0, 0)) for x in turned]
        + [pl.BlockSpec((count, block, share), lambda i: (first // count, i, 0))]
        + [side_block] * len(before),
        flops=2 * count * share * sides * rest * len(orders),
        after=after,
        grid=(rest // block,),
        out_specs=(side_block,) * len(orders),
    )


def last_body(form, running, meta, *refs):
    refs = list(refs)
    parts = take(refs, form.chips)
    lower, before, (out, *sums, turned) = refs[0], refs[1 : 1 + running], refs[2 + running :]

    @pl.when(pl.program_id(0) == 0)
    def _():
        put_solved(form, 1, meta, parts, out, turned)

    sides = form.px * form.sides
    for order, to in enumerate(sums):
        at = pl.multiple_of(lax.rem(meta[3] + order, form.n_cols) * sides, sides)
        total = nt_dot(turned[0, pl.ds(at, sides), :], lower[0])
        if running:
            total = total + before[order][...].astype(F32)
        to[...] = total.astype(to.dtype)


def late_step(s, form, meta, parts, lower, buffer, before=(), after=()):
    steps, rest, share = lower.shape
    total, sides = form.px * form.n_cols * form.sides, form.px * form.sides
    block = max(n for n in (768, 512, 384, 256, 128) if rest % n == 0)
    lower = pltpu.with_memory_space_constraint(lower, pltpu.HBM)
    side_block = pl.BlockSpec((sides, block), lambda i: (0, i))
    return call(
        functools.partial(last_body, form, len(before)),
        [pltpu.HBM((steps, share, total), BF16)]
        + [shaped((sides, rest), F32 if order == 0 else BF16) for order in range(form.n_cols)],
        [meta, *parts, lower, *before, buffer],
        [SMALL]
        + [pl.BlockSpec(x.shape, lambda i, n=x.ndim: (0,) * n) for x in parts]
        + [pl.BlockSpec((1, block, share), lambda i: (s, i, 0))]
        + [side_block] * len(before)
        + [pl.BlockSpec(memory_space=pltpu.HBM)],
        flops=2 * share * total * rest,
        scratch=[pltpu.VMEM((1, total, share), BF16)],
        after=after,
        grid=(rest // block,),
        out_specs=(pl.BlockSpec((1, share, total), lambda i: (s, 0, 0)), *[side_block] * form.n_cols),
        input_output_aliases={len(parts) + 2 + len(before): 0},
    )


@dataclasses.dataclass
class Form:
    py: int
    px: int
    depth: int
    n_cols: int
    eqs: int
    width: int
    sides: int

    def __post_init__(self):
        self.shifts = [(dy, dx) for dx in range(self.px) for dy in range(self.py)]
        self.chips = len(self.shifts)


def form_of(lower_pivot, rhs_pivot):
    n_rows = lax.axis_size("rows")
    plane = split_of(n_rows)
    px = split_of(plane)
    py = plane // px
    return Form(
        py, px, n_rows // plane, lax.axis_size("cols"), lower_pivot.shape[1], lower_pivot.shape[3] // py,
        rhs_pivot.shape[2] // px,
    )


def kernel_path(form, lower_pivot, lower_rest, diag_inverse, rhs_pivot, rhs_rest):
    lower_pivot, lower_rest, diag_inverse, rhs_pivot = (
        pltpu.with_memory_space_constraint(x, pltpu.HBM) for x in (lower_pivot, lower_rest, diag_inverse, rhs_pivot)
    )
    steps = lower_pivot.shape[0]
    rest = lower_rest.shape[0]
    py, px, depth, n_cols, chips = form.py, form.px, form.depth, form.n_cols, form.chips
    row = lax.axis_index("rows")
    meta = jnp.stack([row // px % py, row % px, row // chips, lax.axis_index("cols")]).astype(jnp.int32)

    def along_plane(x, dy, dx):
        pairs = [
            ((b * py + y) * px + i, (b * py + (y + dy) % py) * px + (i + dx) % px)
            for b in range(depth)
            for y in range(py)
            for i in range(px)
        ]
        return lax.ppermute(x, "rows", pairs)

    def along_depth(x, k):
        pairs = [(b * chips + i, (b + k) % depth * chips + i) for b in range(depth) for i in range(chips)]
        return lax.ppermute(x, "rows", pairs)

    def along_cols(x, k):
        return lax.ppermute(x, "cols", [(i, (i + k) % n_cols) for i in range(n_cols)])

    def up(blocks):
        return [blocks[0]] + [along_plane(blocks[dy], dy, 0) for dy in range(1, py)]

    def across(x):
        return [along_plane(x, 0, dx) for dx in range(1, px)]

    def onward(first, direct, after=()):
        rest = [gate(x, after) if after else x for x in first[1:]]
        far = [across(x) for x in rest]
        got = [first[0], *rest]
        for dx in range(px - 1):
            got += [direct[dx]] + [x[dx] for x in far]
        return got

    def held_of(parts, after):
        mine = [pack(parts, after)] if after else parts
        return mine + [along_cols(x, c) for c in range(1, n_cols) for x in mine]

    def joined(ts, after=()):
        parts = []
        for t in ts:
            parts += [known[t][0]] + [along_cols(known[t][k], -k) for k in range(1, n_cols)]
        return join(form, meta, parts, after)

    turns = 3
    block = 128
    while rest % (turns * block):
        turns -= 1
    last = steps - 1
    near, far, own = start(form, meta, diag_inverse, rhs_pivot)
    got = up(near)
    here = [along_plane(x, 0, dx + 1) for dx, x in enumerate(far)]
    packed, ahead = prep(tuple(range(1, steps)), form, meta, diag_inverse, lower_pivot)
    first = up([gate(x, got[1:]) for x in packed[1]])
    got = onward(got, here, [packed[1][0]])
    later = [gate(x, [*got[py + 1 :], *first[1:]]) for x in got[py :: py]]
    held = held_of([later[k // py - 1] if k >= py and k % py == 0 else x for k, x in enumerate(got)], ())
    moved = pack(first)
    moved = [moved, *across(moved)]
    known, sums, turned, flat, buffer = [], [], [], None, None
    by_lower, by_diag, by_sum = ({s: [] for s in range(steps + 1)} for _ in range(3))
    by_diag[0] += [packed[last][0], *first[1:]]
    by_sum[0] += moved
    for s in range(steps):
        if s > 0:
            outs = lower_product(s, form, meta, held, known, pieces, own, here, by_lower[s])
            known.append(outs[py:])
            sums = [outs[0]] + [along_plane(outs[e], e, 0) for e in range(1, py)]
            if s >= last - 1:
                whole = joined(range(s) if s < last else [s - 1], [outs[0]])
                by_diag[s].append(whole)
        products = diag_product(form, meta, held, sums, by_diag[s])
        if s < last - 1:
            first = up([gate(x, [products[0]]) for x in packed[s + 2]])
        else:
            first = up([gate(whole, [products[0]])] * py)
        by_sum[s] += first[1:]
        if s < turns and s % 2 == 0:
            flat, mark = flat_rest(lower_rest, flat, s, turns, block, [products[0]])
            by_sum[s].append(mark)
        arrivals = [along_depth(products[k], -k) for k in range(1, depth)]
        arrivals[-1] = gate(arrivals[-1], by_sum[s])
        total = products[0]
        for x in arrivals:
            total = total + x.astype(F32)
        mine = total.astype(BF16)
        if s < last:
            held = held_of(moved, [mine])
        pieces = [mine] + [along_depth(mine, k) for k in range(1, depth)]
        soon = pieces[1:2] if s == last - 1 else [mine]
        ready, moved = moved, pack(first, soon, ahead.get(s + 2, ()))
        moved = [moved, *across(moved)]
        by_sum[s + 1] += moved if s < last - 1 else []
        if s + 3 in ahead:
            ahead[s + 3] = up([gate(x, pieces[1:2]) for x in ahead[s + 3]])
            by_diag[s + 1] += ahead[s + 3][1:]
        if s < turns and s % 2:
            flat, mark = flat_rest(lower_rest, flat, s, turns, block, [mine])
            by_lower[s + 1].append(mark)
        if s == last:
            buffer, new = write(0, steps, form, meta, ready, buffer, [mine])
            turned.append(new)
            by_lower[s + 1].append(new)
    known.append(place(form, meta, pieces, by_lower[steps]))
    whole = joined([last])
    got = up([whole] * py)
    direct = across(got[0])
    early = rest_product(0, form, meta, turned, flat, (), [whole, *moved])
    got = onward(got, direct, [early[0], *moved])
    buffer, *early = late_step(last - 1, form, meta, moved, flat, buffer, early)
    buffer, *late = late_step(last, form, meta, got, flat, buffer, early)
    total = rhs_rest.astype(F32) - late[0]
    for c in range(1, n_cols):
        total = total - along_cols(late[c], c).astype(F32)
    return buffer, total.astype(BF16)


def per_device(lower_pivot, lower_rest, diag_inverse, rhs_pivot, rhs_rest):
    form = form_of(lower_pivot, rhs_pivot)
    fits = form.eqs % 128 == 0 and form.width % form.eqs == 0 and form.sides % 128 == 0
    fits = fits and (form.width // form.depth) % 16 == 0 and lower_rest.shape[0] % 128 == 0
    if fits:
        return kernel_path(form, lower_pivot, lower_rest, diag_inverse, rhs_pivot, rhs_rest)
    return plain_path(lower_pivot, lower_rest, diag_inverse, rhs_pivot, rhs_rest)


def solution(mesh):
    placed = (
        P(None, "rows", None, "cols"),
        P("rows", None, "cols"),
        P(None, "cols", "rows"),
        P(None, "rows", "cols"),
        P("cols", "rows"),
    )
    return jax.shard_map(
        per_device,
        mesh=mesh,
        in_specs=placed,
        out_specs=(P(None, "cols", None), P("cols", "rows")),
        check_vma=False,
    )
```

```python
import dataclasses
import functools
import math

import jax
import jax.numpy as jnp
from jax import lax
from jax.sharding import PartitionSpec as P
from jax.experimental import pallas as pl
from jax.experimental.pallas import tpu as pltpu

F32 = jnp.float32
BF16 = jnp.bfloat16


def split_of(count):
    best = 1
    for d in range(1, count + 1):
        if count % d == 0 and d * d <= count:
            best = d
    return best


def nt_dot(a, b):
    return lax.dot_general(a, b, (((1,), (1,)), ((), ())), preferred_element_type=F32)


def cut(n_rows, share):
    plane = split_of(n_rows)
    power = plane & (plane - 1) == 0
    code = [g ^ (g >> 1) if power else g for g in range(plane)]
    return plane, n_rows // plane, share // plane, code


def places(plane, code):
    row = lax.axis_index("rows")
    spot = row % plane
    g = sum(jnp.where(spot == code[i], i, 0) for i in range(plane))
    return g, row // plane, lax.axis_index("cols")


def movers(plane, depth, code, n_cols):
    def along_plane(x, k):
        pairs = [(b * plane + code[i], b * plane + code[(i + k) % plane]) for b in range(depth) for i in range(plane)]
        return lax.ppermute(x, "rows", pairs)

    def along_depth(x, k):
        pairs = [(b * plane + i, ((b + k) % depth) * plane + i) for b in range(depth) for i in range(plane)]
        return lax.ppermute(x, "rows", pairs)

    def along_cols(x, k):
        return lax.ppermute(x, "cols", [(i, (i + k) % n_cols) for i in range(n_cols)])

    return along_plane, along_depth, along_cols


def plain_path(lower_pivot, lower_rest, diag_inverse, rhs_pivot, rhs_rest):
    steps = lower_pivot.shape[0]
    eqs = lower_pivot.shape[1]
    share = lower_pivot.shape[3]
    sides = rhs_pivot.shape[2]
    rest = lower_rest.shape[0]
    n_rows = lax.axis_size("rows")
    n_cols = lax.axis_size("cols")
    plane, depth, width, code = cut(n_rows, share)
    g, z, core = places(plane, code)
    part = sides // depth
    along_plane, along_depth, along_cols = movers(plane, depth, code, n_cols)

    def gather(move, count, x, axis):
        return jnp.concatenate([x] + [move(x, k) for k in range(1, count)], axis=axis)

    def my_diag(s):
        block = diag_inverse[s].reshape(plane, width, eqs)
        parts = [lax.dynamic_index_in_dim(block, (g + k) % plane, 0, False) for k in range(plane)]
        held = jnp.concatenate([parts[0]] + [along_plane(parts[k], k) for k in range(1, plane)], axis=1)
        return gather(along_cols, n_cols, held, 0)

    def my_lower(s):
        parts = [
            lax.dynamic_slice_in_dim(lower_pivot[s, :, :s, :], ((g + k) % plane) * width, width, 2)
            for k in range(plane)
        ]
        held = jnp.concatenate([parts[0]] + [along_plane(parts[k], k) for k in range(1, plane)], axis=0)
        return gather(along_cols, n_cols, held, 2)

    def rolled(x, shift, axis):
        return jnp.roll(x, shift, axis)

    rhs_t = jnp.swapaxes(rhs_pivot, 1, 2)
    blocks = rhs_t.reshape(steps, depth, part, eqs)[:, ::-1]
    blocks = rolled(blocks, z + 1, 1).reshape(steps, sides, eqs)

    solved = []
    totals = jnp.zeros((sides, rest), F32)
    outs = []
    for s in range(steps):
        diag = my_diag(s)
        if s == 0:
            own = blocks[0]
        else:
            lower = my_lower(s)
            partial = jnp.zeros((sides, plane * eqs), F32)
            for t in range(s):
                partial = partial + nt_dot(solved[t], lower[:, t, :])
            total = blocks[s].astype(F32) - partial[:, :eqs]
            sent = partial.astype(BF16)
            for k in range(1, plane):
                total = total - along_plane(sent[:, k * eqs : (k + 1) * eqs], -k).astype(F32)
            own = total.astype(BF16)
        residual = gather(along_plane, plane, own, 1)
        product = nt_dot(residual, diag)
        sent = product.astype(BF16)
        total = product[:part]
        for k in range(1, depth):
            total = total + along_depth(sent[k * part : (k + 1) * part], -k).astype(F32)
        mine = total.astype(BF16)
        here = gather(along_depth, depth, mine, 0)
        solved.append(here)
        pieces = [here] + [along_plane(here, k) for k in range(1, plane)]
        pieces = [pieces[(-k) % plane] for k in range(plane)]
        full = jnp.stack([p.reshape(depth, part, n_cols, width) for p in pieces], axis=3)
        full = full[jnp.array([(-k) % depth for k in range(depth)])]
        full = rolled(full, z, 0)
        full = rolled(full, g, 3).reshape(sides, n_cols, share)
        rest_parts = [lower_rest[:, s, :]] + [along_cols(lower_rest[:, s, :], k) for k in range(1, n_cols)]
        for k in range(n_cols):
            totals = totals + nt_dot(full[:, k, :], rest_parts[k])
        theirs = [full[:, 0]] + [along_cols(full[:, k], -k) for k in range(1, n_cols)]
        theirs = rolled(jnp.stack(theirs, 0), core, 0).reshape(n_cols * sides, share)
        outs.append(theirs.T)
    remainder = (rhs_rest.astype(F32) - totals).astype(BF16)
    return jnp.stack(outs), remainder


VMEM_LIMIT = 40 * 1024 * 1024
WEIGHT = 8
SMALL = pl.BlockSpec(memory_space=pltpu.SMEM)
WHOLE = pl.BlockSpec(memory_space=pltpu.VMEM)


def call(body, outs, ins, specs, flops=0, scratch=(), after=(), weight=1, **more):
    size = sum(math.prod(x.shape) * x.dtype.itemsize for x in [*ins, *outs])
    first, last = len(ins), len(ins) + len(after)

    def run(*refs):
        body(*refs[:first], *refs[last:])

    return pl.pallas_call(
        run,
        out_shape=tuple(outs),
        in_specs=list(specs) + [pl.BlockSpec(memory_space=pl.ANY)] * len(after),
        scratch_shapes=list(scratch),
        compiler_params=pltpu.CompilerParams(vmem_limit_bytes=VMEM_LIMIT),
        cost_estimate=pl.CostEstimate(flops=flops, bytes_accessed=size * weight, transcendentals=0),
        **more,
    )(*ins, *after)


def shaped(dims, kind):
    return jax.ShapeDtypeStruct(dims, kind)


def put_diag(form, meta, dy, block, out):
    at = lax.rem(meta[0] + dy, form.py) * form.width
    for h in range(form.width // form.eqs):
        lanes = slice(h * form.eqs, (h + 1) * form.eqs)
        out[:, lanes] = block[pl.ds(pl.multiple_of(at + h * form.eqs, form.eqs), form.eqs), :]


def start_body(form, meta, diag, rhs, *refs):
    py, px, width, sides = form.py, form.px, form.width, form.sides
    own, outs, far = refs[-1], refs[:py], refs[py:-1]

    def part(s, dx):
        return rhs[s, :, pl.ds(pl.multiple_of(lax.rem(meta[1] + dx, px) * sides, sides), sides)]

    for dy in range(py):
        put_diag(form, meta, dy, diag.at[0], outs[dy])
        outs[dy][:, width:] = rhs[0]
    for dx in range(1, px):
        out = far[dx - 1]
        put_diag(form, meta, 0, diag.at[0], out)
        out[:, width : width + px * sides] = rhs[0]
        for s in range(1, rhs.shape[0]):
            out[:, width + (px + s - 1) * sides : width + (px + s) * sides] = part(s, dx)
    for s in range(rhs.shape[0]):
        own[s] = part(s, 0)


def start(form, meta, diag_inverse, rhs_pivot):
    width, eqs, sides, share = form.width, form.eqs, form.sides, form.py * form.width
    steps = rhs_pivot.shape[0]
    dims = [(eqs, width + form.px * sides)] * form.py
    dims += [(eqs, width + (form.px + steps - 1) * sides)] * (form.px - 1) + [(steps, eqs, sides)]
    outs = call(
        functools.partial(start_body, form),
        [shaped(d, BF16) for d in dims],
        [meta, diag_inverse, rhs_pivot],
        [
            SMALL,
            pl.BlockSpec((1, share, eqs), lambda i: (0, 0, 0)),
            pl.BlockSpec(rhs_pivot.shape, lambda i: (0, 0, 0)),
        ],
        weight=WEIGHT,
        grid=(1,),
        out_specs=tuple(pl.BlockSpec(d, lambda i, n=len(d): (0,) * n) for d in dims),
    )
    return outs[: form.py], outs[form.py : -1], outs[-1]


def slots(s):
    return [t for t in range(s) if s < 3 or t > 0], [0] if s > 2 else []


def slot_of(s, t):
    later, ahead = slots(s)
    return 1 + (later + ahead).index(t)


def prep_body(ss, form, meta, diag, lower, *refs):
    py, width = form.py, form.width
    refs, flat = list(refs[:-1]), refs[-1]
    for i, s in enumerate(ss):
        flat[...] = jnp.swapaxes(lower[i], 0, 1)
        later, ahead = slots(s)
        outs = [refs.pop(0) for _ in range(py)]
        early = [refs.pop(0) for _ in range(py)] if ahead else []
        for dy in range(py):
            put_diag(form, meta, dy, diag.at[i], outs[dy])
            at = pl.ds(pl.multiple_of(lax.rem(meta[0] + dy, py) * width, width), width)
            for j, t in enumerate(later):
                outs[dy][:, (1 + j) * width : (2 + j) * width] = flat[t, :, at]
            for j, t in enumerate(ahead):
                early[dy][:, j * width : (j + 1) * width] = flat[t, :, at]


def prep(ss, form, meta, diag_inverse, lower_pivot, after=()):
    width, eqs, share = form.width, form.eqs, form.py * form.width
    steps, count = lower_pivot.shape[0], len(ss)
    dims = []
    for s in ss:
        later, ahead = slots(s)
        dims += [(eqs, (1 + len(later)) * width)] * form.py + [(eqs, len(ahead) * width)] * (form.py if ahead else 0)
    outs = call(
        functools.partial(prep_body, ss, form),
        [shaped(d, BF16) for d in dims],
        [meta, diag_inverse, lower_pivot],
        [
            SMALL,
            pl.BlockSpec((pl.Element(count), pl.Element(share), pl.Element(eqs)), lambda i: (ss[0], 0, 0)),
            pl.BlockSpec(
                (pl.Element(count), pl.Element(eqs), pl.Element(steps), pl.Element(share)), lambda i: (ss[0], 0, 0, 0)
            ),
        ],
        scratch=[pltpu.VMEM((steps, eqs, share), BF16)],
        after=after,
        weight=WEIGHT,
        grid=(1,),
        out_specs=tuple(pl.BlockSpec(d, lambda i: (0, 0)) for d in dims),
    )
    packed, ahead, outs = {}, {}, list(outs)
    for s in ss:
        packed[s] = [outs.pop(0) for _ in range(form.py)]
        if slots(s)[1]:
            ahead[s] = [outs.pop(0) for _ in range(form.py)]
    return packed, ahead


def pack_body(count, first, *refs):
    refs = list(refs)
    for k, part in enumerate(take(refs, count)):
        refs[-1][k, :, :first] = part[...]
    for k in range(len(refs) - 1):
        refs[-1][k, :, first:] = refs[k][...]


def pack(parts, after=(), beside=()):
    count = sum(1 if x.ndim == 2 else x.shape[0] for x in parts)
    rows, first = parts[0].shape[-2:]
    lanes = first + (beside[0].shape[-1] if beside else 0)
    ins = [*parts, *beside]
    return call(
        functools.partial(pack_body, count, first),
        [shaped((count, rows, lanes), BF16)],
        ins,
        [WHOLE] * len(ins),
        after=after,
        weight=WEIGHT,
    )[0]


def take(refs, count):
    got = []
    while len(got) < count:
        ref = refs.pop(0)
        got += [ref] if len(ref.shape) == 2 else [ref.at[k] for k in range(ref.shape[0])]
    return got


def diag_body(form, terms, meta, *refs):
    chips, n_cols, depth, eqs, width, sides = form.chips, form.n_cols, form.depth, form.eqs, form.width, form.sides
    refs = list(refs)
    held = take(refs, n_cols * chips)
    sums = [refs.pop(0) for _ in range(terms)]
    outs, product = refs[:-1], refs[-1]
    sub = width // depth
    if terms:
        total = sums[0][...]
        for x in sums[1:]:
            total = total + x[...].astype(F32)
        residual = (-total).astype(BF16)
    else:
        right = pl.ds(pl.multiple_of(width + meta[1] * sides, sides), sides)
        residual = jnp.concatenate([held[k][:, right] for k in range(chips)], axis=0)
    for c in range(n_cols):
        rows = [
            jnp.concatenate([held[c * chips + k][:, h * eqs : (h + 1) * eqs] for k in range(chips)], axis=1)
            for h in range(width // eqs)
        ]
        product[c] = jnp.dot(jnp.concatenate(rows, axis=0), residual, preferred_element_type=F32)
    for k in range(depth):
        at = pl.multiple_of(lax.rem(meta[2] + depth - k, depth) * sub, sub)
        for c in range(n_cols):
            outs[k][c * sub : (c + 1) * sub] = product[c, pl.ds(at, sub)].astype(outs[k].dtype)


def diag_product(form, meta, held, sums, after=()):
    width, eqs, sides, depth, n_cols, chips = form.width, form.eqs, form.sides, form.depth, form.n_cols, form.chips
    dims = (n_cols * (width // depth), sides)
    return call(
        functools.partial(diag_body, form, len(sums)),
        [shaped(dims, F32)] + [shaped(dims, BF16)] * (depth - 1),
        [meta, *held, *sums],
        [SMALL] + [WHOLE] * (len(held) + len(sums)),
        flops=2 * n_cols * width * chips * eqs * sides,
        scratch=[pltpu.VMEM((n_cols, width, sides), F32)],
        after=after,
    )


def put_pieces(form, meta, pieces, outs):
    depth, sub = form.depth, form.width // form.depth
    for k in range(depth):
        at = pl.multiple_of(lax.rem(meta[2] + depth - k, depth) * sub, sub)
        for c in range(form.n_cols):
            outs[c][pl.ds(at, sub)] = pieces[k][c * sub : (c + 1) * sub]


def lower_body(s, form, meta, *refs):
    chips, n_cols, eqs = form.chips, form.n_cols, form.eqs
    refs = list(refs)
    held = take(refs, n_cols * chips)
    width = form.width
    known = [[refs.pop(0) for _ in range(n_cols)] for _ in range(s - 1)]
    pieces = [refs.pop(0) for _ in range(form.depth)]
    own = refs.pop(0)
    far = [refs.pop(0) for _ in range(form.px - 1)]
    outs, newest = refs[: form.py], refs[form.py :]
    put_pieces(form, meta, pieces, newest)
    total = None
    for t, blocks in enumerate(known + [newest]):
        for c in range(n_cols):
            lanes = slice(slot_of(s, t) * width, (slot_of(s, t) + 1) * width)
            rows = jnp.concatenate([held[c * chips + k][:, lanes] for k in range(chips)], axis=0)
            term = jnp.dot(rows, blocks[c][...], preferred_element_type=F32)
            total = term if total is None else total + term
    parts = [total[k * eqs : (k + 1) * eqs] for k in range(chips)]
    lane = width + (form.px + s - 1) * form.sides
    for k, (dy, dx) in enumerate(form.shifts):
        if dy == 0:
            right = far[dx - 1][:, lane : lane + form.sides] if dx else own[s]
            parts[k] = parts[k] - right.astype(F32)
    for e in range(form.py):
        for k, (dy, dx) in enumerate(form.shifts):
            mine = form.shifts.index(((dy - e) % form.py, dx))
            outs[e][k * eqs : (k + 1) * eqs] = parts[mine].astype(outs[e].dtype)


def lower_product(s, form, meta, held, known, pieces, own, far, after=()):
    rows, sides = form.chips * form.eqs, form.sides
    flat = [x for blocks in known for x in blocks]
    ins = [meta, *held, *flat, *pieces, own, *far]
    return call(
        functools.partial(lower_body, s, form),
        [shaped((rows, sides), F32)]
        + [shaped((rows, sides), BF16)] * (form.py - 1)
        + [shaped((form.width, sides), BF16)] * form.n_cols,
        ins,
        [SMALL] + [WHOLE] * (len(ins) - 1),
        flops=2 * s * form.n_cols * form.width * rows * sides,
        after=after,
    )


def place_body(form, meta, *refs):
    put_pieces(form, meta, refs[: form.depth], refs[form.depth :])


def place(form, meta, pieces, after=()):
    return call(
        functools.partial(place_body, form),
        [shaped((form.width, form.sides), BF16)] * form.n_cols,
        [meta, *pieces],
        [SMALL] + [WHOLE] * form.depth,
        after=after,
    )


def gate_body(*refs):
    pass


def gate(x, after):
    return call(
        gate_body,
        [shaped(x.shape, x.dtype)],
        [x],
        [pl.BlockSpec(memory_space=pl.ANY)],
        after=after,
        out_specs=(pl.BlockSpec(memory_space=pl.ANY),),
        input_output_aliases={0: 0},
    )[0]


def join_body(form, count, meta, *refs):
    width, sides = form.width, form.sides
    for i in range(count):
        for k in range(form.n_cols):
            at = pl.multiple_of(lax.rem(meta[3] + k, form.n_cols) * sides, sides)
            refs[-1][i * width : (i + 1) * width, pl.ds(at, sides)] = refs[i * form.n_cols + k][...]


def join(form, meta, parts, after=()):
    count = len(parts) // form.n_cols
    return call(
        functools.partial(join_body, form, count),
        [shaped((count * form.width, form.n_cols * form.sides), BF16)],
        [meta, *parts],
        [SMALL] + [WHOLE] * len(parts),
        after=after,
    )[0]


def flat_body(x, *refs):
    refs[-2][...] = jnp.swapaxes(x[...], 0, 1)
    refs[-1][...] = jnp.zeros_like(refs[-1])


def flat_rest(lower_rest, buffer, turn, turns, block, after=()):
    rest, steps, share = lower_rest.shape
    first = turn * (rest // turns // block)
    ins, alias = [lower_rest], {}
    specs = [pl.BlockSpec((block, steps, share), lambda i: (first + i, 0, 0))]
    if buffer is not None:
        alias = {1: 0}
        ins.append(buffer)
        specs.append(pl.BlockSpec(memory_space=pltpu.HBM))
    return call(
        flat_body,
        [pltpu.HBM((steps, rest, share), BF16), shaped((8, 128), F32)],
        ins,
        specs,
        after=after,
        grid=(rest // turns // block,),
        out_specs=(
            pl.BlockSpec((steps, block, share), lambda i: (0, first + i, 0)),
            pl.BlockSpec((8, 128), lambda i: (0, 0)),
        ),
        input_output_aliases=alias,
    )


def write_body(form, count, meta, *refs):
    parts = take(list(refs), form.chips)
    put_solved(form, count, meta, parts, *refs[-2:])


def put_solved(form, count, meta, parts, out, turned):
    width, sides = form.width, form.sides
    for i in range(count):
        for k, (dy, dx) in enumerate(form.shifts):
            y, x = lax.rem(meta[0] + form.py - dy, form.py), lax.rem(meta[1] + form.px - dx, form.px)
            block = parts[k][i * width : (i + 1) * width]
            row = pl.ds(pl.multiple_of(y * width, width), width)
            for c in range(form.n_cols):
                lane = pl.ds(pl.multiple_of((c * form.px + x) * sides, sides), sides)
                piece = block[:, c * sides : (c + 1) * sides]
                out[i, row, lane] = piece
                turned[i, lane, row] = piece.T


def write(s, steps, form, meta, parts, buffer, after=()):
    share, total = form.py * form.width, form.px * form.n_cols * form.sides
    count = parts[0].shape[-2] // form.width
    ins = [meta, *parts]
    specs = [SMALL] + [pl.BlockSpec(x.shape, lambda i, n=x.ndim: (0,) * n) for x in parts]
    alias = {}
    if buffer is not None:
        alias = {len(ins): 0}
        ins.append(buffer)
        specs.append(pl.BlockSpec(memory_space=pltpu.HBM))
    return call(
        functools.partial(write_body, form, count),
        [pltpu.HBM((steps, share, total), BF16), shaped((count, total, share), BF16)],
        ins,
        specs,
        after=after,
        grid=(1,),
        out_specs=(
            pl.BlockSpec((count, share, total), lambda i: (s // count, 0, 0)),
            pl.BlockSpec((count, total, share), lambda i: (0, 0, 0)),
        ),
        input_output_aliases=alias,
    )


def rest_body(form, counts, running, meta, *refs):
    turned, lower, refs = refs[: len(counts)], refs[len(counts)], refs[len(counts) + 1 :]
    before, outs = refs[:running], refs[running:]
    sides = form.px * form.sides
    for order, out in enumerate(outs):
        at = pl.multiple_of(lax.rem(meta[3] + order, form.n_cols) * sides, sides)
        total, t = None, 0
        for x, count in zip(turned, counts):
            for i in range(count):
                term = nt_dot(x[i, pl.ds(at, sides), :], lower[t])
                total = term if total is None else total + term
                t += 1
        if running:
            total = total + before[order][...].astype(F32)
        out[...] = total.astype(out.dtype)


def rest_product(first, form, meta, turned, lower, before=(), after=()):
    orders = range(form.n_cols)
    _, rest, share = lower.shape
    counts = [x.shape[0] for x in turned]
    count = sum(counts)
    sides = form.px * form.sides
    block = max(n for n in (768, 512, 384, 256, 128) if rest % n == 0)
    side_block = pl.BlockSpec((sides, block), lambda i: (0, i))
    return call(
        functools.partial(rest_body, form, counts, len(before)),
        [shaped((sides, rest), F32 if order == 0 else BF16) for order in orders],
        [meta, *turned, pltpu.with_memory_space_constraint(lower, pltpu.HBM), *before],
        [SMALL]
        + [pl.BlockSpec(x.shape, lambda i: (0, 0, 0)) for x in turned]
        + [pl.BlockSpec((count, block, share), lambda i: (first // count, i, 0))]
        + [side_block] * len(before),
        flops=2 * count * share * sides * rest * len(orders),
        after=after,
        grid=(rest // block,),
        out_specs=(side_block,) * len(orders),
    )


def last_body(form, running, meta, *refs):
    refs = list(refs)
    parts = take(refs, form.chips)
    lower, before, (out, *sums, turned) = refs[0], refs[1 : 1 + running], refs[2 + running :]

    @pl.when(pl.program_id(0) == 0)
    def _():
        put_solved(form, 1, meta, parts, out, turned)

    sides = form.px * form.sides
    for order, to in enumerate(sums):
        at = pl.multiple_of(lax.rem(meta[3] + order, form.n_cols) * sides, sides)
        total = nt_dot(turned[0, pl.ds(at, sides), :], lower[0])
        if running:
            total = total + before[order][...].astype(F32)
        to[...] = total.astype(to.dtype)


def late_step(s, form, meta, parts, lower, buffer, before=(), after=()):
    steps, rest, share = lower.shape
    total, sides = form.px * form.n_cols * form.sides, form.px * form.sides
    block = max(n for n in (768, 512, 384, 256, 128) if rest % n == 0)
    lower = pltpu.with_memory_space_constraint(lower, pltpu.HBM)
    side_block = pl.BlockSpec((sides, block), lambda i: (0, i))
    return call(
        functools.partial(last_body, form, len(before)),
        [pltpu.HBM((steps, share, total), BF16)]
        + [shaped((sides, rest), F32 if order == 0 else BF16) for order in range(form.n_cols)],
        [meta, *parts, lower, *before, buffer],
        [SMALL]
        + [pl.BlockSpec(x.shape, lambda i, n=x.ndim: (0,) * n) for x in parts]
        + [pl.BlockSpec((1, block, share), lambda i: (s, i, 0))]
        + [side_block] * len(before)
        + [pl.BlockSpec(memory_space=pltpu.HBM)],
        flops=2 * share * total * rest,
        scratch=[pltpu.VMEM((1, total, share), BF16)],
        after=after,
        grid=(rest // block,),
        out_specs=(pl.BlockSpec((1, share, total), lambda i: (s, 0, 0)), *[side_block] * form.n_cols),
        input_output_aliases={len(parts) + 2 + len(before): 0},
    )


@dataclasses.dataclass
class Form:
    py: int
    px: int
    depth: int
    n_cols: int
    eqs: int
    width: int
    sides: int

    def __post_init__(self):
        self.shifts = [(dy, dx) for dx in range(self.px) for dy in range(self.py)]
        self.chips = len(self.shifts)


def form_of(lower_pivot, rhs_pivot):
    n_rows = lax.axis_size("rows")
    plane = split_of(n_rows)
    px = split_of(plane)
    py = plane // px
    return Form(
        py, px, n_rows // plane, lax.axis_size("cols"), lower_pivot.shape[1], lower_pivot.shape[3] // py,
        rhs_pivot.shape[2] // px,
    )


def kernel_path(form, lower_pivot, lower_rest, diag_inverse, rhs_pivot, rhs_rest):
    lower_pivot, lower_rest, diag_inverse, rhs_pivot = (
        pltpu.with_memory_space_constraint(x, pltpu.HBM) for x in (lower_pivot, lower_rest, diag_inverse, rhs_pivot)
    )
    steps = lower_pivot.shape[0]
    rest = lower_rest.shape[0]
    py, px, depth, n_cols, chips = form.py, form.px, form.depth, form.n_cols, form.chips
    row = lax.axis_index("rows")
    meta = jnp.stack([row // px % py, row % px, row // chips, lax.axis_index("cols")]).astype(jnp.int32)

    def along_plane(x, dy, dx):
        pairs = [
            ((b * py + y) * px + i, (b * py + (y + dy) % py) * px + (i + dx) % px)
            for b in range(depth)
            for y in range(py)
            for i in range(px)
        ]
        return lax.ppermute(x, "rows", pairs)

    def along_depth(x, k):
        pairs = [(b * chips + i, (b + k) % depth * chips + i) for b in range(depth) for i in range(chips)]
        return lax.ppermute(x, "rows", pairs)

    def along_cols(x, k):
        return lax.ppermute(x, "cols", [(i, (i + k) % n_cols) for i in range(n_cols)])

    def up(blocks):
        return [blocks[0]] + [along_plane(blocks[dy], dy, 0) for dy in range(1, py)]

    def across(x):
        return [along_plane(x, 0, dx) for dx in range(1, px)]

    def onward(first, direct, after=()):
        rest = [gate(x, after) if after else x for x in first[1:]]
        far = [across(x) for x in rest]
        got = [first[0], *rest]
        for dx in range(px - 1):
            got += [direct[dx]] + [x[dx] for x in far]
        return got

    def held_of(parts, after):
        mine = [pack(parts, after)] if after else parts
        return mine + [along_cols(x, c) for c in range(1, n_cols) for x in mine]

    def joined(ts, after=()):
        parts = []
        for t in ts:
            parts += [known[t][0]] + [along_cols(known[t][k], -k) for k in range(1, n_cols)]
        return join(form, meta, parts, after)

    turns = 3
    block = 256
    while rest % (turns * block):
        turns -= 1
    last = steps - 1
    near, far, own = start(form, meta, diag_inverse, rhs_pivot)
    got = up(near)
    here = [along_plane(x, 0, dx + 1) for dx, x in enumerate(far)]
    packed, ahead = prep(tuple(range(1, steps)), form, meta, diag_inverse, lower_pivot)
    first = up([gate(x, got[1:]) for x in packed[1]])
    got = onward(got, here, [packed[1][0]])
    later = [gate(x, [*got[py + 1 :], *first[1:]]) for x in got[py :: py]]
    held = held_of([later[k // py - 1] if k >= py and k % py == 0 else x for k, x in enumerate(got)], ())
    moved = pack(first)
    moved = [moved, *across(moved)]
    known, sums, turned, flat, buffer = [], [], [], None, None
    by_lower, by_diag, by_sum = ({s: [] for s in range(steps + 1)} for _ in range(3))
    by_diag[0] += [packed[last][0], *first[1:]]
    by_sum[0] += moved
    for s in range(steps):
        if s > 0:
            outs = lower_product(s, form, meta, held, known, pieces, own, here, by_lower[s])
            known.append(outs[py:])
            sums = [outs[0]] + [along_plane(outs[e], e, 0) for e in range(1, py)]
            if s >= last - 1:
                whole = joined(range(s) if s < last else [s - 1], [outs[0]])
                by_diag[s].append(whole)
        products = diag_product(form, meta, held, sums, by_diag[s])
        if s < last - 1:
            first = up([gate(x, [products[0]]) for x in packed[s + 2]])
        else:
            first = up([gate(whole, [products[0]])] * py)
        by_sum[s] += first[1:]
        if s < turns:
            flat, mark = flat_rest(lower_rest, flat, s, turns, block, [products[0]])
            by_sum[s].append(mark)
        arrivals = [along_depth(products[k], -k) for k in range(1, depth)]
        arrivals[-1] = gate(arrivals[-1], by_sum[s])
        total = products[0]
        for x in arrivals:
            total = total + x.astype(F32)
        mine = total.astype(BF16)
        if s < last:
            held = held_of(moved, [mine])
        pieces = [mine] + [along_depth(mine, k) for k in range(1, depth)]
        soon = pieces[1:2] if s == last - 1 else [mine]
        ready, moved = moved, pack(first, soon, ahead.get(s + 2, ()))
        moved = [moved, *across(moved)]
        by_sum[s + 1] += moved if s < last - 1 else []
        if s + 3 in ahead:
            ahead[s + 3] = up([gate(x, pieces[1:2]) for x in ahead[s + 3]])
            by_diag[s + 1] += ahead[s + 3][1:]
        if s == last:
            buffer, new = write(0, steps, form, meta, ready, buffer, [mine])
            turned.append(new)
            by_lower[s + 1].append(new)
    known.append(place(form, meta, pieces, by_lower[steps]))
    whole = joined([last])
    got = up([whole] * py)
    direct = across(got[0])
    early = rest_product(0, form, meta, turned, flat, (), [whole, *moved])
    got = onward(got, direct, [early[0], *moved])
    buffer, *early = late_step(last - 1, form, meta, moved, flat, buffer, early)
    buffer, *late = late_step(last, form, meta, got, flat, buffer, early)
    total = rhs_rest.astype(F32) - late[0]
    for c in range(1, n_cols):
        total = total - along_cols(late[c], c).astype(F32)
    return buffer, total.astype(BF16)


def per_device(lower_pivot, lower_rest, diag_inverse, rhs_pivot, rhs_rest):
    form = form_of(lower_pivot, rhs_pivot)
    fits = form.eqs % 128 == 0 and form.width % form.eqs == 0 and form.sides % 128 == 0
    fits = fits and (form.width // form.depth) % 16 == 0 and lower_rest.shape[0] % 128 == 0
    if fits:
        return kernel_path(form, lower_pivot, lower_rest, diag_inverse, rhs_pivot, rhs_rest)
    return plain_path(lower_pivot, lower_rest, diag_inverse, rhs_pivot, rhs_rest)


def solution(mesh):
    placed = (
        P(None, "rows", None, "cols"),
        P("rows", None, "cols"),
        P(None, "cols", "rows"),
        P(None, "rows", "cols"),
        P("cols", "rows"),
    )
    return jax.shard_map(
        per_device,
        mesh=mesh,
        in_specs=placed,
        out_specs=(P(None, "cols", None), P("cols", "rows")),
        check_vma=False,
    )
```

```python
import dataclasses
import functools
import math

import jax
import jax.numpy as jnp
from jax import lax
from jax.sharding import PartitionSpec as P
from jax.experimental import pallas as pl
from jax.experimental.pallas import tpu as pltpu

F32 = jnp.float32
BF16 = jnp.bfloat16


def split_of(count):
    best = 1
    for d in range(1, count + 1):
        if count % d == 0 and d * d <= count:
            best = d
    return best


def nt_dot(a, b):
    return lax.dot_general(a, b, (((1,), (1,)), ((), ())), preferred_element_type=F32)


def cut(n_rows, share):
    plane = split_of(n_rows)
    power = plane & (plane - 1) == 0
    code = [g ^ (g >> 1) if power else g for g in range(plane)]
    return plane, n_rows // plane, share // plane, code


def places(plane, code):
    row = lax.axis_index("rows")
    spot = row % plane
    g = sum(jnp.where(spot == code[i], i, 0) for i in range(plane))
    return g, row // plane, lax.axis_index("cols")


def movers(plane, depth, code, n_cols):
    def along_plane(x, k):
        pairs = [(b * plane + code[i], b * plane + code[(i + k) % plane]) for b in range(depth) for i in range(plane)]
        return lax.ppermute(x, "rows", pairs)

    def along_depth(x, k):
        pairs = [(b * plane + i, ((b + k) % depth) * plane + i) for b in range(depth) for i in range(plane)]
        return lax.ppermute(x, "rows", pairs)

    def along_cols(x, k):
        return lax.ppermute(x, "cols", [(i, (i + k) % n_cols) for i in range(n_cols)])

    return along_plane, along_depth, along_cols


def plain_path(lower_pivot, lower_rest, diag_inverse, rhs_pivot, rhs_rest):
    steps = lower_pivot.shape[0]
    eqs = lower_pivot.shape[1]
    share = lower_pivot.shape[3]
    sides = rhs_pivot.shape[2]
    rest = lower_rest.shape[0]
    n_rows = lax.axis_size("rows")
    n_cols = lax.axis_size("cols")
    plane, depth, width, code = cut(n_rows, share)
    g, z, core = places(plane, code)
    part = sides // depth
    along_plane, along_depth, along_cols = movers(plane, depth, code, n_cols)

    def gather(move, count, x, axis):
        return jnp.concatenate([x] + [move(x, k) for k in range(1, count)], axis=axis)

    def my_diag(s):
        block = diag_inverse[s].reshape(plane, width, eqs)
        parts = [lax.dynamic_index_in_dim(block, (g + k) % plane, 0, False) for k in range(plane)]
        held = jnp.concatenate([parts[0]] + [along_plane(parts[k], k) for k in range(1, plane)], axis=1)
        return gather(along_cols, n_cols, held, 0)

    def my_lower(s):
        parts = [
            lax.dynamic_slice_in_dim(lower_pivot[s, :, :s, :], ((g + k) % plane) * width, width, 2)
            for k in range(plane)
        ]
        held = jnp.concatenate([parts[0]] + [along_plane(parts[k], k) for k in range(1, plane)], axis=0)
        return gather(along_cols, n_cols, held, 2)

    def rolled(x, shift, axis):
        return jnp.roll(x, shift, axis)

    rhs_t = jnp.swapaxes(rhs_pivot, 1, 2)
    blocks = rhs_t.reshape(steps, depth, part, eqs)[:, ::-1]
    blocks = rolled(blocks, z + 1, 1).reshape(steps, sides, eqs)

    solved = []
    totals = jnp.zeros((sides, rest), F32)
    outs = []
    for s in range(steps):
        diag = my_diag(s)
        if s == 0:
            own = blocks[0]
        else:
            lower = my_lower(s)
            partial = jnp.zeros((sides, plane * eqs), F32)
            for t in range(s):
                partial = partial + nt_dot(solved[t], lower[:, t, :])
            total = blocks[s].astype(F32) - partial[:, :eqs]
            sent = partial.astype(BF16)
            for k in range(1, plane):
                total = total - along_plane(sent[:, k * eqs : (k + 1) * eqs], -k).astype(F32)
            own = total.astype(BF16)
        residual = gather(along_plane, plane, own, 1)
        product = nt_dot(residual, diag)
        sent = product.astype(BF16)
        total = product[:part]
        for k in range(1, depth):
            total = total + along_depth(sent[k * part : (k + 1) * part], -k).astype(F32)
        mine = total.astype(BF16)
        here = gather(along_depth, depth, mine, 0)
        solved.append(here)
        pieces = [here] + [along_plane(here, k) for k in range(1, plane)]
        pieces = [pieces[(-k) % plane] for k in range(plane)]
        full = jnp.stack([p.reshape(depth, part, n_cols, width) for p in pieces], axis=3)
        full = full[jnp.array([(-k) % depth for k in range(depth)])]
        full = rolled(full, z, 0)
        full = rolled(full, g, 3).reshape(sides, n_cols, share)
        rest_parts = [lower_rest[:, s, :]] + [along_cols(lower_rest[:, s, :], k) for k in range(1, n_cols)]
        for k in range(n_cols):
            totals = totals + nt_dot(full[:, k, :], rest_parts[k])
        theirs = [full[:, 0]] + [along_cols(full[:, k], -k) for k in range(1, n_cols)]
        theirs = rolled(jnp.stack(theirs, 0), core, 0).reshape(n_cols * sides, share)
        outs.append(theirs.T)
    remainder = (rhs_rest.astype(F32) - totals).astype(BF16)
    return jnp.stack(outs), remainder


VMEM_LIMIT = 40 * 1024 * 1024
WEIGHT = 8
SMALL = pl.BlockSpec(memory_space=pltpu.SMEM)
WHOLE = pl.BlockSpec(memory_space=pltpu.VMEM)


def call(body, outs, ins, specs, flops=0, scratch=(), after=(), weight=1, **more):
    size = sum(math.prod(x.shape) * x.dtype.itemsize for x in [*ins, *outs])
    first, last = len(ins), len(ins) + len(after)

    def run(*refs):
        body(*refs[:first], *refs[last:])

    return pl.pallas_call(
        run,
        out_shape=tuple(outs),
        in_specs=list(specs) + [pl.BlockSpec(memory_space=pl.ANY)] * len(after),
        scratch_shapes=list(scratch),
        compiler_params=pltpu.CompilerParams(vmem_limit_bytes=VMEM_LIMIT),
        cost_estimate=pl.CostEstimate(flops=flops, bytes_accessed=size * weight, transcendentals=0),
        **more,
    )(*ins, *after)


def shaped(dims, kind):
    return jax.ShapeDtypeStruct(dims, kind)


def put_diag(form, meta, dy, block, out):
    at = lax.rem(meta[0] + dy, form.py) * form.width
    for h in range(form.width // form.eqs):
        lanes = slice(h * form.eqs, (h + 1) * form.eqs)
        out[:, lanes] = block[pl.ds(pl.multiple_of(at + h * form.eqs, form.eqs), form.eqs), :]


def start_body(form, meta, diag, rhs, *refs):
    py, px, width, sides = form.py, form.px, form.width, form.sides
    own, outs, far = refs[-1], refs[:py], refs[py:-1]

    def part(s, dx):
        return rhs[s, :, pl.ds(pl.multiple_of(lax.rem(meta[1] + dx, px) * sides, sides), sides)]

    for dy in range(py):
        put_diag(form, meta, dy, diag.at[0], outs[dy])
        outs[dy][:, width:] = rhs[0]
    for dx in range(1, px):
        out = far[dx - 1]
        put_diag(form, meta, 0, diag.at[0], out)
        out[:, width : width + px * sides] = rhs[0]
        for s in range(1, rhs.shape[0]):
            out[:, width + (px + s - 1) * sides : width + (px + s) * sides] = part(s, dx)
    for s in range(rhs.shape[0]):
        own[s] = part(s, 0)


def start(form, meta, diag_inverse, rhs_pivot):
    width, eqs, sides, share = form.width, form.eqs, form.sides, form.py * form.width
    steps = rhs_pivot.shape[0]
    dims = [(eqs, width + form.px * sides)] * form.py
    dims += [(eqs, width + (form.px + steps - 1) * sides)] * (form.px - 1) + [(steps, eqs, sides)]
    outs = call(
        functools.partial(start_body, form),
        [shaped(d, BF16) for d in dims],
        [meta, diag_inverse, rhs_pivot],
        [
            SMALL,
            pl.BlockSpec((1, share, eqs), lambda i: (0, 0, 0)),
            pl.BlockSpec(rhs_pivot.shape, lambda i: (0, 0, 0)),
        ],
        weight=WEIGHT,
        grid=(1,),
        out_specs=tuple(pl.BlockSpec(d, lambda i, n=len(d): (0,) * n) for d in dims),
    )
    return outs[: form.py], outs[form.py : -1], outs[-1]


def slots(s):
    return [t for t in range(s) if s < 3 or t > 0], [0] if s > 2 else []


def slot_of(s, t):
    later, ahead = slots(s)
    return 1 + (later + ahead).index(t)


def prep_body(ss, form, meta, diag, lower, *refs):
    py, width = form.py, form.width
    refs, flat = list(refs[:-1]), refs[-1]
    for i, s in enumerate(ss):
        flat[...] = jnp.swapaxes(lower[i], 0, 1)
        later, ahead = slots(s)
        outs = [refs.pop(0) for _ in range(py)]
        early = [refs.pop(0) for _ in range(py)] if ahead else []
        for dy in range(py):
            put_diag(form, meta, dy, diag.at[i], outs[dy])
            at = pl.ds(pl.multiple_of(lax.rem(meta[0] + dy, py) * width, width), width)
            for j, t in enumerate(later):
                outs[dy][:, (1 + j) * width : (2 + j) * width] = flat[t, :, at]
            for j, t in enumerate(ahead):
                early[dy][:, j * width : (j + 1) * width] = flat[t, :, at]


def prep(ss, form, meta, diag_inverse, lower_pivot, after=()):
    width, eqs, share = form.width, form.eqs, form.py * form.width
    steps, count = lower_pivot.shape[0], len(ss)
    dims = []
    for s in ss:
        later, ahead = slots(s)
        dims += [(eqs, (1 + len(later)) * width)] * form.py + [(eqs, len(ahead) * width)] * (form.py if ahead else 0)
    outs = call(
        functools.partial(prep_body, ss, form),
        [shaped(d, BF16) for d in dims],
        [meta, diag_inverse, lower_pivot],
        [
            SMALL,
            pl.BlockSpec((pl.Element(count), pl.Element(share), pl.Element(eqs)), lambda i: (ss[0], 0, 0)),
            pl.BlockSpec(
                (pl.Element(count), pl.Element(eqs), pl.Element(steps), pl.Element(share)), lambda i: (ss[0], 0, 0, 0)
            ),
        ],
        scratch=[pltpu.VMEM((steps, eqs, share), BF16)],
        after=after,
        weight=WEIGHT,
        grid=(1,),
        out_specs=tuple(pl.BlockSpec(d, lambda i: (0, 0)) for d in dims),
    )
    packed, ahead, outs = {}, {}, list(outs)
    for s in ss:
        packed[s] = [outs.pop(0) for _ in range(form.py)]
        if slots(s)[1]:
            ahead[s] = [outs.pop(0) for _ in range(form.py)]
    return packed, ahead


def pack_body(count, first, *refs):
    refs = list(refs)
    for k, part in enumerate(take(refs, count)):
        refs[-1][k, :, :first] = part[...]
    for k in range(len(refs) - 1):
        refs[-1][k, :, first:] = refs[k][...]


def pack(parts, after=(), beside=()):
    count = sum(1 if x.ndim == 2 else x.shape[0] for x in parts)
    rows, first = parts[0].shape[-2:]
    lanes = first + (beside[0].shape[-1] if beside else 0)
    ins = [*parts, *beside]
    return call(
        functools.partial(pack_body, count, first),
        [shaped((count, rows, lanes), BF16)],
        ins,
        [WHOLE] * len(ins),
        after=after,
        weight=WEIGHT,
    )[0]


def take(refs, count):
    got = []
    while len(got) < count:
        ref = refs.pop(0)
        got += [ref] if len(ref.shape) == 2 else [ref.at[k] for k in range(ref.shape[0])]
    return got


def diag_body(form, terms, meta, *refs):
    chips, n_cols, depth, eqs, width, sides = form.chips, form.n_cols, form.depth, form.eqs, form.width, form.sides
    refs = list(refs)
    held = take(refs, n_cols * chips)
    sums = [refs.pop(0) for _ in range(terms)]
    outs, product = refs[:-1], refs[-1]
    sub = width // depth
    if terms:
        total = sums[0][...]
        for x in sums[1:]:
            total = total + x[...].astype(F32)
        residual = (-total).astype(BF16)
    else:
        right = pl.ds(pl.multiple_of(width + meta[1] * sides, sides), sides)
        residual = jnp.concatenate([held[k][:, right] for k in range(chips)], axis=0)
    for c in range(n_cols):
        rows = [
            jnp.concatenate([held[c * chips + k][:, h * eqs : (h + 1) * eqs] for k in range(chips)], axis=1)
            for h in range(width // eqs)
        ]
        product[c] = jnp.dot(jnp.concatenate(rows, axis=0), residual, preferred_element_type=F32)
    for k in range(depth):
        at = pl.multiple_of(lax.rem(meta[2] + depth - k, depth) * sub, sub)
        for c in range(n_cols):
            outs[k][c * sub : (c + 1) * sub] = product[c, pl.ds(at, sub)].astype(outs[k].dtype)


def diag_product(form, meta, held, sums, after=()):
    width, eqs, sides, depth, n_cols, chips = form.width, form.eqs, form.sides, form.depth, form.n_cols, form.chips
    dims = (n_cols * (width // depth), sides)
    return call(
        functools.partial(diag_body, form, len(sums)),
        [shaped(dims, F32)] + [shaped(dims, BF16)] * (depth - 1),
        [meta, *held, *sums],
        [SMALL] + [WHOLE] * (len(held) + len(sums)),
        flops=2 * n_cols * width * chips * eqs * sides,
        scratch=[pltpu.VMEM((n_cols, width, sides), F32)],
        after=after,
    )


def put_pieces(form, meta, pieces, outs):
    depth, sub = form.depth, form.width // form.depth
    for k in range(depth):
        at = pl.multiple_of(lax.rem(meta[2] + depth - k, depth) * sub, sub)
        for c in range(form.n_cols):
            outs[c][pl.ds(at, sub)] = pieces[k][c * sub : (c + 1) * sub]


def lower_body(s, form, meta, *refs):
    chips, n_cols, eqs = form.chips, form.n_cols, form.eqs
    refs = list(refs)
    held = take(refs, n_cols * chips)
    width = form.width
    known = [[refs.pop(0) for _ in range(n_cols)] for _ in range(s - 1)]
    pieces = [refs.pop(0) for _ in range(form.depth)]
    own = refs.pop(0)
    far = [refs.pop(0) for _ in range(form.px - 1)]
    outs, newest = refs[: form.py], refs[form.py :]
    put_pieces(form, meta, pieces, newest)
    total = None
    for t, blocks in enumerate(known + [newest]):
        for c in range(n_cols):
            lanes = slice(slot_of(s, t) * width, (slot_of(s, t) + 1) * width)
            rows = jnp.concatenate([held[c * chips + k][:, lanes] for k in range(chips)], axis=0)
            term = jnp.dot(rows, blocks[c][...], preferred_element_type=F32)
            total = term if total is None else total + term
    parts = [total[k * eqs : (k + 1) * eqs] for k in range(chips)]
    lane = width + (form.px + s - 1) * form.sides
    for k, (dy, dx) in enumerate(form.shifts):
        if dy == 0:
            right = far[dx - 1][:, lane : lane + form.sides] if dx else own[s]
            parts[k] = parts[k] - right.astype(F32)
    for e in range(form.py):
        for k, (dy, dx) in enumerate(form.shifts):
            mine = form.shifts.index(((dy - e) % form.py, dx))
            outs[e][k * eqs : (k + 1) * eqs] = parts[mine].astype(outs[e].dtype)


def lower_product(s, form, meta, held, known, pieces, own, far, after=()):
    rows, sides = form.chips * form.eqs, form.sides
    flat = [x for blocks in known for x in blocks]
    ins = [meta, *held, *flat, *pieces, own, *far]
    return call(
        functools.partial(lower_body, s, form),
        [shaped((rows, sides), F32)]
        + [shaped((rows, sides), BF16)] * (form.py - 1)
        + [shaped((form.width, sides), BF16)] * form.n_cols,
        ins,
        [SMALL] + [WHOLE] * (len(ins) - 1),
        flops=2 * s * form.n_cols * form.width * rows * sides,
        after=after,
    )


def place_body(form, meta, *refs):
    put_pieces(form, meta, refs[: form.depth], refs[form.depth :])


def place(form, meta, pieces, after=()):
    return call(
        functools.partial(place_body, form),
        [shaped((form.width, form.sides), BF16)] * form.n_cols,
        [meta, *pieces],
        [SMALL] + [WHOLE] * form.depth,
        after=after,
    )


def gate_body(*refs):
    pass


def gate(x, after):
    return call(
        gate_body,
        [shaped(x.shape, x.dtype)],
        [x],
        [pl.BlockSpec(memory_space=pl.ANY)],
        after=after,
        out_specs=(pl.BlockSpec(memory_space=pl.ANY),),
        input_output_aliases={0: 0},
    )[0]


def join_body(form, count, meta, *refs):
    width, sides = form.width, form.sides
    for i in range(count):
        for k in range(form.n_cols):
            at = pl.multiple_of(lax.rem(meta[3] + k, form.n_cols) * sides, sides)
            refs[-1][i * width : (i + 1) * width, pl.ds(at, sides)] = refs[i * form.n_cols + k][...]


def join(form, meta, parts, after=()):
    count = len(parts) // form.n_cols
    return call(
        functools.partial(join_body, form, count),
        [shaped((count * form.width, form.n_cols * form.sides), BF16)],
        [meta, *parts],
        [SMALL] + [WHOLE] * len(parts),
        after=after,
    )[0]


def flat_body(x, *refs):
    refs[-2][...] = jnp.swapaxes(x[...], 0, 1)
    refs[-1][...] = jnp.zeros_like(refs[-1])


def flat_rest(lower_rest, buffer, turn, turns, block, after=()):
    rest, steps, share = lower_rest.shape
    first = turn * (rest // turns // block)
    ins, alias = [lower_rest], {}
    specs = [pl.BlockSpec((block, steps, share), lambda i: (first + i, 0, 0))]
    if buffer is not None:
        alias = {1: 0}
        ins.append(buffer)
        specs.append(pl.BlockSpec(memory_space=pltpu.HBM))
    return call(
        flat_body,
        [pltpu.HBM((steps, rest, share), BF16), shaped((8, 128), F32)],
        ins,
        specs,
        after=after,
        grid=(rest // turns // block,),
        out_specs=(
            pl.BlockSpec((steps, block, share), lambda i: (0, first + i, 0)),
            pl.BlockSpec((8, 128), lambda i: (0, 0)),
        ),
        input_output_aliases=alias,
    )


def write_body(form, count, meta, *refs):
    parts = take(list(refs), form.chips)
    put_solved(form, count, meta, parts, *refs[-2:])


def put_solved(form, count, meta, parts, out, turned):
    width, sides = form.width, form.sides
    for i in range(count):
        for k, (dy, dx) in enumerate(form.shifts):
            y, x = lax.rem(meta[0] + form.py - dy, form.py), lax.rem(meta[1] + form.px - dx, form.px)
            block = parts[k][i * width : (i + 1) * width]
            row = pl.ds(pl.multiple_of(y * width, width), width)
            for c in range(form.n_cols):
                lane = pl.ds(pl.multiple_of((c * form.px + x) * sides, sides), sides)
                piece = block[:, c * sides : (c + 1) * sides]
                out[i, row, lane] = piece
                turned[i, lane, row] = piece.T


def write(s, steps, form, meta, parts, buffer, after=()):
    share, total = form.py * form.width, form.px * form.n_cols * form.sides
    count = parts[0].shape[-2] // form.width
    ins = [meta, *parts]
    specs = [SMALL] + [pl.BlockSpec(x.shape, lambda i, n=x.ndim: (0,) * n) for x in parts]
    alias = {}
    if buffer is not None:
        alias = {len(ins): 0}
        ins.append(buffer)
        specs.append(pl.BlockSpec(memory_space=pltpu.HBM))
    return call(
        functools.partial(write_body, form, count),
        [pltpu.HBM((steps, share, total), BF16), shaped((count, total, share), BF16)],
        ins,
        specs,
        after=after,
        grid=(1,),
        out_specs=(
            pl.BlockSpec((count, share, total), lambda i: (s // count, 0, 0)),
            pl.BlockSpec((count, total, share), lambda i: (0, 0, 0)),
        ),
        input_output_aliases=alias,
    )


def rest_body(form, counts, running, meta, *refs):
    turned, lower, refs = refs[: len(counts)], refs[len(counts)], refs[len(counts) + 1 :]
    before, outs = refs[:running], refs[running:]
    sides = form.px * form.sides
    for order, out in enumerate(outs):
        at = pl.multiple_of(lax.rem(meta[3] + order, form.n_cols) * sides, sides)
        total, t = None, 0
        for x, count in zip(turned, counts):
            for i in range(count):
                term = nt_dot(x[i, pl.ds(at, sides), :], lower[t])
                total = term if total is None else total + term
                t += 1
        if running:
            total = total + before[order][...].astype(F32)
        out[...] = total.astype(out.dtype)


def rest_product(first, form, meta, turned, lower, before=(), after=()):
    orders = range(form.n_cols)
    _, rest, share = lower.shape
    counts = [x.shape[0] for x in turned]
    count = sum(counts)
    sides = form.px * form.sides
    block = max(n for n in (768, 512, 384, 256, 128) if rest % n == 0)
    side_block = pl.BlockSpec((sides, block), lambda i: (0, i))
    return call(
        functools.partial(rest_body, form, counts, len(before)),
        [shaped((sides, rest), F32 if order == 0 else BF16) for order in orders],
        [meta, *turned, pltpu.with_memory_space_constraint(lower, pltpu.HBM), *before],
        [SMALL]
        + [pl.BlockSpec(x.shape, lambda i: (0, 0, 0)) for x in turned]
        + [pl.BlockSpec((count, block, share), lambda i: (first // count, i, 0))]
        + [side_block] * len(before),
        flops=2 * count * share * sides * rest * len(orders),
        after=after,
        grid=(rest // block,),
        out_specs=(side_block,) * len(orders),
    )


def last_body(form, running, meta, *refs):
    refs = list(refs)
    parts = take(refs, form.chips)
    lower, before, (out, *sums, turned) = refs[0], refs[1 : 1 + running], refs[2 + running :]

    @pl.when(pl.program_id(0) == 0)
    def _():
        put_solved(form, 1, meta, parts, out, turned)

    sides = form.px * form.sides
    for order, to in enumerate(sums):
        at = pl.multiple_of(lax.rem(meta[3] + order, form.n_cols) * sides, sides)
        total = nt_dot(turned[0, pl.ds(at, sides), :], lower[0])
        if running:
            total = total + before[order][...].astype(F32)
        to[...] = total.astype(to.dtype)


def late_step(s, form, meta, parts, lower, buffer, before=(), after=()):
    steps, rest, share = lower.shape
    total, sides = form.px * form.n_cols * form.sides, form.px * form.sides
    block = max(n for n in (768, 512, 384, 256, 128) if rest % n == 0)
    lower = pltpu.with_memory_space_constraint(lower, pltpu.HBM)
    side_block = pl.BlockSpec((sides, block), lambda i: (0, i))
    return call(
        functools.partial(last_body, form, len(before)),
        [pltpu.HBM((steps, share, total), BF16)]
        + [shaped((sides, rest), F32 if order == 0 else BF16) for order in range(form.n_cols)],
        [meta, *parts, lower, *before, buffer],
        [SMALL]
        + [pl.BlockSpec(x.shape, lambda i, n=x.ndim: (0,) * n) for x in parts]
        + [pl.BlockSpec((1, block, share), lambda i: (s, i, 0))]
        + [side_block] * len(before)
        + [pl.BlockSpec(memory_space=pltpu.HBM)],
        flops=2 * share * total * rest,
        scratch=[pltpu.VMEM((1, total, share), BF16)],
        after=after,
        grid=(rest // block,),
        out_specs=(pl.BlockSpec((1, share, total), lambda i: (s, 0, 0)), *[side_block] * form.n_cols),
        input_output_aliases={len(parts) + 2 + len(before): 0},
    )


@dataclasses.dataclass
class Form:
    py: int
    px: int
    depth: int
    n_cols: int
    eqs: int
    width: int
    sides: int

    def __post_init__(self):
        self.shifts = [(dy, dx) for dx in range(self.px) for dy in range(self.py)]
        self.chips = len(self.shifts)


def form_of(lower_pivot, rhs_pivot):
    n_rows = lax.axis_size("rows")
    plane = split_of(n_rows)
    px = split_of(plane)
    py = plane // px
    return Form(
        py, px, n_rows // plane, lax.axis_size("cols"), lower_pivot.shape[1], lower_pivot.shape[3] // py,
        rhs_pivot.shape[2] // px,
    )


def kernel_path(form, lower_pivot, lower_rest, diag_inverse, rhs_pivot, rhs_rest):
    lower_pivot, lower_rest, diag_inverse, rhs_pivot = (
        pltpu.with_memory_space_constraint(x, pltpu.HBM) for x in (lower_pivot, lower_rest, diag_inverse, rhs_pivot)
    )
    steps = lower_pivot.shape[0]
    rest = lower_rest.shape[0]
    py, px, depth, n_cols, chips = form.py, form.px, form.depth, form.n_cols, form.chips
    row = lax.axis_index("rows")
    meta = jnp.stack([row // px % py, row % px, row // chips, lax.axis_index("cols")]).astype(jnp.int32)

    def along_plane(x, dy, dx):
        pairs = [
            ((b * py + y) * px + i, (b * py + (y + dy) % py) * px + (i + dx) % px)
            for b in range(depth)
            for y in range(py)
            for i in range(px)
        ]
        return lax.ppermute(x, "rows", pairs)

    def along_depth(x, k):
        pairs = [(b * chips + i, (b + k) % depth * chips + i) for b in range(depth) for i in range(chips)]
        return lax.ppermute(x, "rows", pairs)

    def along_cols(x, k):
        return lax.ppermute(x, "cols", [(i, (i + k) % n_cols) for i in range(n_cols)])

    def up(blocks):
        return [blocks[0]] + [along_plane(blocks[dy], dy, 0) for dy in range(1, py)]

    def across(x):
        return [along_plane(x, 0, dx) for dx in range(1, px)]

    def onward(first, direct, after=()):
        rest = [gate(x, after) if after else x for x in first[1:]]
        far = [across(x) for x in rest]
        got = [first[0], *rest]
        for dx in range(px - 1):
            got += [direct[dx]] + [x[dx] for x in far]
        return got

    def held_of(parts, after):
        mine = [pack(parts, after)] if after else parts
        return mine + [along_cols(x, c) for c in range(1, n_cols) for x in mine]

    def joined(ts, after=()):
        parts = []
        for t in ts:
            parts += [known[t][0]] + [along_cols(known[t][k], -k) for k in range(1, n_cols)]
        return join(form, meta, parts, after)

    turns = 3
    block = 512
    while rest % (turns * block):
        turns -= 1
    last = steps - 1
    near, far, own = start(form, meta, diag_inverse, rhs_pivot)
    got = up(near)
    here = [along_plane(x, 0, dx + 1) for dx, x in enumerate(far)]
    packed, ahead = prep(tuple(range(1, steps)), form, meta, diag_inverse, lower_pivot)
    first = up([gate(x, got[1:]) for x in packed[1]])
    got = onward(got, here, [packed[1][0]])
    later = [gate(x, [*got[py + 1 :], *first[1:]]) for x in got[py :: py]]
    held = held_of([later[k // py - 1] if k >= py and k % py == 0 else x for k, x in enumerate(got)], ())
    moved = pack(first)
    moved = [moved, *across(moved)]
    known, sums, turned, flat, buffer = [], [], [], None, None
    by_lower, by_diag, by_sum = ({s: [] for s in range(steps + 1)} for _ in range(3))
    by_diag[0] += [packed[last][0], *first[1:]]
    by_sum[0] += moved
    for s in range(steps):
        if s > 0:
            outs = lower_product(s, form, meta, held, known, pieces, own, here, by_lower[s])
            known.append(outs[py:])
            sums = [outs[0]] + [along_plane(outs[e], e, 0) for e in range(1, py)]
            if s >= last - 1:
                whole = joined(range(s) if s < last else [s - 1], [outs[0]])
                by_diag[s].append(whole)
        products = diag_product(form, meta, held, sums, by_diag[s])
        if s < last - 1:
            first = up([gate(x, [products[0]]) for x in packed[s + 2]])
        else:
            first = up([gate(whole, [products[0]])] * py)
        by_sum[s] += first[1:]
        if s < turns:
            flat, mark = flat_rest(lower_rest, flat, s, turns, block, [products[0]])
            by_sum[s].append(mark)
        arrivals = [along_depth(products[k], -k) for k in range(1, depth)]
        arrivals[-1] = gate(arrivals[-1], by_sum[s])
        total = products[0]
        for x in arrivals:
            total = total + x.astype(F32)
        mine = total.astype(BF16)
        if s < last:
            held = held_of(moved, [mine])
        pieces = [mine] + [along_depth(mine, k) for k in range(1, depth)]
        soon = pieces[1:2] if s == last - 1 else [mine]
        ready, moved = moved, pack(first, soon, ahead.get(s + 2, ()))
        moved = [moved, *across(moved)]
        by_sum[s + 1] += moved if s < last - 1 else []
        if s + 3 in ahead:
            ahead[s + 3] = up([gate(x, pieces[1:2]) for x in ahead[s + 3]])
            by_diag[s + 1] += ahead[s + 3][1:]
        if s == last:
            buffer, new = write(0, steps, form, meta, ready, buffer, [mine])
            turned.append(new)
            by_lower[s + 1].append(new)
    known.append(place(form, meta, pieces, by_lower[steps]))
    whole = joined([last])
    got = up([whole] * py)
    direct = across(got[0])
    early = rest_product(0, form, meta, turned, flat, (), [whole, *moved])
    got = onward(got, direct, [early[0], *moved])
    buffer, *early = late_step(last - 1, form, meta, moved, flat, buffer, early)
    buffer, *late = late_step(last, form, meta, got, flat, buffer, early)
    total = rhs_rest.astype(F32) - late[0]
    for c in range(1, n_cols):
        total = total - along_cols(late[c], c).astype(F32)
    return buffer, total.astype(BF16)


def per_device(lower_pivot, lower_rest, diag_inverse, rhs_pivot, rhs_rest):
    form = form_of(lower_pivot, rhs_pivot)
    fits = form.eqs % 128 == 0 and form.width % form.eqs == 0 and form.sides % 128 == 0
    fits = fits and (form.width // form.depth) % 16 == 0 and lower_rest.shape[0] % 128 == 0
    if fits:
        return kernel_path(form, lower_pivot, lower_rest, diag_inverse, rhs_pivot, rhs_rest)
    return plain_path(lower_pivot, lower_rest, diag_inverse, rhs_pivot, rhs_rest)


def solution(mesh):
    placed = (
        P(None, "rows", None, "cols"),
        P("rows", None, "cols"),
        P(None, "cols", "rows"),
        P(None, "rows", "cols"),
        P("cols", "rows"),
    )
    return jax.shard_map(
        per_device,
        mesh=mesh,
        in_specs=placed,
        out_specs=(P(None, "cols", None), P("cols", "rows")),
        check_vma=False,
    )
```
